128 devices in a mesh: gx: 16 (over x, z), gy: 8 (over y, core).
Axes of the slice: x: 4, y: 4, z: 4, core: 2. Of those that a mesh axis runs over, the one named last changes fastest.
Arguments:
- start: float32 [6144, 64], P(('gx', 'gy')), may hold values from -6 to 6
- shifts: float32 [4], replicated, may hold values from 0.2 to 0.8
- diag_blocks: float32 [6144, 64, 64], P(('gx', 'gy'))
- off_blocks: float32 [6144, 6, 64, 64], P(('gx', 'gy')), may hold values from -0.24 to 0.24
- jacobi_inv: float32 [6144, 64, 64], P(('gx', 'gy'))
- prolong: float32 [6144, 64, 8], P(('gx', 'gy')), may hold values from -0.75 to 0.75
- coarse_inv: float32 [3072, 8, 8], P(('gx', 'gy')), may hold values from -1 to 1
- cols: int32 [6144, 6], P(('gx', 'gy')), may hold values from 0 to 111
- send_rows: int32 [128, 4, 16], P(('gx', 'gy')), may hold values from 0 to 47
- owner: int32 [6144, 1], P(('gx', 'gy')), may hold values from 0 to 127; in each aligned block of 48 rows (0 to 47, 48 to 95, ...) at most 2 rows name the same one
- agg_slot: int32 [6144], P(('gx', 'gy')), may hold values from 0 to 23
Outputs:
- basis_q: float32 [5, 6144, 64], P(None, ('gx', 'gy'))
- r_factor: float32 [5, 5], replicated
The draws below stay inside these ranges and needn't reach their ends.
Inputs may be any that keep to these rules, and one draw needn't show every extreme that they name: In the rows of one device (aligned blocks of 48 rows) no owner id appears more than 2 times, and some id appears exactly 2 times.
All inputs are finite; a program needn't handle non-finite values.
Results may differ from the reference program's by a relative error of at most 0.0003.
Values sent between devices are 32-bit elements; how exact they have to be, the bound alone decides.
No kernel may reach another device: no remote copies, remote signals or barrier semaphores. Data moves between devices by JAX's collectives and lax.ppermute only.
A program may use at most 128 MiB of HBM per device.

```python
import math
import jax
import jax.numpy as jnp
import numpy as np
from jax import lax

BS = 64
CW = 8
K = 6
S = 4
NB_DEV = 48
H = 16
AGG_DEV = 24
NBLK = 6144
NAGG = 3072
CAP = 2
N_GX = 16
N_GY = 8


def draw_diag_blocks(key, part):
    key = jax.random.fold_in(key, 11)
    scale_key, noise_key = jax.random.split(key)
    diag_levels = jax.random.uniform(scale_key, (NBLK, BS), jnp.float32, 1.0, 2.0)
    noise_part = 0.04 * jax.random.normal(noise_key, (NBLK, BS, BS), jnp.float32)
    return diag_levels[:, :, None] * jnp.eye(BS, dtype=jnp.float32)[None] + noise_part


def draw_jacobi_inv(key, part):
    key = jax.random.fold_in(key, 23)
    scale_key, noise_key = jax.random.split(key)
    diag_levels = jax.random.uniform(scale_key, (NBLK, BS), jnp.float32, 0.5, 1.0)
    noise_part = 0.03 * jax.random.normal(noise_key, (NBLK, BS, BS), jnp.float32)
    return diag_levels[:, :, None] * jnp.eye(BS, dtype=jnp.float32)[None] + noise_part


def place_ends(entries, stream_key, smallest, top_value):
    spot = [jax.random.randint(jax.random.fold_in(stream_key, axis), (), 0, length) for axis, length in enumerate(entries.shape)]
    longest = entries.shape.index(max(entries.shape))
    next_to = spot[:longest] + [(spot[longest] + 1) % entries.shape[longest]] + spot[longest + 1:]
    return entries.at[tuple(spot)].set(smallest).at[tuple(next_to)].set(top_value)


def shard_levels(own_key, extent, pieces, least, high):
    factor_of = 1.0
    for axis_at, shards_of in pieces:
        draws = jax.random.uniform(jax.random.fold_in(jax.random.fold_in(own_key, 6), axis_at), (shards_of,), jnp.float32, least / len(pieces), high / len(pieces))
        factor_of = factor_of * jnp.repeat(jnp.exp(draws), extent[axis_at] // shards_of).reshape((-1,) + (1,) * (len(extent) - 1 - axis_at))
    return factor_of


def routed_block(rng, own, number, rows, number_of, top, reach, slope):
    ranking = jax.random.permutation(rng, number_of)
    crowded, common = portions_of(number_of, rows * top, reach, slope, True), portions_of(number_of, rows * top, reach, slope, False)
    places = jnp.arange(number_of)

    def named(tallies, rotation):
        used = int((tallies > 0).sum())
        fixed = max(1, used // 4)
        passed = fixed + (places - fixed + rotation * (used - fixed)) % max(1, number_of - fixed)
        return jnp.zeros((number_of,), jnp.int32).at[ranking[jnp.where(places < fixed, places, passed)]].set(jnp.asarray(tallies, jnp.int32))

    tallies = jnp.where(number % 4 == 0, named(crowded, number // 4), named(common, number - number // 4 - 1))
    mixed = jax.random.permutation(jax.random.fold_in(own, 3), number_of)
    source_of, sink = mixed[0:number_of // 2 * 2:2], mixed[1:number_of // 2 * 2:2]
    margin = jnp.minimum(tallies[source_of] - 1, reach - tallies[sink]) // 2
    margin = jnp.where((source_of == ranking[0]) | (sink == ranking[0]) | (tallies[sink] == 0), 0, jnp.maximum(margin, 0))
    passed = jax.random.randint(jax.random.fold_in(own, 4), (number_of // 2,), 0, 1 << 20) % (margin + 1)
    tallies = tallies.at[source_of].add(-passed).at[sink].add(passed)
    items = jnp.searchsorted(jnp.cumsum(tallies), jnp.arange(rows * top), side="right").astype(jnp.int32)
    listing = items.reshape(top, rows).T
    listing = listing[jax.random.permutation(jax.random.fold_in(own, 1), rows)]
    rotation = jax.random.randint(jax.random.fold_in(own, 2), (rows, 1), 0, top)
    return jnp.take_along_axis(listing, (jnp.arange(top)[None, :] + rotation) % top, axis=1)


def portions_of(count, total, most, slope, full):
    loads = [(1 << 20) // math.isqrt(grade ** slope) + 1 for grade in range(1, count + 1)]
    largest = most if full else min(most, max(-(-total // count), total * loads[0] // sum(loads)))
    least = 1 if total - largest >= count - 1 else 0
    counts, rest = [largest] + [least] * (count - 1), total - largest - least * (count - 1)
    while rest > 0:
        free = [i for i in range(1, count) if counts[i] < largest] or [i for i in range(1, count) if counts[i] < most]
        mass, left = sum([loads[i] for i in free]), rest
        for i in free:
            extra = min(most - counts[i], max(1, left * loads[i] // mass), rest)
            counts[i] = counts[i] + extra
            rest = rest - extra
    return np.array(counts)


def scatter_about(key, shape, spread, most, cuts=(), held_as=jnp.bfloat16):
    values = jax.random.normal(key, shape, jnp.float32) * spread
    if len(cuts) > 0:
        values = shard_levels(key, shape, cuts, -0.22, 0.18) * values
    return jnp.clip(values, min=-most, max=most).astype(held_as)


def setup_inputs(seed: int = 0) -> dict:
    keys = jax.random.split(jax.random.key(seed), 12)
    start = scatter_about(keys[0], (NBLK, BS), 1.0, 6.0, ((0, 128),), jnp.float32)
    shifts = jnp.clip(jax.random.uniform(keys[1], (S,), jnp.float32, 0.2, 0.8), 0.2, 0.8)
    diag_blocks = draw_diag_blocks(jax.random.fold_in(keys[11], 71), 0)
    off_blocks = scatter_about(keys[3], (NBLK, K, BS, BS), 0.04, 0.24, ((0, 128),), jnp.float32)
    jacobi_inv = draw_jacobi_inv(jax.random.fold_in(keys[11], 71), 0)
    prolong = scatter_about(keys[5], (NBLK, BS, CW), BS ** -0.5, 0.75, ((0, 128),), jnp.float32)
    coarse_inv = scatter_about(keys[6], (NAGG, CW, CW), (4 * CW) ** -0.5, 1.0, ((0, 128),), jnp.float32)
    cols = place_ends(jax.random.randint(keys[7], (NBLK, K), 0, NB_DEV + 4 * H), jax.random.fold_in(keys[7], 1), 0, (NB_DEV + 4 * H) - 1).astype(jnp.int32)
    send_rows = place_ends(jax.random.randint(keys[8], (N_GX * N_GY, 4, H), 0, NB_DEV), jax.random.fold_in(keys[8], 1), 0, NB_DEV - 1).astype(jnp.int32)
    owner_keys = jax.random.split(jax.random.fold_in(keys[9], 1), NBLK // NB_DEV)
    owner_turns = jax.random.permutation(jax.random.fold_in(keys[9], 3), NBLK // NB_DEV)
    owner = jax.vmap(lambda own, number: routed_block(jax.random.fold_in(keys[9], 2), own, number, NB_DEV, N_GX * N_GY, 1, CAP, 2))(owner_keys, owner_turns).reshape((NBLK, 1))
    agg_slot = place_ends(jax.random.randint(keys[10], (NBLK,), 0, AGG_DEV), jax.random.fold_in(keys[10], 1), 0, AGG_DEV - 1).astype(jnp.int32)
    return dict(start=start, shifts=shifts, diag_blocks=diag_blocks, off_blocks=off_blocks, jacobi_inv=jacobi_inv, prolong=prolong, coarse_inv=coarse_inv, cols=cols, send_rows=send_rows, owner=owner, agg_slot=agg_slot)


highest = lax.Precision.HIGHEST
jacobi_weight = 2.0 / 3.0

def apply_operator(vector, diag_blocks, off_blocks, cols, send_rows):
    grid = vector.reshape(N_GX, N_GY, NB_DEV, BS)
    send_lists = send_rows.reshape(N_GX, N_GY, 4, H)
    picked = jax.vmap(jax.vmap(lambda part_v, part_s: part_v[part_s]))(grid, send_lists)
    from_xlow = jnp.roll(picked[:, :, 0], 1, axis=0)
    from_xhigh = jnp.roll(picked[:, :, 1], -1, axis=0)
    from_ylow = jnp.roll(picked[:, :, 2], 1, axis=1)
    from_yhigh = jnp.roll(picked[:, :, 3], -1, axis=1)
    extended = jnp.concatenate([grid, from_xlow, from_xhigh, from_ylow, from_yhigh], axis=2)
    col_grid = cols.reshape(N_GX, N_GY, NB_DEV, K)
    nearby = jax.vmap(jax.vmap(lambda part_e, part_c: part_e[part_c]))(extended, col_grid)
    nearby = nearby.reshape(NBLK, K, BS)
    own_term = jnp.einsum('rij,rj->ri', diag_blocks, vector, precision=highest)
    rest_term = jnp.einsum('rkij,rkj->ri', off_blocks, nearby, precision=highest)
    return own_term + rest_term

def coarse_correct(vector, prolong, coarse_inv, owner, agg_slot):
    global_ids = owner[:, 0] * AGG_DEV + agg_slot
    partial_value = jnp.einsum('rbc,rb->rc', prolong, vector, precision=highest)
    coarse = jax.ops.segment_sum(partial_value, global_ids, num_segments=NAGG)
    answer = jnp.einsum('acd,ad->ac', coarse_inv, coarse, precision=highest)
    return jnp.einsum('rbc,rc->rb', prolong, answer[global_ids], precision=highest)

def reference(start, shifts, diag_blocks, off_blocks, jacobi_inv, prolong, coarse_inv, cols, send_rows, owner, agg_slot):

    def operator(vector):
        return apply_operator(vector, diag_blocks, off_blocks, cols, send_rows)

    def smooth(vector):
        return jacobi_weight * jnp.einsum('rij,rj->ri', jacobi_inv, vector, precision=highest)

    def precondition(vector):
        first = smooth(vector)
        second = first + coarse_correct(vector - operator(first), prolong, coarse_inv, owner, agg_slot)
        return second + smooth(vector - operator(second))
    basis = [start]
    for section in range(S):
        latest = basis[-1]
        basis.append(operator(precondition(latest)) - shifts[section] * latest)
    stacked = jnp.stack(basis)
    flat = stacked.reshape(S + 1, NBLK * BS)
    gram = jnp.dot(flat, flat.T, precision=highest) / (NBLK * BS)
    lower = jnp.linalg.cholesky(gram)
    solved = jax.scipy.linalg.solve_triangular(lower, flat, lower=True)
    return (solved.reshape(S + 1, NBLK, BS), lower.T)
```

```python
import functools

import jax
import jax.numpy as jnp
from jax import lax
from jax.experimental import pallas as pl
from jax.experimental.pallas import tpu as pltpu
from jax.sharding import PartitionSpec as P

F32 = jnp.float32
BF16 = jnp.bfloat16
ROWS = 48
BS = 64
CW = 8
HALO = 16
EXT = ROWS + 4 * HALO
KOFF = 6
WIDTH = 7 * 128
jacobi_weight = 2.0 / 3.0
PAIRS = [(j, l) for j in range(5) for l in range(j, 5)]

VM = pl.BlockSpec(memory_space=pltpu.VMEM)
SM = pl.BlockSpec(memory_space=pltpu.SMEM)
ANY = pl.BlockSpec(memory_space=pl.ANY)
LAST = (((1,), (1,)), ((), ()))


def low_lanes(x):
    return lax.broadcasted_iota(jnp.int32, x.shape, 1) < BS


def swap(x):
    return pltpu.roll(x, BS, 1)


def twice(x):
    return jnp.concatenate([x, x], axis=1)


def pack(x):
    high = x.astype(BF16).astype(F32)
    return jnp.where(low_lanes(x), high, (x - high).astype(BF16).astype(F32))


def lhs_parts(packed):
    low = low_lanes(packed)
    turned = swap(packed)
    return jnp.where(low, packed, turned), jnp.where(low, turned, 0.0)


def row_blocks(top, bottom, w_ref):
    out = []
    for g in range(ROWS // 8):
        lhs = jnp.concatenate([top[8 * g : 8 * g + 8], bottom[8 * g : 8 * g + 8]], axis=0).astype(BF16)
        r = lax.dot_general(lhs, w_ref[512 * g : 512 * g + 512, :], LAST, preferred_element_type=F32)
        s = r[:8] + r[8:]
        own = lax.broadcasted_iota(jnp.int32, s.shape, 0) == lax.broadcasted_iota(jnp.int32, s.shape, 1) // BS
        s = jnp.where(own, s, 0.0)
        t = (s[:, 0:128] + s[:, 128:256]) + (s[:, 256:384] + s[:, 384:512])
        out.append(t + swap(t))
    return jnp.concatenate(out, axis=0)


def smooth(x, wj_ref):
    top, bottom = lhs_parts(pack(x))
    return row_blocks(top, bottom, wj_ref)


def operate(packed, w_ref, gather_ref):
    e = jnp.concatenate([packed, jnp.zeros((128 - EXT, 128), F32)], axis=0)
    s = swap(e)
    low = low_lanes(e)
    zero = jnp.zeros_like(e)
    rhs = jnp.concatenate(
        [
            jnp.concatenate([jnp.where(low, e, zero), jnp.where(low, s, zero)], axis=1),
            jnp.concatenate([jnp.where(low, zero, s), jnp.where(low, zero, e)], axis=1),
        ],
        axis=0,
    ).astype(BF16)
    x = jnp.dot(gather_ref[...], rhs, preferred_element_type=F32)
    high = [x[ROWS * p : ROWS * p + ROWS, 0:128] for p in range(3)]
    rest = [x[ROWS * p : ROWS * p + ROWS, 128:256] for p in range(3)]
    top, bottom = lhs_parts(packed[:ROWS])
    none = [jnp.zeros((ROWS, 128), F32)] * 3
    return row_blocks(
        jnp.concatenate(high + high + [top], axis=1), jnp.concatenate(rest + none + [bottom], axis=1), w_ref
    )


def send_lists(packed, pick_ref, outs):
    picked = jnp.dot(pick_ref[...], packed.astype(BF16), preferred_element_type=F32)
    for s, out in enumerate(outs):
        out[...] = picked[HALO * s : HALO * s + HALO]


def first_kernel(start, jac, pt, ids, listed, v, wj, ptd, pick, z, ze, s0, s1, s2, s3):
    v[...] = twice(start[...])
    for g in range(ROWS // 8):
        wj[512 * g : 512 * g + 512, :] = pack(twice(jac[512 * g : 512 * g + 512, :] * jacobi_weight)).astype(BF16)
    for c in range(CW):
        ptd[c] = twice(pt[c])
    chosen = (listed[...] == lax.broadcasted_iota(jnp.int32, (4 * HALO, ROWS), 1)).astype(F32)
    pick[...] = chosen.astype(BF16)
    z[...] = smooth(v[...], wj)
    ze[...] = pack(z[...])
    low = lax.broadcasted_iota(jnp.int32, (ROWS, 128), 1) < BS
    parts = [jnp.where(low, ptd[r], ptd[r + 4]) for r in range(4)] + [ids[...]]
    parts = [jnp.dot(chosen, x, precision=lax.Precision.HIGHEST, preferred_element_type=F32) for x in parts]
    parts = [jnp.dot(pick[...], ze[...].astype(BF16), preferred_element_type=F32)] + parts
    for s, out in enumerate((s0, s1, s2, s3)):
        for k, x in enumerate(parts):
            out[k] = x[HALO * s : HALO * s + HALO]


def operator_kernel(off, diag, cols, w, gather, buf, dbuf, sems, dsems):
    def copies(g):
        slot = g % 2
        return (
            pltpu.make_async_copy(off.at[pl.ds(8 * g, 8)], buf.at[slot], sems.at[slot]),
            pltpu.make_async_copy(diag.at[pl.ds(8 * g, 8)], dbuf.at[slot], dsems.at[slot]),
        )

    for c in copies(0):
        c.start()
    lane = lax.broadcasted_iota(jnp.int32, (ROWS, 256), 1)
    for p in range(3):
        hit = (lane == cols[:, 2 * p : 2 * p + 1]) | (lane == cols[:, 2 * p + 1 : 2 * p + 2] + 128)
        gather[ROWS * p : ROWS * p + ROWS, :] = hit.astype(F32).astype(BF16)
    for g in range(ROWS // 8):
        if g + 1 < ROWS // 8:
            for c in copies(g + 1):
                c.start()
        for c in copies(g):
            c.wait()
        slot = g % 2

        def row(i, carry):
            at = pl.ds(pl.multiple_of((8 * g + i) * BS, BS), BS)
            for p in range(3):
                x = jnp.concatenate([buf[slot, i, 2 * p], buf[slot, i, 2 * p + 1]], axis=1)
                high = x.astype(BF16)
                w[at, 128 * p : 128 * p + 128] = high
                w[at, 384 + 128 * p : 512 + 128 * p] = (x - high.astype(F32)).astype(BF16)
            w[at, 768:896] = pack(twice(dbuf[slot, i])).astype(BF16)
            return carry

        lax.fori_loop(0, 8, row, 0)


def restrict_kernel(v, ze, h0, h1, h2, h3, w_op, gather, ptd, w, p):
    ext = jnp.concatenate([ze[...], h0[...], h1[...], h2[...], h3[...]], axis=0)
    r = v[...] - operate(ext, w_op, gather)
    w[...] = r
    ones = jnp.ones((16, 128), BF16)
    pad = jnp.zeros((16, 128), F32)
    for k in range(4):
        x = jnp.concatenate([pack(ptd[k] * r), pad, pack(ptd[k + 4] * r), pad], axis=0).astype(BF16)
        p[k : k + 1, :] = lax.dot_general(ones, x, LAST, preferred_element_type=F32)[0:1]


def coarse_kernel(x0, ids, ptd, g0, g1, g2, g3, mask, pte, xp):
    idc = jnp.concatenate(
        [ids[...], g0[5], g1[5], g2[5], g3[5], jnp.full((128 - EXT, 128), -1.0, F32)], axis=0
    )
    low = low_lanes(idc)
    low8 = lax.broadcasted_iota(jnp.int32, (1, 128), 1) < BS
    for q in range(64):
        line = jnp.where(low8, x0[2 * q, 4:5, :], x0[2 * q + 1, 4:5, :])
        mask[:, 128 * q : 128 * q + 128] = (idc == line).astype(F32).astype(BF16)
        xp[q] = jnp.concatenate([x0[2 * q, 0:4, :], x0[2 * q + 1, 0:4, :]], axis=0)
    device = jnp.floor((idc + 0.5) * (1.0 / 24.0))
    slot = idc - 24.0 * device
    upper = slot >= 11.5
    place = device * 16.0 + jnp.where(upper, slot - 12.0, slot)
    total = jnp.zeros((128, 128), F32)
    for b in range(8):
        src = x0[16 * b : 16 * b + 16, 8:24, :].reshape(256, 128)
        high = src.astype(BF16)
        mid = (src - high.astype(F32)).astype(BF16)
        rest = (src - high.astype(F32) - mid.astype(F32)).astype(BF16)
        lane = lax.broadcasted_iota(jnp.int32, (128, 256), 1).astype(F32) + 256.0 * b
        hit = (twice(place) == lane).astype(F32).astype(BF16)
        got = jnp.dot(hit, jnp.concatenate([high, mid, rest], axis=1), preferred_element_type=F32)
        total = total + (got[:, 0:128] + got[:, 128:256] + got[:, 256:384])
    inverse = jnp.where(upper, swap(total), total)[:EXT]
    wide = []
    for c in range(CW):
        around = [g[1 + c % 4] for g in (g0, g1, g2, g3)]
        around = jnp.concatenate(around, axis=0)
        lowh = low_lanes(around)
        turned = swap(around)
        around = jnp.where(lowh, around, turned) if c < 4 else jnp.where(lowh, turned, around)
        wide.append(jnp.concatenate([ptd[c], around], axis=0))
    for d in range(CW):
        acc = wide[0] * inverse[:, d : d + 1]
        for c in range(1, CW):
            acc = acc + wide[c] * inverse[:, c * CW + d : c * CW + d + 1]
        pte[d] = acc


def correct_kernel(x, mask, pte, z, w, w_op, gather, wj, pick, ye, s0, s1, s2, s3, parts):
    sub = lax.broadcasted_iota(jnp.int32, (8, 128), 0) < 4
    lane = lax.broadcasted_iota(jnp.int32, (8, 128), 1) < BS
    keep = sub == lane
    for q in range(64):
        t = x[q]
        t = jnp.where(keep, t, pltpu.roll(swap(t), 4, 0))
        high = t.astype(BF16).astype(F32)
        parts[:, 128 * q : 128 * q + 128] = jnp.concatenate([high, t - high], axis=0).astype(BF16)
    got = lax.dot_general(mask[...], parts[...], LAST, preferred_element_type=F32)
    coarse = got[:EXT, 0:8] + got[:EXT, 8:16]
    u = pte[0] * coarse[:, 0:1]
    for d in range(1, CW):
        u = u + pte[d] * coarse[:, d : d + 1]
    r = w[...] - operate(pack(u), w_op, gather)
    y = z[...] + u[:ROWS] + smooth(r, wj)
    ye[...] = pack(y)
    send_lists(ye[...], pick, (s0, s1, s2, s3))


def advance(k, shifts, v, ye, h0, h1, h2, h3, w_op, gather):
    ext = jnp.concatenate([ye[...], h0[...], h1[...], h2[...], h3[...]], axis=0)
    return operate(ext, w_op, gather) - shifts[k] * v[...]


def advance_kernel(k, shifts, v, ye, h0, h1, h2, h3, w_op, gather, wj, pick, vn, z, ze, s0, s1, s2, s3):
    vn[...] = advance(k, shifts, v, ye, h0, h1, h2, h3, w_op, gather)
    z[...] = smooth(vn[...], wj)
    ze[...] = pack(z[...])
    send_lists(ze[...], pick, (s0, s1, s2, s3))


def last_kernel(shifts, ye, h0, h1, h2, h3, w_op, gather, v0, v1, v2, v3, v4, gram):
    v4[...] = advance(3, shifts, v3, ye, h0, h1, h2, h3, w_op, gather)
    basis = [v[...] for v in (v0, v1, v2, v3, v4)]
    rows = []
    for j, l in PAIRS:
        rows.append(jnp.sum(basis[j] * basis[l], axis=0, keepdims=True))
    rows.append(jnp.zeros((128 - len(rows), 128), F32))
    rows = jnp.concatenate(rows, axis=0)
    sums = lax.dot_general(
        jnp.ones((8, 128), F32), rows, LAST, precision=lax.Precision.HIGHEST, preferred_element_type=F32
    )
    gram[...] = sums[0:1]


def orthogonal_kernel(total, grams, v0, v1, v2, v3, v4, q_out, r_out):
    sums = jnp.sum(grams[...], axis=0, keepdims=True) * (1.0 / (2.0 * total))
    g = {pair: sums[:, n : n + 1] for n, pair in enumerate(PAIRS)}
    lower = {}
    for j in range(5):
        d = g[(j, j)]
        for k in range(j):
            d = d - lower[(j, k)] * lower[(j, k)]
        lower[(j, j)] = jnp.sqrt(d)
        for i in range(j + 1, 5):
            t = g[(j, i)]
            for k in range(j):
                t = t - lower[(i, k)] * lower[(j, k)]
            lower[(i, j)] = t / lower[(j, j)]
    at_row = lax.broadcasted_iota(jnp.int32, (8, 128), 0)
    at_col = lax.broadcasted_iota(jnp.int32, (8, 128), 1)
    r = jnp.zeros((8, 128), F32)
    for (i, j), value in lower.items():
        r = jnp.where((at_row == j) & (at_col == i), value, r)
    r_out[...] = r[0:5, 0:5]
    solved = []
    for i, v in enumerate((v0, v1, v2, v3, v4)):
        t = v[...]
        for k in range(i):
            t = t - lower[(i, k)] * solved[k]
        t = t / lower[(i, i)]
        solved.append(t)
        q_out[i] = t[:, 0:BS]


def shape(*dims, dtype=F32):
    return jax.ShapeDtypeStruct(dims, dtype)


def kept(*dims, dtype=F32):
    return pltpu.VMEM(dims, dtype)


def call(kernel, outs, *args, specs=None, scratch=(), flops=2_000_000, name=None):
    return pl.pallas_call(
        kernel,
        out_shape=outs,
        in_specs=specs or [VM] * len(args),
        out_specs=jax.tree.map(lambda _: VM, outs),
        scratch_shapes=list(scratch),
        compiler_params=pltpu.CompilerParams(vmem_limit_bytes=24 << 20),
        cost_estimate=pl.CostEstimate(flops=flops, bytes_accessed=100_000, transcendentals=0),
        name=name,
    )(*args)


def swap_pairs(count, phase):
    if phase == 0:
        return [(i, i ^ 1) for i in range(count)]
    return [(i, (i - 1) % count if i % 2 == 0 else (i + 1) % count) for i in range(count)]


def exchange(sends):
    nx, ny = lax.axis_size("gx"), lax.axis_size("gy")
    b = lax.ppermute(sends[1], "gx", swap_pairs(nx, 1))
    d = lax.ppermute(sends[3], "gy", swap_pairs(ny, 1))
    a = lax.ppermute(sends[0], "gx", swap_pairs(nx, 0))
    c = lax.ppermute(sends[2], "gy", swap_pairs(ny, 0))
    return a, b, c, d


def everywhere(x):
    count = lax.axis_size("gx") * lax.axis_size("gy")
    y = jnp.broadcast_to(x[None], (count,) + x.shape)
    return lax.all_to_all(y, ("gx", "gy"), split_axis=0, concat_axis=0, tiled=True)


def per_device(start, shifts, diag_blocks, off_blocks, jacobi_inv, prolong, coarse_inv, cols, send_rows, owner, agg_slot):
    odd_x = lax.axis_index("gx") % 2
    odd_y = lax.axis_index("gy") % 2
    lists = send_rows[0]
    lists = jnp.concatenate(
        [jnp.where(odd_x == 1, lists[1::-1], lists[0:2]), jnp.where(odd_y == 1, lists[3:1:-1], lists[2:4])]
    ).reshape(4 * HALO, 1)
    beyond = cols - ROWS
    turn = jnp.where(beyond < 2 * HALO, 1 - odd_x, 1 - odd_y) * HALO
    cols = jnp.where(beyond >= 0, ROWS + (beyond ^ turn), cols)
    ids = (owner[:, 0] * coarse_inv.shape[0] + agg_slot).astype(F32)
    id_col = jnp.broadcast_to(ids[:, None], (ROWS, 128))
    id_pad = jnp.concatenate([ids, jnp.full((BS - ROWS,), -1.0, F32)])
    inv = coarse_inv.reshape(24, BS)
    extra = jnp.concatenate(
        [
            jnp.concatenate([id_pad, id_pad])[None],
            jnp.zeros((3, 128), F32),
            jnp.concatenate([inv[:12], inv[12:]], axis=1),
            jnp.zeros((4, 128), F32),
        ]
    )
    pt = jnp.transpose(prolong, (2, 0, 1))

    halo = [shape(HALO, 128)] * 4
    v, wj, ptd, pick, z, ze, *sends = call(
        first_kernel,
        [
            shape(ROWS, 128),
            kept(ROWS * BS, 128, dtype=BF16),
            shape(CW, ROWS, 128),
            shape(4 * HALO, ROWS, dtype=BF16),
            shape(ROWS, 128),
            shape(ROWS, 128),
        ]
        + [shape(6, HALO, 128)] * 4,
        start,
        jacobi_inv.reshape(ROWS * BS, BS),
        pt,
        id_col,
        lists,
        name="first",
    )
    got = exchange(sends)
    w_op, gather = call(
        operator_kernel,
        [kept(ROWS * BS, WIDTH, dtype=BF16), shape(3 * ROWS, 256, dtype=BF16)],
        off_blocks,
        diag_blocks,
        cols,
        specs=[ANY, ANY, VM],
        scratch=[
            pltpu.VMEM((2, 8, KOFF, BS, BS), F32),
            pltpu.VMEM((2, 8, BS, BS), F32),
            pltpu.SemaphoreType.DMA((2,)),
            pltpu.SemaphoreType.DMA((2,)),
        ],
        flops=2_000_000_000,
        name="operator",
    )
    around = [g[0] for g in got]
    basis = [v]
    mask = pte = None
    for k in range(4):
        w, p = call(
            restrict_kernel, [shape(ROWS, 128), shape(4, 128)], v, ze, *around, w_op, gather, ptd, name="restrict"
        )
        if k == 0:
            both = everywhere(jnp.concatenate([p, extra]))
            mask, pte, x = call(
                coarse_kernel,
                [kept(128, 64 * 128, dtype=BF16), shape(CW, EXT, 128), shape(64, 8, 128)],
                both,
                id_col,
                ptd,
                *got,
                name="coarse",
            )
        else:
            x = everywhere(p).reshape(64, 8, 128)
        ye, *sends = call(
            correct_kernel,
            [shape(ROWS, 128)] + halo,
            x,
            mask,
            pte,
            z,
            w,
            w_op,
            gather,
            wj,
            pick,
            scratch=[pltpu.VMEM((16, 64 * 128), BF16)],
            name="correct",
        )
        around = exchange(sends)
        if k < 3:
            v, z, ze, *sends = call(
                functools.partial(advance_kernel, k),
                [shape(ROWS, 128)] * 3 + halo,
                shifts,
                v,
                ye,
                *around,
                w_op,
                gather,
                wj,
                pick,
                specs=[SM] + [VM] * 10,
                name="advance",
            )
            basis.append(v)
            around = exchange(sends)
    v, gram = call(
        last_kernel,
        [shape(ROWS, 128), shape(1, 128)],
        shifts,
        ye,
        *around,
        w_op,
        gather,
        *basis,
        specs=[SM] + [VM] * 11,
        name="last",
    )
    basis.append(v)
    grams = everywhere(gram).reshape(128, 128)
    total = float(ROWS * BS * 128)
    return tuple(
        call(
            functools.partial(orthogonal_kernel, total),
            [shape(5, ROWS, BS), shape(5, 5)],
            grams,
            *basis,
            name="orthogonal",
        )
    )


def solution(mesh):
    rows = ("gx", "gy")
    in_specs = (
        P(rows, None),
        P(),
        P(rows, None, None),
        P(rows, None, None, None),
        P(rows, None, None),
        P(rows, None, None),
        P(rows, None, None),
        P(rows, None),
        P(rows, None, None),
        P(rows, None),
        P(rows),
    )
    return jax.shard_map(
        per_device, mesh=mesh, in_specs=in_specs, out_specs=(P(None, rows, None), P()), check_vma=False
    )
```

```python
import functools

import jax
import jax.numpy as jnp
from jax import lax
from jax.experimental import pallas as pl
from jax.experimental.pallas import tpu as pltpu
from jax.sharding import PartitionSpec as P

F32 = jnp.float32
BF16 = jnp.bfloat16
ROWS = 48
BS = 64
CW = 8
HALO = 16
EXT = ROWS + 4 * HALO
KOFF = 6
WIDTH = 7 * 128
jacobi_weight = 2.0 / 3.0
PAIRS = [(j, l) for j in range(5) for l in range(j, 5)]

VM = pl.BlockSpec(memory_space=pltpu.VMEM)
HBM = pl.BlockSpec(memory_space=pltpu.HBM)
LAST = (((1,), (1,)), ((), ()))


def low_lanes(x):
    return lax.broadcasted_iota(jnp.int32, x.shape, 1) < BS


def swap(x):
    return pltpu.roll(x, BS, 1)


def twice(x):
    return jnp.concatenate([x, x], axis=1)


def pack(x):
    high = x.astype(BF16).astype(F32)
    return jnp.where(low_lanes(x), high, (x - high).astype(BF16).astype(F32))


def lhs_parts(packed):
    low = low_lanes(packed)
    turned = swap(packed)
    return jnp.where(low, packed, turned), jnp.where(low, turned, 0.0)


def row_blocks(top, bottom, w_ref):
    out = []
    for g in range(ROWS // 8):
        lhs = jnp.concatenate([top[8 * g : 8 * g + 8], bottom[8 * g : 8 * g + 8]], axis=0).astype(BF16)
        r = jnp.dot(lhs, w_ref[:, 512 * g : 512 * g + 512], preferred_element_type=F32)
        s = r[:8] + r[8:]
        own = lax.broadcasted_iota(jnp.int32, s.shape, 0) == lax.broadcasted_iota(jnp.int32, s.shape, 1) // BS
        s = jnp.where(own, s, 0.0)
        t = (s[:, 0:128] + s[:, 128:256]) + (s[:, 256:384] + s[:, 384:512])
        out.append(t + swap(t))
    return jnp.concatenate(out, axis=0)


def smooth(x, wj_ref):
    top, bottom = lhs_parts(pack(x))
    return row_blocks(top, bottom, wj_ref)


def operate(packed, w_ref, gather_ref):
    e = jnp.concatenate([packed, jnp.zeros((128 - EXT, 128), F32)], axis=0)
    s = swap(e)
    low = low_lanes(e)
    zero = jnp.zeros_like(e)
    rhs = jnp.concatenate(
        [
            jnp.concatenate([jnp.where(low, e, zero), jnp.where(low, s, zero)], axis=1),
            jnp.concatenate([jnp.where(low, zero, s), jnp.where(low, zero, e)], axis=1),
        ],
        axis=0,
    ).astype(BF16)
    x = jnp.dot(gather_ref[...], rhs, preferred_element_type=F32)
    high = [x[ROWS * p : ROWS * p + ROWS, 0:128] for p in range(3)]
    rest = [x[ROWS * p : ROWS * p + ROWS, 128:256] for p in range(3)]
    top, bottom = lhs_parts(packed[:ROWS])
    none = [jnp.zeros((ROWS, 128), F32)] * 3
    return row_blocks(
        jnp.concatenate(high + high + [top], axis=1), jnp.concatenate(rest + none + [bottom], axis=1), w_ref
    )


def send_lists(packed, pick_ref, outs):
    picked = jnp.dot(pick_ref[...], packed.astype(BF16), preferred_element_type=F32)
    for s, out in enumerate(outs):
        out[...] = picked[HALO * s : HALO * s + HALO]


def pair_rows(x):
    t = twice(x).T
    high = t.astype(BF16).astype(F32)
    return jnp.where(lax.broadcasted_iota(jnp.int32, t.shape, 0) < BS, high, t - high).astype(BF16)


def first_kernel(start, jac, pt, ids, listed, v, wj, ptd, pick, z, ze, s0, s1, s2, s3):
    v[...] = twice(start[...])
    for n in range(ROWS // 2):
        wj[:, 128 * n : 128 * n + 128] = pair_rows(jac[128 * n : 128 * n + 128, :] * jacobi_weight)
    for c in range(CW):
        ptd[c] = twice(pt[:, c, :])
    chosen = (listed[...] == lax.broadcasted_iota(jnp.int32, (4 * HALO, ROWS), 1)).astype(F32)
    pick[...] = chosen.astype(BF16)
    z[...] = smooth(v[...], wj)
    ze[...] = pack(z[...])
    low = lax.broadcasted_iota(jnp.int32, (ROWS, 128), 1) < BS
    parts = [jnp.where(low, ptd[r], ptd[r + 4]) for r in range(4)] + [ids[...]]
    parts = [jnp.dot(chosen, x, precision=lax.Precision.HIGHEST, preferred_element_type=F32) for x in parts]
    parts = [jnp.dot(pick[...], ze[...].astype(BF16), preferred_element_type=F32)] + parts
    for s, out in enumerate((s0, s1, s2, s3)):
        for k, x in enumerate(parts):
            out[k] = x[HALO * s : HALO * s + HALO]


def operator_kernel(off, diag, cols, w, gather, buf, dbuf, sems, dsems):
    def copies(g):
        slot = g % 2
        return (
            pltpu.make_async_copy(off.at[pl.ds(8 * g, 8)], buf.at[slot], sems.at[slot]),
            pltpu.make_async_copy(diag.at[pl.ds(8 * g, 8)], dbuf.at[slot], dsems.at[slot]),
        )

    for c in copies(0):
        c.start()
    lane = lax.broadcasted_iota(jnp.int32, (ROWS, 256), 1)
    for p in range(3):
        hit = (lane == cols[:, 2 * p : 2 * p + 1]) | (lane == cols[:, 2 * p + 1 : 2 * p + 2] + 128)
        gather[ROWS * p : ROWS * p + ROWS, :] = hit.astype(F32).astype(BF16)
    for g in range(ROWS // 8):
        if g + 1 < ROWS // 8:
            for c in copies(g + 1):
                c.start()
        for c in copies(g):
            c.wait()
        slot = g % 2

        for n in range(4):
            at = slice(128 * (4 * g + n), 128 * (4 * g + n) + 128)
            i, j = 2 * n, 2 * n + 1
            for p in range(3):
                x = jnp.concatenate(
                    [
                        jnp.concatenate([buf[slot, i, 2 * p], buf[slot, i, 2 * p + 1]], axis=1),
                        jnp.concatenate([buf[slot, j, 2 * p], buf[slot, j, 2 * p + 1]], axis=1),
                    ],
                    axis=0,
                ).T
                high = x.astype(BF16)
                w[128 * p : 128 * p + 128, at] = high
                w[384 + 128 * p : 512 + 128 * p, at] = (x - high.astype(F32)).astype(BF16)
            w[768:896, at] = pair_rows(jnp.concatenate([dbuf[slot, i], dbuf[slot, j]], axis=0))


def restrict_kernel(v, ze, h0, h1, h2, h3, w_op, gather, ptd, *rest):
    *extra, w, p = rest
    ext = jnp.concatenate([ze[...], h0[...], h1[...], h2[...], h3[...]], axis=0)
    r = v[...] - operate(ext, w_op, gather)
    w[...] = r
    ones = jnp.ones((16, 128), BF16)
    pad = jnp.zeros((16, 128), F32)
    for k in range(4):
        x = jnp.concatenate([pack(ptd[k] * r), pad, pack(ptd[k + 4] * r), pad], axis=0).astype(BF16)
        line = lax.dot_general(ones, x, LAST, preferred_element_type=F32)[0:1]
        p[k : k + 1, :] = line + extra[0][k : k + 1, :] if extra else line
    if extra:
        p[4:16, :] = extra[0][4:16, :]


def coarse_kernel(x0, ids, ptd, g0, g1, g2, g3, mask, pte, xp):
    idc = jnp.concatenate(
        [ids[...], g0[5], g1[5], g2[5], g3[5], jnp.full((128 - EXT, 128), -1.0, F32)], axis=0
    )
    wanted = idc.T[0:1]
    given = [x0[:, r, :].T[ROWS:BS] for r in range(3)] + [jnp.full((BS - ROWS, 128), -1.0, F32)]
    given = jnp.concatenate(given + given, axis=0)
    upper_rows = lax.broadcasted_iota(jnp.int32, (128, 1), 0) < BS
    for q in range(64):
        line = jnp.where(upper_rows, given[:, 2 * q : 2 * q + 1], given[:, 2 * q + 1 : 2 * q + 2])
        mask[128 * q : 128 * q + 128, :] = (line == wanted).astype(F32).astype(BF16)
        xp[q] = jnp.concatenate([x0[2 * q, 0:4, :], x0[2 * q + 1, 0:4, :]], axis=0)
    device = jnp.floor((idc + 0.5) * (1.0 / 24.0))
    slot = idc - 24.0 * device
    upper = slot >= 11.5
    place = device * 16.0 + 4.0 + jnp.where(upper, slot - 12.0, slot)
    total = jnp.zeros((128, 128), F32)
    for b in range(8):
        src = x0[16 * b : 16 * b + 16].reshape(256, 128)
        high = src.astype(BF16)
        mid = (src - high.astype(F32)).astype(BF16)
        rest = (src - high.astype(F32) - mid.astype(F32)).astype(BF16)
        lane = lax.broadcasted_iota(jnp.int32, (128, 256), 1).astype(F32) + 256.0 * b
        hit = (twice(place) == lane).astype(F32).astype(BF16)
        got = jnp.dot(hit, jnp.concatenate([high, mid, rest], axis=1), preferred_element_type=F32)
        total = total + (got[:, 0:128] + got[:, 128:256] + got[:, 256:384])
    inverse = jnp.where(upper, swap(total), total)[:EXT]
    wide = []
    for c in range(CW):
        around = [g[1 + c % 4] for g in (g0, g1, g2, g3)]
        around = jnp.concatenate(around, axis=0)
        lowh = low_lanes(around)
        turned = swap(around)
        around = jnp.where(lowh, around, turned) if c < 4 else jnp.where(lowh, turned, around)
        wide.append(jnp.concatenate([ptd[c], around], axis=0))
    for d in range(CW):
        acc = wide[0] * inverse[:, d : d + 1]
        for c in range(1, CW):
            acc = acc + wide[c] * inverse[:, c * CW + d : c * CW + d + 1]
        pte[d] = acc


def correct_kernel(x, mask, pte, z, w, w_op, gather, wj, pick, ye, s0, s1, s2, s3, parts):
    sub = lax.broadcasted_iota(jnp.int32, (8, 128), 0) < 4
    lane = lax.broadcasted_iota(jnp.int32, (8, 128), 1) < BS
    keep = sub == lane
    for q in range(64):
        t = x[q]
        t = jnp.where(keep, t, pltpu.roll(swap(t), 4, 0))
        high = t.astype(BF16).astype(F32)
        parts[:, 128 * q : 128 * q + 128] = jnp.concatenate([high, t - high], axis=0).astype(BF16)
    got = jnp.dot(parts[...], mask[...], preferred_element_type=F32)
    coarse = jnp.concatenate([got[0:8] + got[8:16], jnp.zeros((120, 128), F32)], axis=0).T[:EXT]
    u = pte[0] * coarse[:, 0:1]
    for d in range(1, CW):
        u = u + pte[d] * coarse[:, d : d + 1]
    r = w[...] - operate(pack(u), w_op, gather)
    y = z[...] + u[:ROWS] + smooth(r, wj)
    ye[...] = pack(y)
    send_lists(ye[...], pick, (s0, s1, s2, s3))


def advance(k, shifts, v, ye, h0, h1, h2, h3, w_op, gather):
    ext = jnp.concatenate([ye[...], h0[...], h1[...], h2[...], h3[...]], axis=0)
    return operate(ext, w_op, gather) - shifts[k : k + 1, :] * v[...]


def advance_kernel(k, shifts, v, ye, h0, h1, h2, h3, w_op, gather, wj, pick, vn, z, ze, s0, s1, s2, s3):
    vn[...] = advance(k, shifts, v, ye, h0, h1, h2, h3, w_op, gather)
    z[...] = smooth(vn[...], wj)
    ze[...] = pack(z[...])
    send_lists(ze[...], pick, (s0, s1, s2, s3))


def last_kernel(shifts, ye, h0, h1, h2, h3, w_op, gather, v0, v1, v2, v3, v4, gram):
    v4[...] = advance(3, shifts, v3, ye, h0, h1, h2, h3, w_op, gather)
    basis = [v[...] for v in (v0, v1, v2, v3, v4)]
    rows = []
    for j, l in PAIRS:
        rows.append(jnp.sum(basis[j] * basis[l], axis=0, keepdims=True))
    rows.append(jnp.zeros((128 - len(rows), 128), F32))
    rows = jnp.concatenate(rows, axis=0)
    sums = lax.dot_general(
        jnp.ones((8, 128), F32), rows, LAST, precision=lax.Precision.HIGHEST, preferred_element_type=F32
    )
    gram[...] = sums[0:1]


def orthogonal_kernel(total, grams, v0, v1, v2, v3, v4, q_out, r_out):
    sums = jnp.sum(grams[...], axis=0, keepdims=True) * (1.0 / (2.0 * total))
    g = {pair: sums[:, n : n + 1] for n, pair in enumerate(PAIRS)}
    lower = {}
    for j in range(5):
        d = g[(j, j)]
        for k in range(j):
            d = d - lower[(j, k)] * lower[(j, k)]
        lower[(j, j)] = jnp.sqrt(d)
        for i in range(j + 1, 5):
            t = g[(j, i)]
            for k in range(j):
                t = t - lower[(i, k)] * lower[(j, k)]
            lower[(i, j)] = t / lower[(j, j)]
    at_row = lax.broadcasted_iota(jnp.int32, (8, 128), 0)
    at_col = lax.broadcasted_iota(jnp.int32, (8, 128), 1)
    r = jnp.zeros((8, 128), F32)
    for (i, j), value in lower.items():
        r = jnp.where((at_row == j) & (at_col == i), value, r)
    r_out[...] = r[0:5, 0:5]
    solved = []
    for i, v in enumerate((v0, v1, v2, v3, v4)):
        t = v[...]
        for k in range(i):
            t = t - lower[(i, k)] * solved[k]
        t = t / lower[(i, i)]
        solved.append(t)
        q_out[i] = t[:, 0:BS]


def shape(*dims, dtype=F32):
    return jax.ShapeDtypeStruct(dims, dtype)


def kept(*dims, dtype=F32):
    return pltpu.VMEM(dims, dtype)


def call(kernel, outs, *args, specs=None, scratch=(), flops=2_000_000, name=None):
    return pl.pallas_call(
        kernel,
        out_shape=outs,
        in_specs=specs or [VM] * len(args),
        out_specs=jax.tree.map(lambda _: VM, outs),
        scratch_shapes=list(scratch),
        compiler_params=pltpu.CompilerParams(vmem_limit_bytes=24 << 20),
        cost_estimate=pl.CostEstimate(flops=flops, bytes_accessed=100_000, transcendentals=0),
        name=name,
    )(*args)


def swap_pairs(count, phase):
    if phase == 0:
        return [(i, i ^ 1) for i in range(count)]
    return [(i, (i - 1) % count if i % 2 == 0 else (i + 1) % count) for i in range(count)]


def exchange(sends):
    nx, ny = lax.axis_size("gx"), lax.axis_size("gy")
    b = lax.ppermute(sends[1], "gx", swap_pairs(nx, 1))
    d = lax.ppermute(sends[3], "gy", swap_pairs(ny, 1))
    a = lax.ppermute(sends[0], "gx", swap_pairs(nx, 0))
    c = lax.ppermute(sends[2], "gy", swap_pairs(ny, 0))
    return a, b, c, d


def everywhere(x):
    count = lax.axis_size("gx") * lax.axis_size("gy")
    y = jnp.broadcast_to(x[None], (count,) + x.shape)
    return lax.all_to_all(y, ("gx", "gy"), split_axis=0, concat_axis=0, tiled=True)


def per_device(start, shifts, diag_blocks, off_blocks, jacobi_inv, prolong, coarse_inv, cols, send_rows, owner, agg_slot):
    odd_x = lax.axis_index("gx") % 2
    odd_y = lax.axis_index("gy") % 2
    lists = send_rows[0]
    lists = jnp.concatenate(
        [jnp.where(odd_x == 1, lists[1::-1], lists[0:2]), jnp.where(odd_y == 1, lists[3:1:-1], lists[2:4])]
    ).reshape(4 * HALO, 1)
    beyond = cols - ROWS
    turn = jnp.where(beyond < 2 * HALO, 1 - odd_x, 1 - odd_y) * HALO
    cols = jnp.where(beyond >= 0, ROWS + (beyond ^ turn), cols)
    ids = (owner[:, 0] * coarse_inv.shape[0] + agg_slot).astype(F32)
    id_col = jnp.broadcast_to(ids[:, None], (ROWS, 128))
    inv = coarse_inv.reshape(24, BS)
    spare = jnp.pad(ids.reshape(3, BS - ROWS), ((0, 1), (ROWS, BS)))
    extra = jnp.concatenate([spare, jnp.concatenate([inv[:12], inv[12:]], axis=1)])
    slopes = jnp.broadcast_to(shifts[:, None], (4, 128))
    pt = jnp.transpose(prolong, (0, 2, 1))

    halo = [shape(HALO, 128)] * 4
    v, wj, ptd, pick, z, ze, *sends = call(
        first_kernel,
        [
            shape(ROWS, 128),
            kept(128, ROWS * BS, dtype=BF16),
            shape(CW, ROWS, 128),
            shape(4 * HALO, ROWS, dtype=BF16),
            shape(ROWS, 128),
            shape(ROWS, 128),
        ]
        + [shape(6, HALO, 128)] * 4,
        start,
        jacobi_inv.reshape(ROWS * BS, BS),
        pt,
        id_col,
        lists,
        name="first",
    )
    got = exchange(sends)
    w_op, gather = call(
        operator_kernel,
        [kept(WIDTH, ROWS * BS, dtype=BF16), shape(3 * ROWS, 256, dtype=BF16)],
        pltpu.with_memory_space_constraint(off_blocks, pltpu.HBM),
        pltpu.with_memory_space_constraint(diag_blocks, pltpu.HBM),
        cols,
        specs=[HBM, HBM, VM],
        scratch=[
            pltpu.VMEM((2, 8, KOFF, BS, BS), F32),
            pltpu.VMEM((2, 8, BS, BS), F32),
            pltpu.SemaphoreType.DMA((2,)),
            pltpu.SemaphoreType.DMA((2,)),
        ],
        flops=2_000_000_000,
        name="operator",
    )
    around = [g[0] for g in got]
    basis = [v]
    mask = pte = None
    for k in range(4):
        w, p = call(
            restrict_kernel,
            [shape(ROWS, 128), shape(4 if k else 16, 128)],
            v,
            ze,
            *around,
            w_op,
            gather,
            ptd,
            *([] if k else [extra]),
            name="restrict",
        )
        x = everywhere(p)
        if k == 0:
            mask, pte, x = call(
                coarse_kernel,
                [kept(64 * 128, 128, dtype=BF16), shape(CW, EXT, 128), shape(64, 8, 128)],
                x,
                id_col,
                ptd,
                *got,
                name="coarse",
            )
        x = x.reshape(64, 8, 128)
        ye, *sends = call(
            correct_kernel,
            [shape(ROWS, 128)] + halo,
            x,
            mask,
            pte,
            z,
            w,
            w_op,
            gather,
            wj,
            pick,
            scratch=[pltpu.VMEM((16, 64 * 128), BF16)],
            name="correct",
        )
        around = exchange(sends)
        if k < 3:
            v, z, ze, *sends = call(
                functools.partial(advance_kernel, k),
                [shape(ROWS, 128)] * 3 + halo,
                slopes,
                v,
                ye,
                *around,
                w_op,
                gather,
                wj,
                pick,
                name="advance",
            )
            basis.append(v)
            around = exchange(sends)
    v, gram = call(
        last_kernel,
        [shape(ROWS, 128), shape(1, 128)],
        slopes,
        ye,
        *around,
        w_op,
        gather,
        *basis,
        name="last",
    )
    basis.append(v)
    grams = everywhere(gram).reshape(128, 128)
    total = float(ROWS * BS * 128)
    return tuple(
        call(
            functools.partial(orthogonal_kernel, total),
            [shape(5, ROWS, BS), shape(5, 5)],
            grams,
            *basis,
            name="orthogonal",
        )
    )


def solution(mesh):
    rows = ("gx", "gy")
    in_specs = (
        P(rows, None),
        P(),
        P(rows, None, None),
        P(rows, None, None, None),
        P(rows, None, None),
        P(rows, None, None),
        P(rows, None, None),
        P(rows, None),
        P(rows, None, None),
        P(rows, None),
        P(rows),
    )
    return jax.shard_map(
        per_device, mesh=mesh, in_specs=in_specs, out_specs=(P(None, rows, None), P()), check_vma=False
    )
```

```python
import functools

import jax
import jax.numpy as jnp
from jax import lax
from jax.experimental import pallas as pl
from jax.experimental.pallas import tpu as pltpu
from jax.sharding import PartitionSpec as P

F32 = jnp.float32
BF16 = jnp.bfloat16
ROWS = 48
BS = 64
CW = 8
HALO = 16
EXT = ROWS + 4 * HALO
KOFF = 6
WIDTH = 7 * 128
jacobi_weight = 2.0 / 3.0
PAIRS = [(j, l) for j in range(5) for l in range(j, 5)]

VM = pl.BlockSpec(memory_space=pltpu.VMEM)
HBM = pl.BlockSpec(memory_space=pltpu.HBM)
LAST = (((1,), (1,)), ((), ()))


def low_lanes(x):
    return lax.broadcasted_iota(jnp.int32, x.shape, 1) < BS


def swap(x):
    return pltpu.roll(x, BS, 1)


def twice(x):
    return jnp.concatenate([x, x], axis=1)


def pack(x):
    high = x.astype(BF16).astype(F32)
    return jnp.where(low_lanes(x), high, (x - high).astype(BF16).astype(F32))


def lhs_parts(packed):
    low = low_lanes(packed)
    turned = swap(packed)
    return jnp.where(low, packed, turned), jnp.where(low, turned, 0.0)


def row_blocks(top, bottom, w_ref):
    out = []
    for g in range(ROWS // 8):
        lhs = jnp.concatenate([top[8 * g : 8 * g + 8], bottom[8 * g : 8 * g + 8]], axis=0).astype(BF16)
        ref, n = (w_ref[g // 3], g % 3) if isinstance(w_ref, tuple) else (w_ref, g)
        r = jnp.dot(lhs, ref[:, 512 * n : 512 * n + 512], preferred_element_type=F32)
        s = r[:8] + r[8:]
        own = lax.broadcasted_iota(jnp.int32, s.shape, 0) == lax.broadcasted_iota(jnp.int32, s.shape, 1) // BS
        s = jnp.where(own, s, 0.0)
        t = (s[:, 0:128] + s[:, 128:256]) + (s[:, 256:384] + s[:, 384:512])
        out.append(t + swap(t))
    return jnp.concatenate(out, axis=0)


def smooth(x, wj_ref):
    top, bottom = lhs_parts(pack(x))
    return row_blocks(top, bottom, wj_ref)


def operate(packed, w_ref, gather_ref):
    e = jnp.concatenate([packed, jnp.zeros((128 - EXT, 128), F32)], axis=0)
    s = swap(e)
    low = low_lanes(e)
    zero = jnp.zeros_like(e)
    rhs = jnp.concatenate(
        [
            jnp.concatenate([jnp.where(low, e, zero), jnp.where(low, s, zero)], axis=1),
            jnp.concatenate([jnp.where(low, zero, s), jnp.where(low, zero, e)], axis=1),
        ],
        axis=0,
    ).astype(BF16)
    x = jnp.dot(gather_ref[...], rhs, preferred_element_type=F32)
    high = [x[ROWS * p : ROWS * p + ROWS, 0:128] for p in range(3)]
    rest = [x[ROWS * p : ROWS * p + ROWS, 128:256] for p in range(3)]
    top, bottom = lhs_parts(packed[:ROWS])
    none = [jnp.zeros((ROWS, 128), F32)] * 3
    return row_blocks(
        jnp.concatenate(high + high + [top], axis=1), jnp.concatenate(rest + none + [bottom], axis=1), w_ref
    )


def send_lists(packed, pick_ref, outs):
    picked = jnp.dot(pick_ref[...], packed.astype(BF16), preferred_element_type=F32)
    for s, out in enumerate(outs):
        out[...] = picked[HALO * s : HALO * s + HALO]


def pair_rows(x):
    t = twice(x).T
    high = t.astype(BF16).astype(F32)
    return jnp.where(lax.broadcasted_iota(jnp.int32, t.shape, 0) < BS, high, t - high).astype(BF16)


def column(line):
    line = jnp.concatenate([line, jnp.zeros((1, 128 - line.shape[1]), F32)], axis=1)
    return jnp.broadcast_to(line, (128, 128)).T


def first_kernel(*refs):
    sources, off, rest = refs[:8], refs[8], refs[9:]
    v, wj, ptd, pick, z, ze, ids, extra, slopes, s0, s1, s2, s3, near = rest[:14]
    here, sems, far = rest[14:22], rest[22], rest[23]
    copies = [pltpu.make_async_copy(x, y, sems.at[n]) for n, (x, y) in enumerate(zip(sources, here))]
    for c in copies:
        c.start()
    ahead = pltpu.make_async_copy(off.at[pl.ds(0, ROWS // 2)], near, far)
    ahead.start()
    for c in copies:
        c.wait()
    start, jac, pt, inverse, listed, owner, slot, shifts = here
    v[...] = twice(start[...])
    for n in range(ROWS // 2):
        wj[:, 128 * n : 128 * n + 128] = pair_rows(jac[128 * n : 128 * n + 128, :] * jacobi_weight)
    z[...] = smooth(v[...], wj)
    ze[...] = pack(z[...])
    odd_x = lax.axis_index("gx") % 2 == 1
    odd_y = lax.axis_index("gy") % 2 == 1
    lists = listed[...].astype(F32)
    order = [
        jnp.where(odd_x, lists[1:2], lists[0:1]),
        jnp.where(odd_x, lists[0:1], lists[1:2]),
        jnp.where(odd_y, lists[3:4], lists[2:3]),
        jnp.where(odd_y, lists[2:3], lists[3:4]),
    ]
    chosen = jnp.concatenate([column(x)[0:HALO, 0:ROWS] for x in order], axis=0)
    chosen = (chosen == lax.broadcasted_iota(jnp.int32, (4 * HALO, ROWS), 1).astype(F32)).astype(F32)
    pick[...] = chosen.astype(BF16)
    number = (owner[...] * 24 + slot[...]).astype(F32)
    ids[...] = column(number)[0:ROWS]
    for c in range(CW):
        ptd[c] = twice(pt[:, c, :])
    low = lax.broadcasted_iota(jnp.int32, (ROWS, 128), 1) < BS
    parts = [jnp.where(low, ptd[r], ptd[r + 4]) for r in range(4)] + [ids[...]]
    parts = [jnp.dot(chosen, x, precision=lax.Precision.HIGHEST, preferred_element_type=F32) for x in parts]
    parts = [jnp.dot(pick[...], ze[...].astype(BF16), preferred_element_type=F32)] + parts
    for s, out in enumerate((s0, s1, s2, s3)):
        for k, x in enumerate(parts):
            out[k] = x[HALO * s : HALO * s + HALO]
    wide = jnp.concatenate([inverse[...], jnp.zeros((BS, 104), F32)], axis=1)
    wide = jnp.concatenate([wide, jnp.zeros((BS, 128), F32)], axis=0).T[0:24]
    extra[4:16, :] = wide[0:12] + swap(wide[12:24])
    number = jnp.concatenate([number, jnp.zeros((1, 128 - ROWS), F32)], axis=1)
    lane = lax.broadcasted_iota(jnp.int32, (1, 128), 1)
    spare = (lane >= ROWS) & (lane < BS)
    for r in range(3):
        extra[r : r + 1, :] = jnp.where(spare, pltpu.roll(jnp.broadcast_to(number, (8, 128)), ROWS - 16 * r, 1)[0:1], 0.0)
    extra[3:4, :] = jnp.zeros((1, 128), F32)
    for k in range(4):
        slopes[k : k + 1, :] = jnp.broadcast_to(shifts[:, k : k + 1], (1, 128))
    ahead.wait()


def pack_rows(buf, dbuf, n, g, w):
    at = slice(BS * n, BS * n + 128)
    for p in range(3):
        x = jnp.concatenate(
            [
                jnp.concatenate([buf[n, 2 * p], buf[n, 2 * p + 1]], axis=1),
                jnp.concatenate([buf[n + 1, 2 * p], buf[n + 1, 2 * p + 1]], axis=1),
            ],
            axis=0,
        ).T
        high = x.astype(BF16)
        w[128 * p : 128 * p + 128, at] = high
        w[384 + 128 * p : 512 + 128 * p, at] = (x - high.astype(F32)).astype(BF16)
    w[768:896, at] = pair_rows(jnp.concatenate([dbuf[g + n], dbuf[g + n + 1]], axis=0))


def operator_kernel(off, diag, cols, near, wa, wb, gather, buf, dbuf, cbuf, sems):
    half = ROWS // 2
    named = pltpu.make_async_copy(cols, cbuf, sems.at[0])
    named.start()
    middle = pltpu.make_async_copy(diag, dbuf, sems.at[1])
    middle.start()
    later = [
        pltpu.make_async_copy(off.at[pl.ds(half + 8 * g, 8)], buf.at[pl.ds(8 * g, 8)], sems.at[2 + g]) for g in range(3)
    ]
    for c in later:
        c.start()
    named.wait()
    turn_x = (1 - lax.axis_index("gx") % 2) * HALO
    turn_y = (1 - lax.axis_index("gy") % 2) * HALO
    number = cbuf[...]
    beyond = number - ROWS
    turned = ROWS + (beyond ^ jnp.where(beyond < 2 * HALO, turn_x, turn_y))
    number = jnp.where(beyond >= 0, turned, number).astype(F32)
    number = jnp.concatenate([number, jnp.zeros((KOFF, 128 - ROWS), F32)], axis=1)
    number = jnp.concatenate([number, jnp.zeros((128 - KOFF, 128), F32)], axis=0).T[0:ROWS]
    lane = lax.broadcasted_iota(jnp.int32, (ROWS, 256), 1).astype(F32)
    for p in range(3):
        hit = (lane == number[:, 2 * p : 2 * p + 1]) | (lane == number[:, 2 * p + 1 : 2 * p + 2] + 128.0)
        gather[ROWS * p : ROWS * p + ROWS, :] = hit.astype(F32).astype(BF16)
    middle.wait()
    for n in range(0, half, 2):
        pack_rows(near, dbuf, n, 0, wa)
    for g in range(3):
        later[g].wait()
        for n in range(8 * g, 8 * g + 8, 2):
            pack_rows(buf, dbuf, n, half, wb)


def restrict_kernel(v, ze, h0, h1, h2, h3, wa, wb, gather, ptd, *rest):
    *extra, w, p = rest
    ext = jnp.concatenate([ze[...], h0[...], h1[...], h2[...], h3[...]], axis=0)
    r = v[...] - operate(ext, (wa, wb), gather)
    w[...] = r
    ones = jnp.ones((16, 128), BF16)
    pad = jnp.zeros((16, 128), F32)
    for k in range(4):
        x = jnp.concatenate([pack(ptd[k] * r), pad, pack(ptd[k + 4] * r), pad], axis=0).astype(BF16)
        line = lax.dot_general(ones, x, LAST, preferred_element_type=F32)[0:1]
        p[k : k + 1, :] = line + extra[0][k : k + 1, :] if extra else line
    if extra:
        p[4:16, :] = extra[0][4:16, :]


def coarse_kernel(x0, ids, ptd, g0, g1, g2, g3, mask, pte, xp):
    idc = jnp.concatenate(
        [ids[...], g0[5], g1[5], g2[5], g3[5], jnp.full((128 - EXT, 128), -1.0, F32)], axis=0
    )
    wanted = idc.T[0:1]
    given = [x0[:, r, :].T[ROWS:BS] for r in range(3)] + [jnp.full((BS - ROWS, 128), -1.0, F32)]
    given = jnp.concatenate(given + given, axis=0)
    for q in range(64):
        line = jnp.concatenate([given[0:BS, 2 * q : 2 * q + 1], given[BS:128, 2 * q + 1 : 2 * q + 2]], axis=0)
        mask[128 * q : 128 * q + 128, :] = (line == wanted).astype(F32).astype(BF16)
        xp[q] = jnp.concatenate([x0[2 * q, 0:4, :], x0[2 * q + 1, 0:4, :]], axis=0)
    device = jnp.floor((idc + 0.5) * (1.0 / 24.0))
    slot = idc - 24.0 * device
    upper = slot >= 11.5
    place = device * 16.0 + 4.0 + jnp.where(upper, slot - 12.0, slot)
    total = jnp.zeros((128, 128), F32)
    for b in range(8):
        src = x0[16 * b : 16 * b + 16].reshape(256, 128)
        high = src.astype(BF16)
        mid = (src - high.astype(F32)).astype(BF16)
        rest = (src - high.astype(F32) - mid.astype(F32)).astype(BF16)
        lane = lax.broadcasted_iota(jnp.int32, (128, 256), 1).astype(F32) + 256.0 * b
        hit = (twice(place) == lane).astype(F32).astype(BF16)
        got = jnp.dot(hit, jnp.concatenate([high, mid, rest], axis=1), preferred_element_type=F32)
        total = total + (got[:, 0:128] + got[:, 128:256] + got[:, 256:384])
    inverse = jnp.where(upper, swap(total), total)[:EXT]
    wide = []
    for c in range(CW):
        around = [g[1 + c % 4] for g in (g0, g1, g2, g3)]
        around = jnp.concatenate(around, axis=0)
        lowh = low_lanes(around)
        turned = swap(around)
        around = jnp.where(lowh, around, turned) if c < 4 else jnp.where(lowh, turned, around)
        wide.append(jnp.concatenate([ptd[c], around], axis=0))
    for d in range(CW):
        acc = wide[0] * inverse[:, d : d + 1]
        for c in range(1, CW):
            acc = acc + wide[c] * inverse[:, c * CW + d : c * CW + d + 1]
        pte[d] = acc


def correct_kernel(x, mask, pte, z, w, wa, wb, gather, wj, pick, ye, s0, s1, s2, s3, parts):
    sub = lax.broadcasted_iota(jnp.int32, (8, 128), 0) < 4
    lane = lax.broadcasted_iota(jnp.int32, (8, 128), 1) < BS
    keep = sub == lane
    for q in range(64):
        t = x[q]
        t = jnp.where(keep, t, pltpu.roll(swap(t), 4, 0))
        high = t.astype(BF16).astype(F32)
        parts[:, 128 * q : 128 * q + 128] = jnp.concatenate([high, t - high], axis=0).astype(BF16)
    got = jnp.dot(parts[...], mask[...], preferred_element_type=F32)
    coarse = jnp.concatenate([got[0:8] + got[8:16], jnp.zeros((120, 128), F32)], axis=0).T[:EXT]
    u = pte[0] * coarse[:, 0:1]
    for d in range(1, CW):
        u = u + pte[d] * coarse[:, d : d + 1]
    r = w[...] - operate(pack(u), (wa, wb), gather)
    y = z[...] + u[:ROWS] + smooth(r, wj)
    ye[...] = pack(y)
    send_lists(ye[...], pick, (s0, s1, s2, s3))


def advance(k, shifts, v, ye, h0, h1, h2, h3, w_op, gather):
    ext = jnp.concatenate([ye[...], h0[...], h1[...], h2[...], h3[...]], axis=0)
    return operate(ext, w_op, gather) - shifts[k : k + 1, :] * v[...]


def advance_kernel(k, shifts, v, ye, h0, h1, h2, h3, wa, wb, gather, wj, pick, vn, z, ze, s0, s1, s2, s3):
    vn[...] = advance(k, shifts, v, ye, h0, h1, h2, h3, (wa, wb), gather)
    z[...] = smooth(vn[...], wj)
    ze[...] = pack(z[...])
    send_lists(ze[...], pick, (s0, s1, s2, s3))


def last_kernel(shifts, ye, h0, h1, h2, h3, wa, wb, gather, v0, v1, v2, v3, v4, gram):
    v4[...] = advance(3, shifts, v3, ye, h0, h1, h2, h3, (wa, wb), gather)
    basis = [v[...] for v in (v0, v1, v2, v3, v4)]
    rows = []
    for j, l in PAIRS:
        rows.append(jnp.sum(basis[j] * basis[l], axis=0, keepdims=True))
    rows.append(jnp.zeros((128 - len(rows), 128), F32))
    rows = jnp.concatenate(rows, axis=0)
    sums = lax.dot_general(
        jnp.ones((8, 128), F32), rows, LAST, precision=lax.Precision.HIGHEST, preferred_element_type=F32
    )
    gram[...] = sums[0:1]


def orthogonal_kernel(total, grams, v0, v1, v2, v3, v4, q_out, r_out):
    sums = jnp.sum(grams[...], axis=0, keepdims=True) * (1.0 / (2.0 * total))
    g = {pair: sums[:, n : n + 1] for n, pair in enumerate(PAIRS)}
    lower = {}
    for j in range(5):
        d = g[(j, j)]
        for k in range(j):
            d = d - lower[(j, k)] * lower[(j, k)]
        lower[(j, j)] = jnp.sqrt(d)
        for i in range(j + 1, 5):
            t = g[(j, i)]
            for k in range(j):
                t = t - lower[(i, k)] * lower[(j, k)]
            lower[(i, j)] = t / lower[(j, j)]
    at_row = lax.broadcasted_iota(jnp.int32, (8, 128), 0)
    at_col = lax.broadcasted_iota(jnp.int32, (8, 128), 1)
    r = jnp.zeros((8, 128), F32)
    for (i, j), value in lower.items():
        r = jnp.where((at_row == j) & (at_col == i), value, r)
    r_out[...] = r[0:5, 0:5]
    solved = []
    for i, v in enumerate((v0, v1, v2, v3, v4)):
        t = v[...]
        for k in range(i):
            t = t - lower[(i, k)] * solved[k]
        t = t / lower[(i, i)]
        solved.append(t)
        q_out[i] = t[:, 0:BS]


def shape(*dims, dtype=F32):
    return jax.ShapeDtypeStruct(dims, dtype)


def kept(*dims, dtype=F32):
    return pltpu.VMEM(dims, dtype)


def call(kernel, outs, *args, specs=None, scratch=(), flops=2_000_000, name=None):
    return pl.pallas_call(
        kernel,
        out_shape=outs,
        in_specs=specs or [VM] * len(args),
        out_specs=jax.tree.map(lambda _: VM, outs),
        scratch_shapes=list(scratch),
        compiler_params=pltpu.CompilerParams(vmem_limit_bytes=24 << 20),
        cost_estimate=pl.CostEstimate(flops=flops, bytes_accessed=100_000, transcendentals=0),
        name=name,
    )(*args)


def swap_pairs(count, phase):
    if phase == 0:
        return [(i, i ^ 1) for i in range(count)]
    return [(i, (i - 1) % count if i % 2 == 0 else (i + 1) % count) for i in range(count)]


def exchange(sends):
    nx, ny = lax.axis_size("gx"), lax.axis_size("gy")
    b = lax.ppermute(sends[1], "gx", swap_pairs(nx, 1))
    d = lax.ppermute(sends[3], "gy", swap_pairs(ny, 1))
    a = lax.ppermute(sends[0], "gx", swap_pairs(nx, 0))
    c = lax.ppermute(sends[2], "gy", swap_pairs(ny, 0))
    return a, b, c, d


def everywhere(x):
    count = lax.axis_size("gx") * lax.axis_size("gy")
    y = jnp.broadcast_to(x[None], (count,) + x.shape)
    return lax.all_to_all(y, ("gx", "gy"), split_axis=0, concat_axis=0, tiled=True)


def per_device(start, shifts, diag_blocks, off_blocks, jacobi_inv, prolong, coarse_inv, cols, send_rows, owner, agg_slot):
    halo = [shape(HALO, 128)] * 4
    matrices = [pltpu.with_memory_space_constraint(x, pltpu.HBM) for x in (off_blocks, diag_blocks, jnp.transpose(cols))]
    sources = [
        start,
        jacobi_inv.reshape(ROWS * BS, BS),
        jnp.transpose(prolong, (0, 2, 1)),
        jnp.transpose(coarse_inv, (1, 2, 0)).reshape(BS, 24),
        send_rows[0],
        owner.reshape(1, ROWS),
        agg_slot.reshape(1, ROWS),
        shifts.reshape(1, 4),
    ]
    v, wj, ptd, pick, z, ze, id_col, extra, slopes, *sends, near = call(
        first_kernel,
        [
            shape(ROWS, 128),
            kept(128, ROWS * BS, dtype=BF16),
            shape(CW, ROWS, 128),
            shape(4 * HALO, ROWS, dtype=BF16),
            shape(ROWS, 128),
            shape(ROWS, 128),
            shape(ROWS, 128),
            shape(16, 128),
            shape(4, 128),
        ]
        + [shape(6, HALO, 128)] * 4
        + [kept(ROWS // 2, KOFF, BS, BS)],
        *[pltpu.with_memory_space_constraint(x, pltpu.HBM) for x in sources],
        matrices[0],
        specs=[HBM] * (len(sources) + 1),
        scratch=[pltpu.VMEM(x.shape, x.dtype) for x in sources]
        + [pltpu.SemaphoreType.DMA((len(sources),)), pltpu.SemaphoreType.DMA],
        name="first",
    )
    got = exchange(sends)
    half = kept(WIDTH, ROWS * BS // 2, dtype=BF16)
    *w_op, gather = call(
        operator_kernel,
        [half, half, shape(3 * ROWS, 256, dtype=BF16)],
        *matrices,
        near,
        specs=[HBM] * 3 + [VM],
        scratch=[
            pltpu.VMEM((ROWS // 2, KOFF, BS, BS), F32),
            pltpu.VMEM((ROWS, BS, BS), F32),
            pltpu.VMEM((KOFF, ROWS), jnp.int32),
            pltpu.SemaphoreType.DMA((5,)),
        ],
        flops=2_000_000_000,
        name="operator",
    )
    around = [g[0] for g in got]
    basis = [v]
    mask = pte = None
    for k in range(4):
        w, p = call(
            restrict_kernel,
            [shape(ROWS, 128), shape(4 if k else 16, 128)],
            v,
            ze,
            *around,
            *w_op,
            gather,
            ptd,
            *([] if k else [extra]),
            name="restrict",
        )
        x = everywhere(p)
        if k == 0:
            mask, pte, x = call(
                coarse_kernel,
                [kept(64 * 128, 128, dtype=BF16), shape(CW, EXT, 128), shape(64, 8, 128)],
                x,
                id_col,
                ptd,
                *got,
                name="coarse",
            )
        x = x.reshape(64, 8, 128)
        ye, *sends = call(
            correct_kernel,
            [shape(ROWS, 128)] + halo,
            x,
            mask,
            pte,
            z,
            w,
            *w_op,
            gather,
            wj,
            pick,
            scratch=[pltpu.VMEM((16, 64 * 128), BF16)],
            name="correct",
        )
        around = exchange(sends)
        if k < 3:
            v, z, ze, *sends = call(
                functools.partial(advance_kernel, k),
                [shape(ROWS, 128)] * 3 + halo,
                slopes,
                v,
                ye,
                *around,
                *w_op,
                gather,
                wj,
                pick,
                name="advance",
            )
            basis.append(v)
            around = exchange(sends)
    v, gram = call(
        last_kernel,
        [shape(ROWS, 128), shape(1, 128)],
        slopes,
        ye,
        *around,
        *w_op,
        gather,
        *basis,
        name="last",
    )
    basis.append(v)
    grams = everywhere(gram).reshape(128, 128)
    total = float(ROWS * BS * 128)
    return tuple(
        call(
            functools.partial(orthogonal_kernel, total),
            [shape(5, ROWS, BS), shape(5, 5)],
            grams,
            *basis,
            name="orthogonal",
        )
    )


def solution(mesh):
    rows = ("gx", "gy")
    in_specs = (
        P(rows, None),
        P(),
        P(rows, None, None),
        P(rows, None, None, None),
        P(rows, None, None),
        P(rows, None, None),
        P(rows, None, None),
        P(rows, None),
        P(rows, None, None),
        P(rows, None),
        P(rows),
    )
    return jax.shard_map(
        per_device, mesh=mesh, in_specs=in_specs, out_specs=(P(None, rows, None), P()), check_vma=False
    )
```

```python
import functools

import jax
import jax.numpy as jnp
from jax import lax
from jax.experimental import pallas as pl
from jax.experimental.pallas import tpu as pltpu
from jax.sharding import PartitionSpec as P

F32 = jnp.float32
BF16 = jnp.bfloat16
ROWS = 48
BS = 64
CW = 8
HALO = 16
EXT = ROWS + 4 * HALO
KOFF = 6
EARLY = 16
WIDTH = 7 * 128
jacobi_weight = 2.0 / 3.0
PAIRS = [(j, l) for l in range(5) for j in range(l + 1)]

VM = pl.BlockSpec(memory_space=pltpu.VMEM)
HBM = pl.BlockSpec(memory_space=pltpu.HBM)
LAST = (((1,), (1,)), ((), ()))


def low_lanes(x):
    return lax.broadcasted_iota(jnp.int32, x.shape, 1) < BS


def swap(x):
    return pltpu.roll(x, BS, 1)


def twice(x):
    return jnp.concatenate([x, x], axis=1)


def pack(x):
    high = x.astype(BF16).astype(F32)
    return jnp.where(low_lanes(x), high, (x - high).astype(BF16).astype(F32))


def lhs_parts(packed):
    low = low_lanes(packed)
    turned = swap(packed)
    return jnp.where(low, packed, turned), jnp.where(low, turned, 0.0)


def row_blocks(top, bottom, w_ref):
    out = []
    for g in range(ROWS // 8):
        lhs = jnp.concatenate([top[8 * g : 8 * g + 8], bottom[8 * g : 8 * g + 8]], axis=0).astype(BF16)
        ref, n = (w_ref[g // 3], g % 3) if isinstance(w_ref, tuple) else (w_ref, g)
        r = jnp.dot(lhs, ref[:, 512 * n : 512 * n + 512], preferred_element_type=F32)
        s = r[:8] + r[8:]
        own = lax.broadcasted_iota(jnp.int32, s.shape, 0) == lax.broadcasted_iota(jnp.int32, s.shape, 1) // BS
        s = jnp.where(own, s, 0.0)
        t = (s[:, 0:128] + s[:, 128:256]) + (s[:, 256:384] + s[:, 384:512])
        out.append(t + swap(t))
    return jnp.concatenate(out, axis=0)


def smooth(x, wj_ref):
    top, bottom = lhs_parts(pack(x))
    return row_blocks(top, bottom, wj_ref)


def operate(packed, w_ref, gather_ref):
    e = jnp.concatenate([packed, jnp.zeros((128 - EXT, 128), F32)], axis=0)
    s = swap(e)
    low = low_lanes(e)
    zero = jnp.zeros_like(e)
    rhs = jnp.concatenate(
        [
            jnp.concatenate([jnp.where(low, e, zero), jnp.where(low, s, zero)], axis=1),
            jnp.concatenate([jnp.where(low, zero, s), jnp.where(low, zero, e)], axis=1),
        ],
        axis=0,
    ).astype(BF16)
    x = jnp.dot(gather_ref[...], rhs, preferred_element_type=F32)
    high = [x[ROWS * p : ROWS * p + ROWS, 0:128] for p in range(3)]
    rest = [x[ROWS * p : ROWS * p + ROWS, 128:256] for p in range(3)]
    top, bottom = lhs_parts(packed[:ROWS])
    none = [jnp.zeros((ROWS, 128), F32)] * 3
    return row_blocks(
        jnp.concatenate(high + high + [top], axis=1), jnp.concatenate(rest + none + [bottom], axis=1), w_ref
    )


def send_lists(packed, pick_ref, outs):
    picked = jnp.dot(pick_ref[...], packed.astype(BF16), preferred_element_type=F32)
    for s, out in enumerate(outs):
        out[...] = picked[HALO * s : HALO * s + HALO]


def pair_rows(x):
    t = twice(x).T
    high = t.astype(BF16).astype(F32)
    return jnp.where(lax.broadcasted_iota(jnp.int32, t.shape, 0) < BS, high, t - high).astype(BF16)


def column(line):
    line = jnp.concatenate([line, jnp.zeros((1, 128 - line.shape[1]), F32)], axis=1)
    return jnp.broadcast_to(line, (128, 128)).T


def first_kernel(*refs):
    sources, off, rest = refs[:8], refs[8], refs[9:]
    v, wj, ptd, pick, z, ze, ids, extra, slopes, s0, s1, s2, s3, near = rest[:14]
    here, sems, far = rest[14:22], rest[22], rest[23]
    copies = [pltpu.make_async_copy(x, y, sems.at[n]) for n, (x, y) in enumerate(zip(sources, here))]
    for c in copies:
        c.start()
    ahead = pltpu.make_async_copy(off.at[pl.ds(0, EARLY)], near, far)
    ahead.start()
    for c in copies:
        c.wait()
    start, jac, pt, inverse, listed, owner, slot, shifts = here
    v[...] = twice(start[...])
    for n in range(ROWS // 2):
        wj[:, 128 * n : 128 * n + 128] = pair_rows(jac[128 * n : 128 * n + 128, :] * jacobi_weight)
    z[...] = smooth(v[...], wj)
    ze[...] = pack(z[...])
    even_x = lax.axis_index("gx") % 2 == 0
    even_y = lax.axis_index("gy") % 2 == 0
    lists = listed[...].astype(F32)
    order = [
        jnp.where(even_x, lists[1:2], lists[0:1]),
        jnp.where(even_x, lists[0:1], lists[1:2]),
        jnp.where(even_y, lists[3:4], lists[2:3]),
        jnp.where(even_y, lists[2:3], lists[3:4]),
    ]
    chosen = jnp.concatenate([column(x)[0:HALO, 0:ROWS] for x in order], axis=0)
    chosen = (chosen == lax.broadcasted_iota(jnp.int32, (4 * HALO, ROWS), 1).astype(F32)).astype(F32)
    pick[...] = chosen.astype(BF16)
    number = (owner[...] * 24 + slot[...]).astype(F32)
    ids[...] = column(number)[0:ROWS]
    for c in range(CW):
        ptd[c] = twice(pt[:, c, :])
    low = lax.broadcasted_iota(jnp.int32, (ROWS, 128), 1) < BS
    parts = [jnp.where(low, ptd[r], ptd[r + 4]) for r in range(4)] + [ids[...]]
    parts = [jnp.dot(chosen, x, precision=lax.Precision.HIGHEST, preferred_element_type=F32) for x in parts]
    parts = [jnp.dot(pick[...], ze[...].astype(BF16), preferred_element_type=F32)] + parts
    for s, out in enumerate((s0, s1, s2, s3)):
        for k, x in enumerate(parts):
            out[k] = x[HALO * s : HALO * s + HALO]
    wide = jnp.concatenate([inverse[...], jnp.zeros((BS, 104), F32)], axis=1)
    wide = jnp.concatenate([wide, jnp.zeros((BS, 128), F32)], axis=0).T[0:24]
    extra[4:16, :] = wide[0:12] + swap(wide[12:24])
    number = jnp.concatenate([number, jnp.zeros((1, 128 - ROWS), F32)], axis=1)
    lane = lax.broadcasted_iota(jnp.int32, (1, 128), 1)
    spare = (lane >= ROWS) & (lane < BS)
    for r in range(3):
        extra[r : r + 1, :] = jnp.where(spare, pltpu.roll(jnp.broadcast_to(number, (8, 128)), ROWS - 16 * r, 1)[0:1], 0.0)
    extra[3:4, :] = jnp.zeros((1, 128), F32)
    for k in range(4):
        slopes[k : k + 1, :] = jnp.broadcast_to(shifts[:, k : k + 1], (1, 128))
    ahead.wait()


def pack_rows(buf, n, dbuf, row, w):
    at = BS * (row % (ROWS // 2))
    at = slice(at, at + 128)
    for p in range(3):
        x = jnp.concatenate(
            [
                jnp.concatenate([buf[n, 2 * p], buf[n, 2 * p + 1]], axis=1),
                jnp.concatenate([buf[n + 1, 2 * p], buf[n + 1, 2 * p + 1]], axis=1),
            ],
            axis=0,
        ).T
        high = x.astype(BF16)
        w[128 * p : 128 * p + 128, at] = high
        w[384 + 128 * p : 512 + 128 * p, at] = (x - high.astype(F32)).astype(BF16)
    w[768:896, at] = pair_rows(jnp.concatenate([dbuf[row], dbuf[row + 1]], axis=0))


def operator_kernel(off, diag, cols, near, wa, wb, gather, buf, dbuf, cbuf, sems):
    steps = (ROWS - EARLY) // 8
    named = pltpu.make_async_copy(cols, cbuf, sems.at[0])
    named.start()
    middle = pltpu.make_async_copy(diag, dbuf, sems.at[1])
    middle.start()
    later = [
        pltpu.make_async_copy(off.at[pl.ds(EARLY + 8 * g, 8)], buf.at[pl.ds(8 * g, 8)], sems.at[2 + g])
        for g in range(steps)
    ]
    for c in later:
        c.start()
    named.wait()
    turn_x = (lax.axis_index("gx") % 2) * HALO
    turn_y = (lax.axis_index("gy") % 2) * HALO
    number = cbuf[...]
    beyond = number - ROWS
    turned = ROWS + (beyond ^ jnp.where(beyond < 2 * HALO, turn_x, turn_y))
    number = jnp.where(beyond >= 0, turned, number).astype(F32)
    number = jnp.concatenate([number, jnp.zeros((KOFF, 128 - ROWS), F32)], axis=1)
    number = jnp.concatenate([number, jnp.zeros((128 - KOFF, 128), F32)], axis=0).T[0:ROWS]
    lane = lax.broadcasted_iota(jnp.int32, (ROWS, 256), 1).astype(F32)
    for p in range(3):
        hit = (lane == number[:, 2 * p : 2 * p + 1]) | (lane == number[:, 2 * p + 1 : 2 * p + 2] + 128.0)
        gather[ROWS * p : ROWS * p + ROWS, :] = hit.astype(F32).astype(BF16)
    middle.wait()
    for n in range(0, EARLY, 2):
        pack_rows(near, n, dbuf, n, wa)
    for g in range(steps):
        later[g].wait()
        for n in range(8 * g, 8 * g + 8, 2):
            pack_rows(buf, n, dbuf, EARLY + n, wa if EARLY + n < ROWS // 2 else wb)


def restrict_kernel(v, ze, h0, h1, h2, h3, wa, wb, gather, ptd, *rest):
    *extra, w, p = rest
    ext = jnp.concatenate([ze[...], h0[...], h1[...], h2[...], h3[...]], axis=0)
    r = v[...] - operate(ext, (wa, wb), gather)
    w[...] = r
    ones = jnp.ones((16, 128), BF16)
    pad = jnp.zeros((16, 128), F32)
    for k in range(4):
        x = jnp.concatenate([pack(ptd[k] * r), pad, pack(ptd[k + 4] * r), pad], axis=0).astype(BF16)
        line = lax.dot_general(ones, x, LAST, preferred_element_type=F32)[0:1]
        p[k : k + 1, :] = line + extra[0][k : k + 1, :] if extra else line
    if extra:
        p[4:16, :] = extra[0][4:16, :]


def coarse_kernel(x0, ids, ptd, g0, g1, g2, g3, mask, pte, xp):
    idc = jnp.concatenate(
        [ids[...], g0[5], g1[5], g2[5], g3[5], jnp.full((128 - EXT, 128), -1.0, F32)], axis=0
    )
    wanted = idc.T[0:1]
    given = [x0[:, r, :].T[ROWS:BS] for r in range(3)] + [jnp.full((BS - ROWS, 128), -1.0, F32)]
    given = jnp.concatenate(given + given, axis=0)
    for q in range(64):
        line = jnp.concatenate([given[0:BS, 2 * q : 2 * q + 1], given[BS:128, 2 * q + 1 : 2 * q + 2]], axis=0)
        mask[128 * q : 128 * q + 128, :] = (line == wanted).astype(F32).astype(BF16)
        xp[q] = jnp.concatenate([x0[2 * q, 0:4, :], x0[2 * q + 1, 0:4, :]], axis=0)
    device = jnp.floor((idc + 0.5) * (1.0 / 24.0))
    slot = idc - 24.0 * device
    upper = slot >= 11.5
    place = device * 16.0 + 4.0 + jnp.where(upper, slot - 12.0, slot)
    high, rest = [], []
    for b in range(8):
        src = x0[16 * b : 16 * b + 16].reshape(256, 128)
        high.append(src.astype(BF16))
        rest.append((src - high[-1].astype(F32)).astype(BF16))
    lane = lax.broadcasted_iota(jnp.int32, (128, 128), 1).astype(F32)
    hit = jnp.concatenate([(place - 128.0 * b == lane).astype(F32).astype(BF16) for b in range(16)], axis=1)
    source = jnp.concatenate([jnp.concatenate(high, axis=0), jnp.concatenate(rest, axis=0)], axis=1)
    total = jnp.dot(hit, source, preferred_element_type=F32)
    total = total[:, 0:128] + total[:, 128:256]
    inverse = jnp.where(upper, swap(total), total)[:EXT]
    wide = []
    for c in range(CW):
        around = [g[1 + c % 4] for g in (g0, g1, g2, g3)]
        around = jnp.concatenate(around, axis=0)
        lowh = low_lanes(around)
        turned = swap(around)
        around = jnp.where(lowh, around, turned) if c < 4 else jnp.where(lowh, turned, around)
        wide.append(jnp.concatenate([ptd[c], around], axis=0))
    for d in range(CW):
        acc = wide[0] * inverse[:, d : d + 1]
        for c in range(1, CW):
            acc = acc + wide[c] * inverse[:, c * CW + d : c * CW + d + 1]
        pte[d] = acc


def correct_kernel(x, mask, pte, z, w, wa, wb, gather, wj, pick, ye, s0, s1, s2, s3, parts):
    sub = lax.broadcasted_iota(jnp.int32, (8, 128), 0) < 4
    lane = lax.broadcasted_iota(jnp.int32, (8, 128), 1) < BS
    keep = sub == lane
    for q in range(64):
        t = x[q]
        t = jnp.where(keep, t, pltpu.roll(swap(t), 4, 0))
        high = t.astype(BF16).astype(F32)
        parts[:, 128 * q : 128 * q + 128] = jnp.concatenate([high, t - high], axis=0).astype(BF16)
    got = jnp.dot(parts[...], mask[...], preferred_element_type=F32)
    coarse = jnp.concatenate([got[0:8] + got[8:16], jnp.zeros((120, 128), F32)], axis=0).T[:EXT]
    u = pte[0] * coarse[:, 0:1]
    for d in range(1, CW):
        u = u + pte[d] * coarse[:, d : d + 1]
    r = w[...] - operate(pack(u), (wa, wb), gather)
    y = z[...] + u[:ROWS] + smooth(r, wj)
    ye[...] = pack(y)
    send_lists(ye[...], pick, (s0, s1, s2, s3))


def advance(k, shifts, v, ye, h0, h1, h2, h3, w_op, gather):
    ext = jnp.concatenate([ye[...], h0[...], h1[...], h2[...], h3[...]], axis=0)
    return operate(ext, w_op, gather) - shifts[k : k + 1, :] * v[...]


def advance_kernel(k, shifts, v, ye, h0, h1, h2, h3, wa, wb, gather, wj, pick, vn, z, ze, s0, s1, s2, s3):
    vn[...] = advance(k, shifts, v, ye, h0, h1, h2, h3, (wa, wb), gather)
    z[...] = smooth(vn[...], wj)
    ze[...] = pack(z[...])
    send_lists(ze[...], pick, (s0, s1, s2, s3))


def products(basis, pairs):
    return [jnp.sum(basis[j] * basis[l], axis=0, keepdims=True) for j, l in pairs]


def known_kernel(v0, v1, v2, v3, known):
    basis = [v[...] for v in (v0, v1, v2, v3)]
    known[...] = jnp.concatenate(products(basis, PAIRS[:10]) + [jnp.zeros((6, 128), F32)], axis=0)


def last_kernel(slopes, ye, h0, h1, h2, h3, wa, wb, gather, v0, v1, v2, v3, known, v4, gram):
    v4[...] = advance(3, slopes, v3, ye, h0, h1, h2, h3, (wa, wb), gather)
    basis = [v[...] for v in (v0, v1, v2, v3, v4)]
    rows = [known[0:10, :]] + products(basis, PAIRS[10:]) + [jnp.zeros((113, 128), F32)]
    sums = lax.dot_general(
        jnp.ones((8, 128), F32),
        jnp.concatenate(rows, axis=0),
        LAST,
        precision=lax.Precision.HIGHEST,
        preferred_element_type=F32,
    )
    gram[...] = sums[0:1]


def orthogonal_kernel(total, grams, v0, v1, v2, v3, v4, q_out, r_out):
    sums = jnp.sum(grams[...], axis=0, keepdims=True) * (1.0 / (2.0 * total))
    g = {pair: sums[:, n : n + 1] for n, pair in enumerate(PAIRS)}
    lower = {}
    for j in range(5):
        d = g[(j, j)]
        for k in range(j):
            d = d - lower[(j, k)] * lower[(j, k)]
        lower[(j, j)] = jnp.sqrt(d)
        for i in range(j + 1, 5):
            t = g[(j, i)]
            for k in range(j):
                t = t - lower[(i, k)] * lower[(j, k)]
            lower[(i, j)] = t / lower[(j, j)]
    at_row = lax.broadcasted_iota(jnp.int32, (8, 128), 0)
    at_col = lax.broadcasted_iota(jnp.int32, (8, 128), 1)
    r = jnp.zeros((8, 128), F32)
    for (i, j), value in lower.items():
        r = jnp.where((at_row == j) & (at_col == i), value, r)
    r_out[...] = r[0:5, 0:5]
    solved = []
    for i, v in enumerate((v0, v1, v2, v3, v4)):
        t = v[...]
        for k in range(i):
            t = t - lower[(i, k)] * solved[k]
        t = t / lower[(i, i)]
        solved.append(t)
        q_out[i] = t[:, 0:BS]


def shape(*dims, dtype=F32):
    return jax.ShapeDtypeStruct(dims, dtype)


def kept(*dims, dtype=F32):
    return pltpu.VMEM(dims, dtype)


def call(kernel, outs, *args, specs=None, scratch=(), flops=2_000_000, name=None):
    return pl.pallas_call(
        kernel,
        out_shape=outs,
        in_specs=specs or [VM] * len(args),
        out_specs=jax.tree.map(lambda _: VM, outs),
        scratch_shapes=list(scratch),
        compiler_params=pltpu.CompilerParams(vmem_limit_bytes=24 << 20),
        cost_estimate=pl.CostEstimate(flops=flops, bytes_accessed=100_000, transcendentals=0),
        name=name,
    )(*args)


def swap_pairs(count, phase):
    if phase == 0:
        return [(i, i ^ 1) for i in range(count)]
    return [(i, (i - 1) % count if i % 2 == 0 else (i + 1) % count) for i in range(count)]


def exchange(sends):
    nx, ny = lax.axis_size("gx"), lax.axis_size("gy")
    return (
        lax.ppermute(sends[0], "gx", swap_pairs(nx, 1)),
        lax.ppermute(sends[1], "gx", swap_pairs(nx, 0)),
        lax.ppermute(sends[2], "gy", swap_pairs(ny, 1)),
        lax.ppermute(sends[3], "gy", swap_pairs(ny, 0)),
    )


def everywhere(x):
    count = lax.axis_size("gx") * lax.axis_size("gy")
    y = jnp.broadcast_to(x[None], (count,) + x.shape)
    return lax.all_to_all(y, ("gx", "gy"), split_axis=0, concat_axis=0, tiled=True)


def per_device(start, shifts, diag_blocks, off_blocks, jacobi_inv, prolong, coarse_inv, cols, send_rows, owner, agg_slot):
    halo = [shape(HALO, 128)] * 4
    matrices = [pltpu.with_memory_space_constraint(x, pltpu.HBM) for x in (off_blocks, diag_blocks, jnp.transpose(cols))]
    sources = [
        start,
        jacobi_inv.reshape(ROWS * BS, BS),
        jnp.transpose(prolong, (0, 2, 1)),
        jnp.transpose(coarse_inv, (1, 2, 0)).reshape(BS, 24),
        send_rows[0],
        owner.reshape(1, ROWS),
        agg_slot.reshape(1, ROWS),
        shifts.reshape(1, 4),
    ]
    v, wj, ptd, pick, z, ze, id_col, extra, slopes, *sends, near = call(
        first_kernel,
        [
            shape(ROWS, 128),
            kept(128, ROWS * BS, dtype=BF16),
            shape(CW, ROWS, 128),
            shape(4 * HALO, ROWS, dtype=BF16),
            shape(ROWS, 128),
            shape(ROWS, 128),
            shape(ROWS, 128),
            shape(16, 128),
            shape(4, 128),
        ]
        + [shape(6, HALO, 128)] * 4
        + [kept(EARLY, KOFF, BS, BS)],
        *[pltpu.with_memory_space_constraint(x, pltpu.HBM) for x in sources],
        matrices[0],
        specs=[HBM] * (len(sources) + 1),
        scratch=[pltpu.VMEM(x.shape, x.dtype) for x in sources]
        + [pltpu.SemaphoreType.DMA((len(sources),)), pltpu.SemaphoreType.DMA],
        name="first",
    )
    got = exchange(sends)
    half = kept(WIDTH, ROWS * BS // 2, dtype=BF16)
    *w_op, gather = call(
        operator_kernel,
        [half, half, shape(3 * ROWS, 256, dtype=BF16)],
        *matrices,
        near,
        specs=[HBM] * 3 + [VM],
        scratch=[
            pltpu.VMEM((ROWS - EARLY, KOFF, BS, BS), F32),
            pltpu.VMEM((ROWS, BS, BS), F32),
            pltpu.VMEM((KOFF, ROWS), jnp.int32),
            pltpu.SemaphoreType.DMA((2 + (ROWS - EARLY) // 8,)),
        ],
        flops=2_000_000_000,
        name="operator",
    )
    around = [g[0] for g in got]
    basis = [v]
    mask = pte = None
    for k in range(4):
        w, p = call(
            restrict_kernel,
            [shape(ROWS, 128), shape(4 if k else 16, 128)],
            v,
            ze,
            *around,
            *w_op,
            gather,
            ptd,
            *([] if k else [extra]),
            name="restrict",
        )
        x = everywhere(p)
        if k == 0:
            mask, pte, x = call(
                coarse_kernel,
                [kept(64 * 128, 128, dtype=BF16), shape(CW, EXT, 128), shape(64, 8, 128)],
                x,
                id_col,
                ptd,
                *got,
                name="coarse",
            )
        x = x.reshape(64, 8, 128)
        ye, *sends = call(
            correct_kernel,
            [shape(ROWS, 128)] + halo,
            x,
            mask,
            pte,
            z,
            w,
            *w_op,
            gather,
            wj,
            pick,
            scratch=[pltpu.VMEM((16, 64 * 128), BF16)],
            name="correct",
        )
        around = exchange(sends)
        if k < 3:
            v, z, ze, *sends = call(
                functools.partial(advance_kernel, k),
                [shape(ROWS, 128)] * 3 + halo,
                slopes,
                v,
                ye,
                *around,
                *w_op,
                gather,
                wj,
                pick,
                name="advance",
            )
            basis.append(v)
            around = exchange(sends)
    (known,) = call(known_kernel, [shape(16, 128)], *basis, flops=500_000_000, name="known")
    v, gram = call(
        last_kernel,
        [shape(ROWS, 128), shape(1, 128)],
        slopes,
        ye,
        *around,
        *w_op,
        gather,
        *basis,
        known,
        name="last",
    )
    basis.append(v)
    grams = everywhere(gram).reshape(128, 128)
    total = float(ROWS * BS * 128)
    return tuple(
        call(
            functools.partial(orthogonal_kernel, total),
            [shape(5, ROWS, BS), shape(5, 5)],
            grams,
            *basis,
            name="orthogonal",
        )
    )


def solution(mesh):
    rows = ("gx", "gy")
    in_specs = (
        P(rows, None),
        P(),
        P(rows, None, None),
        P(rows, None, None, None),
        P(rows, None, None),
        P(rows, None, None),
        P(rows, None, None),
        P(rows, None),
        P(rows, None, None),
        P(rows, None),
        P(rows),
    )
    return jax.shard_map(
        per_device, mesh=mesh, in_specs=in_specs, out_specs=(P(None, rows, None), P()), check_vma=False
    )
```

```python
import functools

import jax
import jax.numpy as jnp
from jax import lax
from jax.experimental import pallas as pl
from jax.experimental.pallas import tpu as pltpu
from jax.sharding import PartitionSpec as P

F32 = jnp.float32
BF16 = jnp.bfloat16
ROWS = 48
BS = 64
CW = 8
HALO = 16
EXT = ROWS + 4 * HALO
KOFF = 6
EARLY = 16
OWN = 6 * 128
WIDTH = 7 * 128
jacobi_weight = 2.0 / 3.0
PAIRS = [(j, l) for l in range(5) for j in range(l + 1)]

VM = pl.BlockSpec(memory_space=pltpu.VMEM)
HBM = pl.BlockSpec(memory_space=pltpu.HBM)
LAST = (((1,), (1,)), ((), ()))


def low_lanes(x):
    return lax.broadcasted_iota(jnp.int32, x.shape, 1) < BS


def swap(x):
    return pltpu.roll(x, BS, 1)


def twice(x):
    return jnp.concatenate([x, x], axis=1)


def pack(x):
    high = x.astype(BF16).astype(F32)
    return jnp.where(low_lanes(x), high, (x - high).astype(BF16).astype(F32))


def lhs_parts(packed):
    low = low_lanes(packed)
    turned = swap(packed)
    return jnp.where(low, packed, turned), jnp.where(low, turned, 0.0)


def row_blocks(top, bottom, w_ref, first=0):
    out = []
    for g in range(ROWS // 8):
        lhs = jnp.concatenate([top[8 * g : 8 * g + 8], bottom[8 * g : 8 * g + 8]], axis=0).astype(BF16)
        ref, n = (w_ref[g // 3], g % 3) if isinstance(w_ref, tuple) else (w_ref, g)
        r = jnp.dot(
            lhs, ref[first : first + top.shape[1], 512 * n : 512 * n + 512], preferred_element_type=F32
        )
        s = r[:8] + r[8:]
        own = lax.broadcasted_iota(jnp.int32, s.shape, 0) == lax.broadcasted_iota(jnp.int32, s.shape, 1) // BS
        s = jnp.where(own, s, 0.0)
        t = (s[:, 0:128] + s[:, 128:256]) + (s[:, 256:384] + s[:, 384:512])
        out.append(t + swap(t))
    return jnp.concatenate(out, axis=0)


def smooth(x, wj_ref):
    top, bottom = lhs_parts(pack(x))
    return row_blocks(top, bottom, wj_ref)


def operate_own(packed, w_ref):
    top, bottom = lhs_parts(packed)
    return row_blocks(top, bottom, w_ref, OWN)


def operate(packed, w_ref, gather_ref, own=True):
    e = jnp.concatenate([packed, jnp.zeros((128 - EXT, 128), F32)], axis=0)
    s = swap(e)
    low = low_lanes(e)
    zero = jnp.zeros_like(e)
    rhs = jnp.concatenate(
        [
            jnp.concatenate([jnp.where(low, e, zero), jnp.where(low, s, zero)], axis=1),
            jnp.concatenate([jnp.where(low, zero, s), jnp.where(low, zero, e)], axis=1),
        ],
        axis=0,
    ).astype(BF16)
    x = jnp.dot(gather_ref[...], rhs, preferred_element_type=F32)
    high = [x[ROWS * p : ROWS * p + ROWS, 0:128] for p in range(3)]
    rest = [x[ROWS * p : ROWS * p + ROWS, 128:256] for p in range(3)]
    none = [jnp.zeros((ROWS, 128), F32)] * 3
    top, bottom = high + high, rest + none
    if own:
        for x, part in zip((top, bottom), lhs_parts(packed[:ROWS])):
            x.append(part)
    return row_blocks(jnp.concatenate(top, axis=1), jnp.concatenate(bottom, axis=1), w_ref)


def send_lists(packed, pick_ref, outs):
    picked = jnp.dot(pick_ref[...], packed.astype(BF16), preferred_element_type=F32)
    for s, out in enumerate(outs):
        out[...] = picked[HALO * s : HALO * s + HALO]


def pair_rows(x):
    t = twice(x).T
    high = t.astype(BF16).astype(F32)
    return jnp.where(lax.broadcasted_iota(jnp.int32, t.shape, 0) < BS, high, t - high).astype(BF16)


def column(line):
    line = jnp.concatenate([line, jnp.zeros((1, 128 - line.shape[1]), F32)], axis=1)
    return jnp.broadcast_to(line, (128, 128)).T


def first_kernel(*refs):
    sources, off, rest = refs[:8], refs[8], refs[9:]
    v, wj, ptd, pick, z, ze, ids, extra, slopes, s0, s1, s2, s3, near = rest[:14]
    here, sems, far = rest[14:22], rest[22], rest[23]
    copies = [pltpu.make_async_copy(x, y, sems.at[n]) for n, (x, y) in enumerate(zip(sources, here))]
    for c in copies:
        c.start()
    ahead = pltpu.make_async_copy(off.at[pl.ds(0, EARLY)], near, far)
    ahead.start()
    for c in copies:
        c.wait()
    start, jac, pt, inverse, listed, owner, slot, shifts = here
    v[...] = twice(start[...])
    for n in range(ROWS // 2):
        wj[:, 128 * n : 128 * n + 128] = pair_rows(jac[128 * n : 128 * n + 128, :] * jacobi_weight)
    z[...] = smooth(v[...], wj)
    ze[...] = pack(z[...])
    even_x = lax.axis_index("gx") % 2 == 0
    even_y = lax.axis_index("gy") % 2 == 0
    lists = listed[...].astype(F32)
    order = [
        jnp.where(even_x, lists[1:2], lists[0:1]),
        jnp.where(even_x, lists[0:1], lists[1:2]),
        jnp.where(even_y, lists[3:4], lists[2:3]),
        jnp.where(even_y, lists[2:3], lists[3:4]),
    ]
    chosen = jnp.concatenate([column(x)[0:HALO, 0:ROWS] for x in order], axis=0)
    chosen = (chosen == lax.broadcasted_iota(jnp.int32, (4 * HALO, ROWS), 1).astype(F32)).astype(F32)
    pick[...] = chosen.astype(BF16)
    number = (owner[...] * 24 + slot[...]).astype(F32)
    ids[...] = column(number)[0:ROWS]
    for c in range(CW):
        ptd[c] = twice(pt[:, c, :])
    low = lax.broadcasted_iota(jnp.int32, (ROWS, 128), 1) < BS
    parts = [jnp.where(low, ptd[r], ptd[r + 4]) for r in range(4)] + [ids[...]]
    parts = [jnp.dot(chosen, x, precision=lax.Precision.HIGHEST, preferred_element_type=F32) for x in parts]
    parts = [jnp.dot(pick[...], ze[...].astype(BF16), preferred_element_type=F32)] + parts
    for s, out in enumerate((s0, s1, s2, s3)):
        for k, x in enumerate(parts):
            out[k] = x[HALO * s : HALO * s + HALO]
    wide = jnp.concatenate([inverse[...], jnp.zeros((BS, 104), F32)], axis=1)
    wide = jnp.concatenate([wide, jnp.zeros((BS, 128), F32)], axis=0).T[0:24]
    extra[4:16, :] = wide[0:12] + swap(wide[12:24])
    number = jnp.concatenate([number, jnp.zeros((1, 128 - ROWS), F32)], axis=1)
    lane = lax.broadcasted_iota(jnp.int32, (1, 128), 1)
    spare = (lane >= ROWS) & (lane < BS)
    for r in range(3):
        extra[r : r + 1, :] = jnp.where(spare, pltpu.roll(jnp.broadcast_to(number, (8, 128)), ROWS - 16 * r, 1)[0:1], 0.0)
    extra[3:4, :] = jnp.zeros((1, 128), F32)
    for k in range(4):
        slopes[k : k + 1, :] = jnp.broadcast_to(shifts[:, k : k + 1], (1, 128))
    ahead.wait()


def pack_rows(buf, n, dbuf, row, w):
    at = BS * (row % (ROWS // 2))
    at = slice(at, at + 128)
    for p in range(3):
        x = jnp.concatenate(
            [
                jnp.concatenate([buf[n, 2 * p], buf[n, 2 * p + 1]], axis=1),
                jnp.concatenate([buf[n + 1, 2 * p], buf[n + 1, 2 * p + 1]], axis=1),
            ],
            axis=0,
        ).T
        high = x.astype(BF16)
        w[128 * p : 128 * p + 128, at] = high
        w[384 + 128 * p : 512 + 128 * p, at] = (x - high.astype(F32)).astype(BF16)
    w[768:896, at] = pair_rows(jnp.concatenate([dbuf[row], dbuf[row + 1]], axis=0))


def operator_kernel(off, diag, cols, near, wa, wb, gather, buf, dbuf, cbuf, sems):
    steps = (ROWS - EARLY) // 8
    named = pltpu.make_async_copy(cols, cbuf, sems.at[0])
    named.start()
    middle = pltpu.make_async_copy(diag, dbuf, sems.at[1])
    middle.start()
    later = [
        pltpu.make_async_copy(off.at[pl.ds(EARLY + 8 * g, 8)], buf.at[pl.ds(8 * g, 8)], sems.at[2 + g])
        for g in range(steps)
    ]
    for c in later:
        c.start()
    named.wait()
    turn_x = (lax.axis_index("gx") % 2) * HALO
    turn_y = (lax.axis_index("gy") % 2) * HALO
    number = cbuf[...]
    beyond = number - ROWS
    turned = ROWS + (beyond ^ jnp.where(beyond < 2 * HALO, turn_x, turn_y))
    number = jnp.where(beyond >= 0, turned, number).astype(F32)
    number = jnp.concatenate([number, jnp.zeros((KOFF, 128 - ROWS), F32)], axis=1)
    number = jnp.concatenate([number, jnp.zeros((128 - KOFF, 128), F32)], axis=0).T[0:ROWS]
    lane = lax.broadcasted_iota(jnp.int32, (ROWS, 256), 1).astype(F32)
    for p in range(3):
        hit = (lane == number[:, 2 * p : 2 * p + 1]) | (lane == number[:, 2 * p + 1 : 2 * p + 2] + 128.0)
        gather[ROWS * p : ROWS * p + ROWS, :] = hit.astype(F32).astype(BF16)
    middle.wait()
    for n in range(0, EARLY, 2):
        pack_rows(near, n, dbuf, n, wa)
    for g in range(steps):
        later[g].wait()
        for n in range(8 * g, 8 * g + 8, 2):
            pack_rows(buf, n, dbuf, EARLY + n, wa if EARLY + n < ROWS // 2 else wb)


def before_restrict(v, ze, wa, wb, base):
    base[...] = v[...] - operate_own(ze[...], (wa, wb))


def before_advance(k, slopes, v, ye, wa, wb, base):
    base[...] = operate_own(ye[...], (wa, wb)) - slopes[k : k + 1, :] * v[...]


def restrict_kernel(base, ze, h0, h1, h2, h3, wa, wb, gather, ptd, *rest):
    *extra, w, p = rest
    ext = jnp.concatenate([ze[...], h0[...], h1[...], h2[...], h3[...]], axis=0)
    r = base[...] - operate(ext, (wa, wb), gather, own=False)
    w[...] = r
    ones = jnp.ones((16, 128), BF16)
    pad = jnp.zeros((16, 128), F32)
    for k in range(4):
        x = jnp.concatenate([pack(ptd[k] * r), pad, pack(ptd[k + 4] * r), pad], axis=0).astype(BF16)
        line = lax.dot_general(ones, x, LAST, preferred_element_type=F32)[0:1]
        p[k : k + 1, :] = line + extra[0][k : k + 1, :] if extra else line
    if extra:
        p[4:16, :] = extra[0][4:16, :]


def coarse_kernel(x0, ids, ptd, g0, g1, g2, g3, mask, pte, xp):
    idc = jnp.concatenate(
        [ids[...], g0[5], g1[5], g2[5], g3[5], jnp.full((128 - EXT, 128), -1.0, F32)], axis=0
    )
    wanted = idc.T[0:1]
    given = [x0[:, r, :].T[ROWS:BS] for r in range(3)] + [jnp.full((BS - ROWS, 128), -1.0, F32)]
    given = jnp.concatenate(given + given, axis=0)
    for q in range(64):
        line = jnp.concatenate([given[0:BS, 2 * q : 2 * q + 1], given[BS:128, 2 * q + 1 : 2 * q + 2]], axis=0)
        mask[128 * q : 128 * q + 128, :] = (line == wanted).astype(F32).astype(BF16)
        xp[q] = jnp.concatenate([x0[2 * q, 0:4, :], x0[2 * q + 1, 0:4, :]], axis=0)
    device = jnp.floor((idc + 0.5) * (1.0 / 24.0))
    slot = idc - 24.0 * device
    upper = slot >= 11.5
    place = device * 16.0 + 4.0 + jnp.where(upper, slot - 12.0, slot)
    high, rest = [], []
    for b in range(8):
        src = x0[16 * b : 16 * b + 16].reshape(256, 128)
        high.append(src.astype(BF16))
        rest.append((src - high[-1].astype(F32)).astype(BF16))
    lane = lax.broadcasted_iota(jnp.int32, (128, 128), 1).astype(F32)
    hit = jnp.concatenate([(place - 128.0 * b == lane).astype(F32).astype(BF16) for b in range(16)], axis=1)
    source = jnp.concatenate([jnp.concatenate(high, axis=0), jnp.concatenate(rest, axis=0)], axis=1)
    total = jnp.dot(hit, source, preferred_element_type=F32)
    total = total[:, 0:128] + total[:, 128:256]
    inverse = jnp.where(upper, swap(total), total)[:EXT]
    wide = []
    for c in range(CW):
        around = [g[1 + c % 4] for g in (g0, g1, g2, g3)]
        around = jnp.concatenate(around, axis=0)
        lowh = low_lanes(around)
        turned = swap(around)
        around = jnp.where(lowh, around, turned) if c < 4 else jnp.where(lowh, turned, around)
        wide.append(jnp.concatenate([ptd[c], around], axis=0))
    for d in range(CW):
        acc = wide[0] * inverse[:, d : d + 1]
        for c in range(1, CW):
            acc = acc + wide[c] * inverse[:, c * CW + d : c * CW + d + 1]
        pte[d] = acc


def correct_kernel(x, mask, pte, z, w, wa, wb, gather, wj, pick, ye, s0, s1, s2, s3, parts):
    sub = lax.broadcasted_iota(jnp.int32, (8, 128), 0) < 4
    lane = lax.broadcasted_iota(jnp.int32, (8, 128), 1) < BS
    keep = sub == lane
    for q in range(64):
        t = x[q]
        t = jnp.where(keep, t, pltpu.roll(swap(t), 4, 0))
        high = t.astype(BF16).astype(F32)
        parts[:, 128 * q : 128 * q + 128] = jnp.concatenate([high, t - high], axis=0).astype(BF16)
    got = jnp.dot(parts[...], mask[...], preferred_element_type=F32)
    coarse = jnp.concatenate([got[0:8] + got[8:16], jnp.zeros((120, 128), F32)], axis=0).T[:EXT]
    u = pte[0] * coarse[:, 0:1]
    for d in range(1, CW):
        u = u + pte[d] * coarse[:, d : d + 1]
    r = w[...] - operate(pack(u), (wa, wb), gather)
    y = z[...] + u[:ROWS] + smooth(r, wj)
    ye[...] = pack(y)
    send_lists(ye[...], pick, (s0, s1, s2, s3))


def advance(base, ye, h0, h1, h2, h3, w_op, gather):
    ext = jnp.concatenate([ye[...], h0[...], h1[...], h2[...], h3[...]], axis=0)
    return operate(ext, w_op, gather, own=False) + base[...]


def advance_kernel(base, ye, h0, h1, h2, h3, wa, wb, gather, wj, pick, vn, z, ze, s0, s1, s2, s3):
    vn[...] = advance(base, ye, h0, h1, h2, h3, (wa, wb), gather)
    z[...] = smooth(vn[...], wj)
    ze[...] = pack(z[...])
    send_lists(ze[...], pick, (s0, s1, s2, s3))


def products(basis, pairs):
    return [jnp.sum(basis[j] * basis[l], axis=0, keepdims=True) for j, l in pairs]


def known_kernel(v0, v1, v2, v3, known):
    basis = [v[...] for v in (v0, v1, v2, v3)]
    known[...] = jnp.concatenate(products(basis, PAIRS[:10]) + [jnp.zeros((6, 128), F32)], axis=0)


def last_kernel(base, ye, h0, h1, h2, h3, wa, wb, gather, v0, v1, v2, v3, known, v4, gram):
    v4[...] = advance(base, ye, h0, h1, h2, h3, (wa, wb), gather)
    basis = [v[...] for v in (v0, v1, v2, v3, v4)]
    rows = [known[0:10, :]] + products(basis, PAIRS[10:]) + [jnp.zeros((113, 128), F32)]
    sums = lax.dot_general(
        jnp.ones((8, 128), F32),
        jnp.concatenate(rows, axis=0),
        LAST,
        precision=lax.Precision.HIGHEST,
        preferred_element_type=F32,
    )
    gram[...] = sums[0:1]


def orthogonal_kernel(total, grams, v0, v1, v2, v3, v4, q_out, r_out):
    sums = jnp.sum(grams[...], axis=0, keepdims=True) * (1.0 / (2.0 * total))
    g = {pair: sums[:, n : n + 1] for n, pair in enumerate(PAIRS)}
    lower = {}
    for j in range(5):
        d = g[(j, j)]
        for k in range(j):
            d = d - lower[(j, k)] * lower[(j, k)]
        lower[(j, j)] = jnp.sqrt(d)
        for i in range(j + 1, 5):
            t = g[(j, i)]
            for k in range(j):
                t = t - lower[(i, k)] * lower[(j, k)]
            lower[(i, j)] = t / lower[(j, j)]
    at_row = lax.broadcasted_iota(jnp.int32, (8, 128), 0)
    at_col = lax.broadcasted_iota(jnp.int32, (8, 128), 1)
    r = jnp.zeros((8, 128), F32)
    for (i, j), value in lower.items():
        r = jnp.where((at_row == j) & (at_col == i), value, r)
    r_out[...] = r[0:5, 0:5]
    solved = []
    for i, v in enumerate((v0, v1, v2, v3, v4)):
        t = v[...]
        for k in range(i):
            t = t - lower[(i, k)] * solved[k]
        t = t / lower[(i, i)]
        solved.append(t)
        q_out[i] = t[:, 0:BS]


def shape(*dims, dtype=F32):
    return jax.ShapeDtypeStruct(dims, dtype)


def kept(*dims, dtype=F32):
    return pltpu.VMEM(dims, dtype)


def call(kernel, outs, *args, specs=None, scratch=(), flops=2_000_000, name=None):
    return pl.pallas_call(
        kernel,
        out_shape=outs,
        in_specs=specs or [VM] * len(args),
        out_specs=jax.tree.map(lambda _: VM, outs),
        scratch_shapes=list(scratch),
        compiler_params=pltpu.CompilerParams(vmem_limit_bytes=24 << 20),
        cost_estimate=pl.CostEstimate(flops=flops, bytes_accessed=100_000, transcendentals=0),
        name=name,
    )(*args)


def swap_pairs(count, phase):
    if phase == 0:
        return [(i, i ^ 1) for i in range(count)]
    return [(i, (i - 1) % count if i % 2 == 0 else (i + 1) % count) for i in range(count)]


def exchange(sends):
    nx, ny = lax.axis_size("gx"), lax.axis_size("gy")
    return (
        lax.ppermute(sends[0], "gx", swap_pairs(nx, 1)),
        lax.ppermute(sends[1], "gx", swap_pairs(nx, 0)),
        lax.ppermute(sends[2], "gy", swap_pairs(ny, 1)),
        lax.ppermute(sends[3], "gy", swap_pairs(ny, 0)),
    )


def everywhere(x):
    count = lax.axis_size("gx") * lax.axis_size("gy")
    y = jnp.broadcast_to(x[None], (count,) + x.shape)
    return lax.all_to_all(y, ("gx", "gy"), split_axis=0, concat_axis=0, tiled=True)


def per_device(start, shifts, diag_blocks, off_blocks, jacobi_inv, prolong, coarse_inv, cols, send_rows, owner, agg_slot):
    halo = [shape(HALO, 128)] * 4
    matrices = [pltpu.with_memory_space_constraint(x, pltpu.HBM) for x in (off_blocks, diag_blocks, jnp.transpose(cols))]
    sources = [
        start,
        jacobi_inv.reshape(ROWS * BS, BS),
        jnp.transpose(prolong, (0, 2, 1)),
        jnp.transpose(coarse_inv, (1, 2, 0)).reshape(BS, 24),
        send_rows[0],
        owner.reshape(1, ROWS),
        agg_slot.reshape(1, ROWS),
        shifts.reshape(1, 4),
    ]
    v, wj, ptd, pick, z, ze, id_col, extra, slopes, *sends, near = call(
        first_kernel,
        [
            shape(ROWS, 128),
            kept(128, ROWS * BS, dtype=BF16),
            shape(CW, ROWS, 128),
            shape(4 * HALO, ROWS, dtype=BF16),
            shape(ROWS, 128),
            shape(ROWS, 128),
            shape(ROWS, 128),
            shape(16, 128),
            shape(4, 128),
        ]
        + [shape(6, HALO, 128)] * 4
        + [kept(EARLY, KOFF, BS, BS)],
        *[pltpu.with_memory_space_constraint(x, pltpu.HBM) for x in sources],
        matrices[0],
        specs=[HBM] * (len(sources) + 1),
        scratch=[pltpu.VMEM(x.shape, x.dtype) for x in sources]
        + [pltpu.SemaphoreType.DMA((len(sources),)), pltpu.SemaphoreType.DMA],
        name="first",
    )
    got = exchange(sends)
    half = kept(WIDTH, ROWS * BS // 2, dtype=BF16)
    *w_op, gather = call(
        operator_kernel,
        [half, half, shape(3 * ROWS, 256, dtype=BF16)],
        *matrices,
        near,
        specs=[HBM] * 3 + [VM],
        scratch=[
            pltpu.VMEM((ROWS - EARLY, KOFF, BS, BS), F32),
            pltpu.VMEM((ROWS, BS, BS), F32),
            pltpu.VMEM((KOFF, ROWS), jnp.int32),
            pltpu.SemaphoreType.DMA((2 + (ROWS - EARLY) // 8,)),
        ],
        flops=2_000_000_000,
        name="operator",
    )
    around = [g[0] for g in got]
    basis = [v]
    mask = pte = None
    for k in range(4):
        (base,) = call(before_restrict, [shape(ROWS, 128)], v, ze, *w_op, flops=500_000_000, name="before_restrict")
        w, p = call(
            restrict_kernel,
            [shape(ROWS, 128), shape(4 if k else 16, 128)],
            base,
            ze,
            *around,
            *w_op,
            gather,
            ptd,
            *([] if k else [extra]),
            name="restrict",
        )
        x = everywhere(p)
        if k == 0:
            mask, pte, x = call(
                coarse_kernel,
                [kept(64 * 128, 128, dtype=BF16), shape(CW, EXT, 128), shape(64, 8, 128)],
                x,
                id_col,
                ptd,
                *got,
                name="coarse",
            )
        x = x.reshape(64, 8, 128)
        ye, *sends = call(
            correct_kernel,
            [shape(ROWS, 128)] + halo,
            x,
            mask,
            pte,
            z,
            w,
            *w_op,
            gather,
            wj,
            pick,
            scratch=[pltpu.VMEM((16, 64 * 128), BF16)],
            name="correct",
        )
        around = exchange(sends)
        (base,) = call(
            functools.partial(before_advance, k),
            [shape(ROWS, 128)],
            slopes,
            v,
            ye,
            *w_op,
            flops=500_000_000,
            name="before_advance",
        )
        if k < 3:
            v, z, ze, *sends = call(
                advance_kernel,
                [shape(ROWS, 128)] * 3 + halo,
                base,
                ye,
                *around,
                *w_op,
                gather,
                wj,
                pick,
                name="advance",
            )
            basis.append(v)
            around = exchange(sends)
    (known,) = call(known_kernel, [shape(16, 128)], *basis, flops=500_000_000, name="known")
    v, gram = call(
        last_kernel,
        [shape(ROWS, 128), shape(1, 128)],
        base,
        ye,
        *around,
        *w_op,
        gather,
        *basis,
        known,
        name="last",
    )
    basis.append(v)
    grams = everywhere(gram).reshape(128, 128)
    total = float(ROWS * BS * 128)
    return tuple(
        call(
            functools.partial(orthogonal_kernel, total),
            [shape(5, ROWS, BS), shape(5, 5)],
            grams,
            *basis,
            name="orthogonal",
        )
    )


def solution(mesh):
    rows = ("gx", "gy")
    in_specs = (
        P(rows, None),
        P(),
        P(rows, None, None),
        P(rows, None, None, None),
        P(rows, None, None),
        P(rows, None, None),
        P(rows, None, None),
        P(rows, None),
        P(rows, None, None),
        P(rows, None),
        P(rows),
    )
    return jax.shard_map(
        per_device, mesh=mesh, in_specs=in_specs, out_specs=(P(None, rows, None), P()), check_vma=False
    )
```

```python
import functools

import jax
import jax.numpy as jnp
from jax import lax
from jax.experimental import pallas as pl
from jax.experimental.pallas import tpu as pltpu
from jax.sharding import PartitionSpec as P

F32 = jnp.float32
BF16 = jnp.bfloat16
ROWS = 48
BS = 64
CW = 8
HALO = 16
EXT = ROWS + 4 * HALO
KOFF = 6
EARLY = 16
OWN = 6 * 128
WIDTH = 7 * 128
jacobi_weight = 2.0 / 3.0
PAIRS = [(j, l) for l in range(5) for j in range(l + 1)]

VM = pl.BlockSpec(memory_space=pltpu.VMEM)
HBM = pl.BlockSpec(memory_space=pltpu.HBM)
LAST = (((1,), (1,)), ((), ()))


def low_lanes(x):
    return lax.broadcasted_iota(jnp.int32, x.shape, 1) < BS


def swap(x):
    return pltpu.roll(x, BS, 1)


def twice(x):
    return jnp.concatenate([x, x], axis=1)


def pack(x):
    high = x.astype(BF16).astype(F32)
    return jnp.where(low_lanes(x), high, (x - high).astype(BF16).astype(F32))


def lhs_parts(packed):
    low = low_lanes(packed)
    turned = swap(packed)
    return jnp.where(low, packed, turned), jnp.where(low, turned, 0.0)


def row_blocks(top, bottom, w_ref, first=0):
    out = []
    for g in range(ROWS // 8):
        lhs = jnp.concatenate([top[8 * g : 8 * g + 8], bottom[8 * g : 8 * g + 8]], axis=0).astype(BF16)
        ref, n = (w_ref[g // 3], g % 3) if isinstance(w_ref, tuple) else (w_ref, g)
        r = jnp.dot(
            lhs, ref[first : first + top.shape[1], 512 * n : 512 * n + 512], preferred_element_type=F32
        )
        s = r[:8] + r[8:]
        own = lax.broadcasted_iota(jnp.int32, s.shape, 0) == lax.broadcasted_iota(jnp.int32, s.shape, 1) // BS
        s = jnp.where(own, s, 0.0)
        t = (s[:, 0:128] + s[:, 128:256]) + (s[:, 256:384] + s[:, 384:512])
        out.append(t + swap(t))
    return jnp.concatenate(out, axis=0)


def smooth(x, wj_ref):
    top, bottom = lhs_parts(pack(x))
    return row_blocks(top, bottom, wj_ref)


def operate_own(packed, w_ref):
    top, bottom = lhs_parts(packed)
    return row_blocks(top, bottom, w_ref, OWN)


def operate(packed, w_ref, gather_ref, own=True):
    e = jnp.concatenate([packed, jnp.zeros((128 - EXT, 128), F32)], axis=0)
    s = swap(e)
    low = low_lanes(e)
    zero = jnp.zeros_like(e)
    rhs = jnp.concatenate(
        [
            jnp.concatenate([jnp.where(low, e, zero), jnp.where(low, s, zero)], axis=1),
            jnp.concatenate([jnp.where(low, zero, s), jnp.where(low, zero, e)], axis=1),
        ],
        axis=0,
    ).astype(BF16)
    x = jnp.dot(gather_ref[...], rhs, preferred_element_type=F32)
    high = [x[ROWS * p : ROWS * p + ROWS, 0:128] for p in range(3)]
    rest = [x[ROWS * p : ROWS * p + ROWS, 128:256] for p in range(3)]
    none = [jnp.zeros((ROWS, 128), F32)] * 3
    top, bottom = high + high, rest + none
    if own:
        for x, part in zip((top, bottom), lhs_parts(packed[:ROWS])):
            x.append(part)
    return row_blocks(jnp.concatenate(top, axis=1), jnp.concatenate(bottom, axis=1), w_ref)


def send_lists(packed, pick_ref, outs):
    picked = jnp.dot(pick_ref[...], packed.astype(BF16), preferred_element_type=F32)
    for s, out in enumerate(outs):
        out[...] = picked[HALO * s : HALO * s + HALO]


def pair_rows(x):
    t = twice(x).T
    high = t.astype(BF16).astype(F32)
    return jnp.where(lax.broadcasted_iota(jnp.int32, t.shape, 0) < BS, high, t - high).astype(BF16)


def column(line):
    line = jnp.concatenate([line, jnp.zeros((1, 128 - line.shape[1]), F32)], axis=1)
    return jnp.broadcast_to(line, (128, 128)).T


def first_kernel(*refs):
    sources, off, rest = refs[:8], refs[8], refs[9:]
    v, wj, ptd, pick, z, ze, ids, extra, slopes, s0, s1, s2, s3, near = rest[:14]
    here, sems, far = rest[14:22], rest[22], rest[23]
    copies = [pltpu.make_async_copy(x, y, sems.at[n]) for n, (x, y) in enumerate(zip(sources, here))]
    for c in copies:
        c.start()
    ahead = pltpu.make_async_copy(off.at[pl.ds(0, EARLY)], near, far)
    ahead.start()
    for c in copies:
        c.wait()
    start, jac, pt, inverse, listed, owner, slot, shifts = here
    v[...] = twice(start[...])
    for n in range(ROWS // 2):
        wj[:, 128 * n : 128 * n + 128] = pair_rows(jac[128 * n : 128 * n + 128, :] * jacobi_weight)
    z[...] = smooth(v[...], wj)
    ze[...] = pack(z[...])
    even_x = lax.axis_index("gx") % 2 == 0
    even_y = lax.axis_index("gy") % 2 == 0
    lists = listed[...].astype(F32)
    order = [
        jnp.where(even_x, lists[1:2], lists[0:1]),
        jnp.where(even_x, lists[0:1], lists[1:2]),
        jnp.where(even_y, lists[3:4], lists[2:3]),
        jnp.where(even_y, lists[2:3], lists[3:4]),
    ]
    chosen = jnp.concatenate([column(x)[0:HALO, 0:ROWS] for x in order], axis=0)
    chosen = (chosen == lax.broadcasted_iota(jnp.int32, (4 * HALO, ROWS), 1).astype(F32)).astype(F32)
    pick[...] = chosen.astype(BF16)
    number = (owner[...] * 24 + slot[...]).astype(F32)
    ids[...] = column(number)[0:ROWS]
    for c in range(CW):
        ptd[c] = twice(pt[:, c, :])
    low = lax.broadcasted_iota(jnp.int32, (ROWS, 128), 1) < BS
    parts = [jnp.where(low, ptd[r], ptd[r + 4]) for r in range(4)] + [ids[...]]
    parts = [jnp.dot(chosen, x, precision=lax.Precision.HIGHEST, preferred_element_type=F32) for x in parts]
    parts = [jnp.dot(pick[...], ze[...].astype(BF16), preferred_element_type=F32)] + parts
    for s, out in enumerate((s0, s1, s2, s3)):
        for k, x in enumerate(parts):
            out[k] = x[HALO * s : HALO * s + HALO]
    wide = jnp.concatenate([inverse[...], jnp.zeros((BS, 104), F32)], axis=1)
    wide = jnp.concatenate([wide, jnp.zeros((BS, 128), F32)], axis=0).T[0:24]
    extra[4:16, :] = wide[0:12] + swap(wide[12:24])
    number = jnp.concatenate([number, jnp.zeros((1, 128 - ROWS), F32)], axis=1)
    lane = lax.broadcasted_iota(jnp.int32, (1, 128), 1)
    spare = (lane >= ROWS) & (lane < BS)
    for r in range(3):
        extra[r : r + 1, :] = jnp.where(spare, pltpu.roll(jnp.broadcast_to(number, (8, 128)), ROWS - 16 * r, 1)[0:1], 0.0)
    extra[3:4, :] = jnp.zeros((1, 128), F32)
    for k in range(4):
        slopes[k : k + 1, :] = jnp.broadcast_to(shifts[:, k : k + 1], (1, 128))
    ahead.wait()


def pack_rows(buf, n, dbuf, row, w):
    at = BS * (row % (ROWS // 2))
    at = slice(at, at + 128)
    for p in range(3):
        x = jnp.concatenate(
            [
                jnp.concatenate([buf[n, 2 * p], buf[n, 2 * p + 1]], axis=1),
                jnp.concatenate([buf[n + 1, 2 * p], buf[n + 1, 2 * p + 1]], axis=1),
            ],
            axis=0,
        ).T
        high = x.astype(BF16)
        w[128 * p : 128 * p + 128, at] = high
        w[384 + 128 * p : 512 + 128 * p, at] = (x - high.astype(F32)).astype(BF16)
    w[768:896, at] = pair_rows(jnp.concatenate([dbuf[row], dbuf[row + 1]], axis=0))


def operator_kernel(off, diag, cols, near, wa, wb, gather, buf, dbuf, cbuf, sems):
    steps = (ROWS - EARLY) // 8
    named = pltpu.make_async_copy(cols, cbuf, sems.at[0])
    named.start()
    middle = pltpu.make_async_copy(diag, dbuf, sems.at[1])
    middle.start()
    later = [
        pltpu.make_async_copy(off.at[pl.ds(EARLY + 8 * g, 8)], buf.at[pl.ds(8 * g, 8)], sems.at[2 + g])
        for g in range(steps)
    ]
    for c in later:
        c.start()
    named.wait()
    turn_x = (lax.axis_index("gx") % 2) * HALO
    turn_y = (lax.axis_index("gy") % 2) * HALO
    number = cbuf[...]
    beyond = number - ROWS
    turned = ROWS + (beyond ^ jnp.where(beyond < 2 * HALO, turn_x, turn_y))
    number = jnp.where(beyond >= 0, turned, number).astype(F32)
    number = jnp.concatenate([number, jnp.zeros((KOFF, 128 - ROWS), F32)], axis=1)
    number = jnp.concatenate([number, jnp.zeros((128 - KOFF, 128), F32)], axis=0).T[0:ROWS]
    lane = lax.broadcasted_iota(jnp.int32, (ROWS, 256), 1).astype(F32)
    for p in range(3):
        hit = (lane == number[:, 2 * p : 2 * p + 1]) | (lane == number[:, 2 * p + 1 : 2 * p + 2] + 128.0)
        gather[ROWS * p : ROWS * p + ROWS, :] = hit.astype(F32).astype(BF16)
    middle.wait()
    for n in range(0, EARLY, 2):
        pack_rows(near, n, dbuf, n, wa)
    for g in range(steps):
        later[g].wait()
        for n in range(8 * g, 8 * g + 8, 2):
            pack_rows(buf, n, dbuf, EARLY + n, wa if EARLY + n < ROWS // 2 else wb)


def before_restrict(v, ze, wa, wb, base):
    base[...] = v[...] - operate_own(ze[...], (wa, wb))


def before_advance(k, slopes, v, ye, wa, wb, base):
    base[...] = operate_own(ye[...], (wa, wb)) - slopes[k : k + 1, :] * v[...]


def restrict_kernel(base, ze, h0, h1, h2, h3, wa, wb, gather, ptd, *rest):
    *extra, w, p = rest
    ext = jnp.concatenate([ze[...], h0[...], h1[...], h2[...], h3[...]], axis=0)
    r = base[...] - operate(ext, (wa, wb), gather, own=False)
    w[...] = r
    ones = jnp.ones((16, 128), BF16)
    pad = jnp.zeros((16, 128), F32)
    for k in range(4):
        x = jnp.concatenate([pack(ptd[k] * r), pad, pack(ptd[k + 4] * r), pad], axis=0).astype(BF16)
        line = lax.dot_general(ones, x, LAST, preferred_element_type=F32)[0:1]
        p[k : k + 1, :] = line + extra[0][k : k + 1, :] if extra else line
    if extra:
        p[4:16, :] = extra[0][4:16, :]


def coarse_kernel(x0, ids, ptd, g0, g1, g2, g3, mask, pte, xp):
    idc = jnp.concatenate(
        [ids[...], g0[5], g1[5], g2[5], g3[5], jnp.full((128 - EXT, 128), -1.0, F32)], axis=0
    )
    wanted = idc.T[0:1]
    given = [x0[:, r, :].T[ROWS:BS] for r in range(3)] + [jnp.full((BS - ROWS, 128), -1.0, F32)]
    given = jnp.concatenate(given + given, axis=0)
    for q in range(64):
        line = jnp.concatenate([given[0:BS, 2 * q : 2 * q + 1], given[BS:128, 2 * q + 1 : 2 * q + 2]], axis=0)
        mask[128 * q : 128 * q + 128, :] = (line == wanted).astype(F32).astype(BF16)
        xp[q] = jnp.concatenate([x0[2 * q, 0:4, :], x0[2 * q + 1, 0:4, :]], axis=0)
    device = jnp.floor((idc + 0.5) * (1.0 / 24.0))
    slot = idc - 24.0 * device
    upper = slot >= 11.5
    place = device * 16.0 + 4.0 + jnp.where(upper, slot - 12.0, slot)
    high, rest = [], []
    for b in range(8):
        src = x0[16 * b : 16 * b + 16].reshape(256, 128)
        high.append(src.astype(BF16))
        rest.append((src - high[-1].astype(F32)).astype(BF16))
    lane = lax.broadcasted_iota(jnp.int32, (128, 128), 1).astype(F32)
    hit = jnp.concatenate([(place - 128.0 * b == lane).astype(F32).astype(BF16) for b in range(16)], axis=1)
    source = jnp.concatenate([jnp.concatenate(high, axis=0), jnp.concatenate(rest, axis=0)], axis=1)
    total = jnp.dot(hit, source, preferred_element_type=F32)
    total = total[:, 0:128] + total[:, 128:256]
    inverse = jnp.where(upper, swap(total), total)[:EXT]
    wide = []
    for c in range(CW):
        around = [g[1 + c % 4] for g in (g0, g1, g2, g3)]
        around = jnp.concatenate(around, axis=0)
        lowh = low_lanes(around)
        turned = swap(around)
        around = jnp.where(lowh, around, turned) if c < 4 else jnp.where(lowh, turned, around)
        wide.append(jnp.concatenate([ptd[c], around], axis=0))
    for d in range(CW):
        acc = wide[0] * inverse[:, d : d + 1]
        for c in range(1, CW):
            acc = acc + wide[c] * inverse[:, c * CW + d : c * CW + d + 1]
        pte[d] = acc


def correct_kernel(x, mask, pte, z, w, wa, wb, gather, wj, pick, ye, s0, s1, s2, s3, parts):
    sub = lax.broadcasted_iota(jnp.int32, (8, 128), 0) < 4
    lane = lax.broadcasted_iota(jnp.int32, (8, 128), 1) < BS
    keep = sub == lane
    for q in range(64):
        t = x[q]
        t = jnp.where(keep, t, pltpu.roll(swap(t), 4, 0))
        high = t.astype(BF16).astype(F32)
        parts[:, 128 * q : 128 * q + 128] = jnp.concatenate([high, t - high], axis=0).astype(BF16)
    got = jnp.dot(parts[...], mask[...], preferred_element_type=F32)
    coarse = jnp.concatenate([got[0:8] + got[8:16], jnp.zeros((120, 128), F32)], axis=0).T[:EXT]
    u = pte[0] * coarse[:, 0:1]
    for d in range(1, CW):
        u = u + pte[d] * coarse[:, d : d + 1]
    r = w[...] - operate(pack(u), (wa, wb), gather)
    y = z[...] + u[:ROWS] + smooth(r, wj)
    ye[...] = pack(y)
    send_lists(ye[...], pick, (s0, s1, s2, s3))


def advance(base, ye, h0, h1, h2, h3, w_op, gather):
    ext = jnp.concatenate([ye[...], h0[...], h1[...], h2[...], h3[...]], axis=0)
    return operate(ext, w_op, gather, own=False) + base[...]


def advance_kernel(base, ye, h0, h1, h2, h3, wa, wb, gather, wj, pick, vn, z, ze, s0, s1, s2, s3):
    vn[...] = advance(base, ye, h0, h1, h2, h3, (wa, wb), gather)
    z[...] = smooth(vn[...], wj)
    ze[...] = pack(z[...])
    send_lists(ze[...], pick, (s0, s1, s2, s3))


def products(basis, pairs):
    return [jnp.sum(basis[j] * basis[l], axis=0, keepdims=True) for j, l in pairs]


def before_last(slopes, v, ye, wa, wb, v0, v1, v2, base, known):
    before_advance(3, slopes, v, ye, wa, wb, base)
    basis = [x[...] for x in (v0, v1, v2, v)]
    known[...] = jnp.concatenate(products(basis, PAIRS[:10]) + [jnp.zeros((6, 128), F32)], axis=0)


def last_kernel(base, ye, h0, h1, h2, h3, wa, wb, gather, v0, v1, v2, v3, known, v4, gram):
    v4[...] = advance(base, ye, h0, h1, h2, h3, (wa, wb), gather)
    basis = [v[...] for v in (v0, v1, v2, v3, v4)]
    rows = [known[0:10, :]] + products(basis, PAIRS[10:]) + [jnp.zeros((113, 128), F32)]
    sums = lax.dot_general(
        jnp.ones((8, 128), F32),
        jnp.concatenate(rows, axis=0),
        LAST,
        precision=lax.Precision.HIGHEST,
        preferred_element_type=F32,
    )
    gram[...] = sums[0:1]


def orthogonal_kernel(total, grams, v0, v1, v2, v3, v4, q_out, r_out):
    sums = jnp.sum(grams[...], axis=0, keepdims=True) * (1.0 / (2.0 * total))
    g = {pair: sums[:, n : n + 1] for n, pair in enumerate(PAIRS)}
    lower = {}
    for j in range(5):
        d = g[(j, j)]
        for k in range(j):
            d = d - lower[(j, k)] * lower[(j, k)]
        lower[(j, j)] = jnp.sqrt(d)
        for i in range(j + 1, 5):
            t = g[(j, i)]
            for k in range(j):
                t = t - lower[(i, k)] * lower[(j, k)]
            lower[(i, j)] = t / lower[(j, j)]
    at_row = lax.broadcasted_iota(jnp.int32, (8, 128), 0)
    at_col = lax.broadcasted_iota(jnp.int32, (8, 128), 1)
    r = jnp.zeros((8, 128), F32)
    for (i, j), value in lower.items():
        r = jnp.where((at_row == j) & (at_col == i), value, r)
    r_out[...] = r[0:5, 0:5]
    solved = []
    for i, v in enumerate((v0, v1, v2, v3, v4)):
        t = v[...]
        for k in range(i):
            t = t - lower[(i, k)] * solved[k]
        t = t / lower[(i, i)]
        solved.append(t)
        q_out[i] = t[:, 0:BS]


def shape(*dims, dtype=F32):
    return jax.ShapeDtypeStruct(dims, dtype)


def kept(*dims, dtype=F32):
    return pltpu.VMEM(dims, dtype)


def call(kernel, outs, *args, specs=None, scratch=(), flops=2_000_000, name=None):
    return pl.pallas_call(
        kernel,
        out_shape=outs,
        in_specs=specs or [VM] * len(args),
        out_specs=jax.tree.map(lambda _: VM, outs),
        scratch_shapes=list(scratch),
        compiler_params=pltpu.CompilerParams(vmem_limit_bytes=24 << 20),
        cost_estimate=pl.CostEstimate(flops=flops, bytes_accessed=100_000, transcendentals=0),
        name=name,
    )(*args)


def swap_pairs(count, phase):
    if phase == 0:
        return [(i, i ^ 1) for i in range(count)]
    return [(i, (i - 1) % count if i % 2 == 0 else (i + 1) % count) for i in range(count)]


def exchange(sends):
    nx, ny = lax.axis_size("gx"), lax.axis_size("gy")
    return (
        lax.ppermute(sends[0], "gx", swap_pairs(nx, 1)),
        lax.ppermute(sends[1], "gx", swap_pairs(nx, 0)),
        lax.ppermute(sends[2], "gy", swap_pairs(ny, 1)),
        lax.ppermute(sends[3], "gy", swap_pairs(ny, 0)),
    )


def everywhere(x):
    count = lax.axis_size("gx") * lax.axis_size("gy")
    y = jnp.broadcast_to(x[None], (count,) + x.shape)
    return lax.all_to_all(y, ("gx", "gy"), split_axis=0, concat_axis=0, tiled=True)


def per_device(start, shifts, diag_blocks, off_blocks, jacobi_inv, prolong, coarse_inv, cols, send_rows, owner, agg_slot):
    halo = [shape(HALO, 128)] * 4
    matrices = [pltpu.with_memory_space_constraint(x, pltpu.HBM) for x in (off_blocks, diag_blocks, jnp.transpose(cols))]
    sources = [
        start,
        jacobi_inv.reshape(ROWS * BS, BS),
        jnp.transpose(prolong, (0, 2, 1)),
        jnp.transpose(coarse_inv, (1, 2, 0)).reshape(BS, 24),
        send_rows[0],
        owner.reshape(1, ROWS),
        agg_slot.reshape(1, ROWS),
        shifts.reshape(1, 4),
    ]
    v, wj, ptd, pick, z, ze, id_col, extra, slopes, *sends, near = call(
        first_kernel,
        [
            shape(ROWS, 128),
            kept(128, ROWS * BS, dtype=BF16),
            shape(CW, ROWS, 128),
            shape(4 * HALO, ROWS, dtype=BF16),
            shape(ROWS, 128),
            shape(ROWS, 128),
            shape(ROWS, 128),
            shape(16, 128),
            shape(4, 128),
        ]
        + [shape(6, HALO, 128)] * 4
        + [kept(EARLY, KOFF, BS, BS)],
        *[pltpu.with_memory_space_constraint(x, pltpu.HBM) for x in sources],
        matrices[0],
        specs=[HBM] * (len(sources) + 1),
        scratch=[pltpu.VMEM(x.shape, x.dtype) for x in sources]
        + [pltpu.SemaphoreType.DMA((len(sources),)), pltpu.SemaphoreType.DMA],
        name="first",
    )
    got = exchange(sends)
    half = kept(WIDTH, ROWS * BS // 2, dtype=BF16)
    *w_op, gather = call(
        operator_kernel,
        [half, half, shape(3 * ROWS, 256, dtype=BF16)],
        *matrices,
        near,
        specs=[HBM] * 3 + [VM],
        scratch=[
            pltpu.VMEM((ROWS - EARLY, KOFF, BS, BS), F32),
            pltpu.VMEM((ROWS, BS, BS), F32),
            pltpu.VMEM((KOFF, ROWS), jnp.int32),
            pltpu.SemaphoreType.DMA((2 + (ROWS - EARLY) // 8,)),
        ],
        flops=2_000_000_000,
        name="operator",
    )
    around = [g[0] for g in got]
    basis = [v]
    mask = pte = None
    for k in range(4):
        (base,) = call(before_restrict, [shape(ROWS, 128)], v, ze, *w_op, flops=500_000_000, name="before_restrict")
        w, p = call(
            restrict_kernel,
            [shape(ROWS, 128), shape(4 if k else 16, 128)],
            base,
            ze,
            *around,
            *w_op,
            gather,
            ptd,
            *([] if k else [extra]),
            name="restrict",
        )
        x = everywhere(p)
        if k == 0:
            mask, pte, x = call(
                coarse_kernel,
                [kept(64 * 128, 128, dtype=BF16), shape(CW, EXT, 128), shape(64, 8, 128)],
                x,
                id_col,
                ptd,
                *got,
                name="coarse",
            )
        x = x.reshape(64, 8, 128)
        ye, *sends = call(
            correct_kernel,
            [shape(ROWS, 128)] + halo,
            x,
            mask,
            pte,
            z,
            w,
            *w_op,
            gather,
            wj,
            pick,
            scratch=[pltpu.VMEM((16, 64 * 128), BF16)],
            name="correct",
        )
        around = exchange(sends)
        base, *known = call(
            functools.partial(before_advance, k) if k < 3 else before_last,
            [shape(ROWS, 128)] if k < 3 else [shape(ROWS, 128), shape(16, 128)],
            slopes,
            v,
            ye,
            *w_op,
            *([] if k < 3 else basis[:3]),
            flops=500_000_000,
            name="before_advance",
        )
        if k < 3:
            v, z, ze, *sends = call(
                advance_kernel,
                [shape(ROWS, 128)] * 3 + halo,
                base,
                ye,
                *around,
                *w_op,
                gather,
                wj,
                pick,
                name="advance",
            )
            basis.append(v)
            around = exchange(sends)
    v, gram = call(
        last_kernel,
        [shape(ROWS, 128), shape(1, 128)],
        base,
        ye,
        *around,
        *w_op,
        gather,
        *basis,
        *known,
        name="last",
    )
    basis.append(v)
    grams = everywhere(gram).reshape(128, 128)
    total = float(ROWS * BS * 128)
    return tuple(
        call(
            functools.partial(orthogonal_kernel, total),
            [shape(5, ROWS, BS), shape(5, 5)],
            grams,
            *basis,
            name="orthogonal",
        )
    )


def solution(mesh):
    rows = ("gx", "gy")
    in_specs = (
        P(rows, None),
        P(),
        P(rows, None, None),
        P(rows, None, None, None),
        P(rows, None, None),
        P(rows, None, None),
        P(rows, None, None),
        P(rows, None),
        P(rows, None, None),
        P(rows, None),
        P(rows),
    )
    return jax.shard_map(
        per_device, mesh=mesh, in_specs=in_specs, out_specs=(P(None, rows, None), P()), check_vma=False
    )
```

```python
import functools

import jax
import jax.numpy as jnp
from jax import lax
from jax.experimental import pallas as pl
from jax.experimental.pallas import tpu as pltpu
from jax.sharding import PartitionSpec as P

F32 = jnp.float32
BF16 = jnp.bfloat16
ROWS = 48
BS = 64
CW = 8
HALO = 16
EXT = ROWS + 4 * HALO
KOFF = 6
EARLY = 16
OWN = 6 * 128
WIDTH = 7 * 128
jacobi_weight = 2.0 / 3.0
PAIRS = [(j, l) for l in range(5) for j in range(l + 1)]

VM = pl.BlockSpec(memory_space=pltpu.VMEM)
HBM = pl.BlockSpec(memory_space=pltpu.HBM)
LAST = (((1,), (1,)), ((), ()))


def low_lanes(x):
    return lax.broadcasted_iota(jnp.int32, x.shape, 1) < BS


def swap(x):
    return pltpu.roll(x, BS, 1)


def twice(x):
    return jnp.concatenate([x, x], axis=1)


def pack(x):
    high = x.astype(BF16).astype(F32)
    return jnp.where(low_lanes(x), high, (x - high).astype(BF16).astype(F32))


def lhs_parts(packed):
    low = low_lanes(packed)
    turned = swap(packed)
    return jnp.where(low, packed, turned), jnp.where(low, turned, 0.0)


def row_blocks(top, bottom, w_ref, first=0):
    out = []
    for g in range(ROWS // 8):
        lhs = jnp.concatenate([top[8 * g : 8 * g + 8], bottom[8 * g : 8 * g + 8]], axis=0).astype(BF16)
        ref, n = (w_ref[g // 3], g % 3) if isinstance(w_ref, tuple) else (w_ref, g)
        r = jnp.dot(
            lhs, ref[first : first + top.shape[1], 512 * n : 512 * n + 512], preferred_element_type=F32
        )
        s = r[:8] + r[8:]
        own = lax.broadcasted_iota(jnp.int32, s.shape, 0) == lax.broadcasted_iota(jnp.int32, s.shape, 1) // BS
        s = jnp.where(own, s, 0.0)
        t = (s[:, 0:128] + s[:, 128:256]) + (s[:, 256:384] + s[:, 384:512])
        out.append(t + swap(t))
    return jnp.concatenate(out, axis=0)


def smooth(x, wj_ref):
    top, bottom = lhs_parts(pack(x))
    return row_blocks(top, bottom, wj_ref)


def operate_own(packed, w_ref):
    top, bottom = lhs_parts(packed)
    return row_blocks(top, bottom, w_ref, OWN)


def operate(packed, w_ref, gather_ref, own=True):
    e = jnp.concatenate([packed, jnp.zeros((128 - EXT, 128), F32)], axis=0)
    s = swap(e)
    low = low_lanes(e)
    zero = jnp.zeros_like(e)
    rhs = jnp.concatenate(
        [
            jnp.concatenate([jnp.where(low, e, zero), jnp.where(low, s, zero)], axis=1),
            jnp.concatenate([jnp.where(low, zero, s), jnp.where(low, zero, e)], axis=1),
        ],
        axis=0,
    ).astype(BF16)
    x = jnp.dot(gather_ref[...], rhs, preferred_element_type=F32)
    high = [x[ROWS * p : ROWS * p + ROWS, 0:128] for p in range(3)]
    rest = [x[ROWS * p : ROWS * p + ROWS, 128:256] for p in range(3)]
    none = [jnp.zeros((ROWS, 128), F32)] * 3
    top, bottom = high + high, rest + none
    if own:
        for x, part in zip((top, bottom), lhs_parts(packed[:ROWS])):
            x.append(part)
    return row_blocks(jnp.concatenate(top, axis=1), jnp.concatenate(bottom, axis=1), w_ref)


def send_lists(packed, pick_ref, outs):
    picked = jnp.dot(pick_ref[...], packed.astype(BF16), preferred_element_type=F32)
    for s, out in enumerate(outs):
        out[...] = picked[HALO * s : HALO * s + HALO]


def pair_rows(x):
    t = twice(x).T
    high = t.astype(BF16).astype(F32)
    return jnp.where(lax.broadcasted_iota(jnp.int32, t.shape, 0) < BS, high, t - high).astype(BF16)


def column(line):
    line = jnp.concatenate([line, jnp.zeros((1, 128 - line.shape[1]), F32)], axis=1)
    return jnp.broadcast_to(line, (128, 128)).T


def first_kernel(*refs):
    sources, off, rest = refs[:8], refs[8], refs[9:]
    v, wj, ptd, pick, z, ze, ids, extra, slopes, s0, s1, s2, s3, near = rest[:14]
    here, sems, far = rest[14:22], rest[22], rest[23]
    copies = [pltpu.make_async_copy(x, y, sems.at[n]) for n, (x, y) in enumerate(zip(sources, here))]
    for c in copies:
        c.start()
    ahead = pltpu.make_async_copy(off.at[pl.ds(0, EARLY)], near, far)
    ahead.start()
    for c in copies:
        c.wait()
    start, jac, pt, inverse, listed, owner, slot, shifts = here
    v[...] = twice(start[...])
    for n in range(ROWS // 2):
        wj[:, 128 * n : 128 * n + 128] = pair_rows(jac[128 * n : 128 * n + 128, :] * jacobi_weight)
    z[...] = smooth(v[...], wj)
    ze[...] = pack(z[...])
    even_x = lax.axis_index("gx") % 2 == 0
    even_y = lax.axis_index("gy") % 2 == 0
    lists = listed[...].astype(F32)
    order = [
        jnp.where(even_x, lists[1:2], lists[0:1]),
        jnp.where(even_x, lists[0:1], lists[1:2]),
        jnp.where(even_y, lists[3:4], lists[2:3]),
        jnp.where(even_y, lists[2:3], lists[3:4]),
    ]
    chosen = jnp.concatenate([column(x)[0:HALO, 0:ROWS] for x in order], axis=0)
    chosen = (chosen == lax.broadcasted_iota(jnp.int32, (4 * HALO, ROWS), 1).astype(F32)).astype(F32)
    pick[...] = chosen.astype(BF16)
    number = (owner[...] * 24 + slot[...]).astype(F32)
    ids[...] = column(number)[0:ROWS]
    for c in range(CW):
        ptd[c] = twice(pt[:, c, :])
    low = lax.broadcasted_iota(jnp.int32, (ROWS, 128), 1) < BS
    parts = [jnp.where(low, ptd[r], ptd[r + 4]) for r in range(4)] + [ids[...]]
    parts = [jnp.dot(chosen, x, precision=lax.Precision.HIGHEST, preferred_element_type=F32) for x in parts]
    parts = [jnp.dot(pick[...], ze[...].astype(BF16), preferred_element_type=F32)] + parts
    for s, out in enumerate((s0, s1, s2, s3)):
        for k, x in enumerate(parts):
            out[k] = x[HALO * s : HALO * s + HALO]
    wide = jnp.concatenate([inverse[...], jnp.zeros((BS, 104), F32)], axis=1)
    wide = jnp.concatenate([wide, jnp.zeros((BS, 128), F32)], axis=0).T[0:24]
    extra[4:16, :] = wide[0:12] + swap(wide[12:24])
    number = jnp.concatenate([number, jnp.zeros((1, 128 - ROWS), F32)], axis=1)
    lane = lax.broadcasted_iota(jnp.int32, (1, 128), 1)
    spare = (lane >= ROWS) & (lane < BS)
    for r in range(3):
        extra[r : r + 1, :] = jnp.where(spare, pltpu.roll(jnp.broadcast_to(number, (8, 128)), ROWS - 16 * r, 1)[0:1], 0.0)
    extra[3:4, :] = jnp.zeros((1, 128), F32)
    for k in range(4):
        slopes[k : k + 1, :] = jnp.broadcast_to(shifts[:, k : k + 1], (1, 128))
    ahead.wait()


def pack_rows(buf, n, dbuf, row, w):
    at = BS * (row % (ROWS // 2))
    at = slice(at, at + 128)
    for p in range(3):
        x = jnp.concatenate(
            [
                jnp.concatenate([buf[n, 2 * p], buf[n, 2 * p + 1]], axis=1),
                jnp.concatenate([buf[n + 1, 2 * p], buf[n + 1, 2 * p + 1]], axis=1),
            ],
            axis=0,
        ).T
        high = x.astype(BF16)
        w[128 * p : 128 * p + 128, at] = high
        w[384 + 128 * p : 512 + 128 * p, at] = (x - high.astype(F32)).astype(BF16)
    w[768:896, at] = pair_rows(jnp.concatenate([dbuf[row], dbuf[row + 1]], axis=0))


def operator_kernel(off, diag, cols, near, wa, wb, gather, buf, dbuf, cbuf, sems):
    steps = (ROWS - EARLY) // 8
    named = pltpu.make_async_copy(cols, cbuf, sems.at[0])
    named.start()
    middle = pltpu.make_async_copy(diag, dbuf, sems.at[1])
    middle.start()
    later = [
        pltpu.make_async_copy(off.at[pl.ds(EARLY + 8 * g, 8)], buf.at[pl.ds(8 * g, 8)], sems.at[2 + g])
        for g in range(steps)
    ]
    for c in later:
        c.start()
    named.wait()
    turn_x = (lax.axis_index("gx") % 2) * HALO
    turn_y = (lax.axis_index("gy") % 2) * HALO
    number = cbuf[...]
    beyond = number - ROWS
    turned = ROWS + (beyond ^ jnp.where(beyond < 2 * HALO, turn_x, turn_y))
    number = jnp.where(beyond >= 0, turned, number).astype(F32)
    number = jnp.concatenate([number, jnp.zeros((KOFF, 128 - ROWS), F32)], axis=1)
    number = jnp.concatenate([number, jnp.zeros((128 - KOFF, 128), F32)], axis=0).T[0:ROWS]
    lane = lax.broadcasted_iota(jnp.int32, (ROWS, 256), 1).astype(F32)
    for p in range(3):
        hit = (lane == number[:, 2 * p : 2 * p + 1]) | (lane == number[:, 2 * p + 1 : 2 * p + 2] + 128.0)
        gather[ROWS * p : ROWS * p + ROWS, :] = hit.astype(F32).astype(BF16)
    middle.wait()
    for n in range(0, EARLY, 2):
        pack_rows(near, n, dbuf, n, wa)
    for g in range(steps):
        later[g].wait()
        for n in range(8 * g, 8 * g + 8, 2):
            pack_rows(buf, n, dbuf, EARLY + n, wa if EARLY + n < ROWS // 2 else wb)


def before_restrict(v, ze, wa, wb, base):
    base[...] = v[...] - operate_own(ze[...], (wa, wb))


def before_advance(k, slopes, v, ye, wa, wb, base):
    base[...] = operate_own(ye[...], (wa, wb)) - slopes[k : k + 1, :] * v[...]


def restrict_kernel(base, ze, h0, h1, h2, h3, wa, wb, gather, ptd, *rest):
    *extra, w, p = rest
    ext = jnp.concatenate([ze[...], h0[...], h1[...], h2[...], h3[...]], axis=0)
    r = base[...] - operate(ext, (wa, wb), gather, own=False)
    w[...] = r
    ones = jnp.ones((16, 128), BF16)
    pad = jnp.zeros((16, 128), F32)
    for k in range(4):
        x = jnp.concatenate([pack(ptd[k] * r), pad, pack(ptd[k + 4] * r), pad], axis=0).astype(BF16)
        line = lax.dot_general(ones, x, LAST, preferred_element_type=F32)[0:1]
        p[k : k + 1, :] = line + extra[0][k : k + 1, :] if extra else line
    if extra:
        p[4:16, :] = extra[0][4:16, :]


def coarse_kernel(same, other, ids, ptd, g0, g1, g2, g3, mask, pte, xp):
    idc = jnp.concatenate(
        [ids[...], g0[5], g1[5], g2[5], g3[5], jnp.full((128 - EXT, 128), -1.0, F32)], axis=0
    )
    wanted = idc.T[0:1]
    even = lax.axis_index("gy") % 2 == 0

    def by_core(x, y):
        return jnp.where(even, x, y), jnp.where(even, y, x)

    given = [jnp.concatenate(by_core(same[:, r, :], other[:, r, :]), axis=0).T[ROWS:BS] for r in range(3)] + [jnp.full((BS - ROWS, 128), -1.0, F32)]
    given = jnp.concatenate(given + given, axis=0)
    for q in range(64):
        line = jnp.concatenate([given[0:BS, q : q + 1], given[BS:128, BS + q : BS + q + 1]], axis=0)
        mask[128 * q : 128 * q + 128, :] = (line == wanted).astype(F32).astype(BF16)
        xp[q] = jnp.concatenate(by_core(same[q, 0:4, :], other[q, 0:4, :]), axis=0)
    device = jnp.floor((idc + 0.5) * (1.0 / 24.0))
    slot = idc - 24.0 * device
    upper = slot >= 11.5
    chip = jnp.floor(device * 0.5)
    core = device - 2.0 * chip
    core = jnp.where(even, core, 1.0 - core)
    place = core * 1024.0 + chip * 16.0 + 4.0 + jnp.where(upper, slot - 12.0, slot)
    high, rest = [], []
    for b in range(8):
        src = (same if b < 4 else other)[16 * (b % 4) : 16 * (b % 4) + 16].reshape(256, 128)
        high.append(src.astype(BF16))
        rest.append((src - high[-1].astype(F32)).astype(BF16))
    lane = lax.broadcasted_iota(jnp.int32, (128, 128), 1).astype(F32)
    hit = jnp.concatenate([(place - 128.0 * b == lane).astype(F32).astype(BF16) for b in range(16)], axis=1)
    source = jnp.concatenate([jnp.concatenate(high, axis=0), jnp.concatenate(rest, axis=0)], axis=1)
    total = jnp.dot(hit, source, preferred_element_type=F32)
    total = total[:, 0:128] + total[:, 128:256]
    inverse = jnp.where(upper, swap(total), total)[:EXT]
    wide = []
    for c in range(CW):
        around = [g[1 + c % 4] for g in (g0, g1, g2, g3)]
        around = jnp.concatenate(around, axis=0)
        lowh = low_lanes(around)
        turned = swap(around)
        around = jnp.where(lowh, around, turned) if c < 4 else jnp.where(lowh, turned, around)
        wide.append(jnp.concatenate([ptd[c], around], axis=0))
    for d in range(CW):
        acc = wide[0] * inverse[:, d : d + 1]
        for c in range(1, CW):
            acc = acc + wide[c] * inverse[:, c * CW + d : c * CW + d + 1]
        pte[d] = acc


def correct_kernel(x, mask, pte, z, w, wa, wb, gather, wj, pick, ye, s0, s1, s2, s3, parts):
    sub = lax.broadcasted_iota(jnp.int32, (8, 128), 0) < 4
    lane = lax.broadcasted_iota(jnp.int32, (8, 128), 1) < BS
    keep = sub == lane
    for q in range(64):
        t = x[q]
        t = jnp.where(keep, t, pltpu.roll(swap(t), 4, 0))
        high = t.astype(BF16).astype(F32)
        parts[:, 128 * q : 128 * q + 128] = jnp.concatenate([high, t - high], axis=0).astype(BF16)
    got = jnp.dot(parts[...], mask[...], preferred_element_type=F32)
    coarse = jnp.concatenate([got[0:8] + got[8:16], jnp.zeros((120, 128), F32)], axis=0).T[:EXT]
    u = pte[0] * coarse[:, 0:1]
    for d in range(1, CW):
        u = u + pte[d] * coarse[:, d : d + 1]
    r = w[...] - operate(pack(u), (wa, wb), gather)
    y = z[...] + u[:ROWS] + smooth(r, wj)
    ye[...] = pack(y)
    send_lists(ye[...], pick, (s0, s1, s2, s3))


def advance(base, ye, h0, h1, h2, h3, w_op, gather):
    ext = jnp.concatenate([ye[...], h0[...], h1[...], h2[...], h3[...]], axis=0)
    return operate(ext, w_op, gather, own=False) + base[...]


def advance_kernel(base, ye, h0, h1, h2, h3, wa, wb, gather, wj, pick, vn, z, ze, s0, s1, s2, s3):
    vn[...] = advance(base, ye, h0, h1, h2, h3, (wa, wb), gather)
    z[...] = smooth(vn[...], wj)
    ze[...] = pack(z[...])
    send_lists(ze[...], pick, (s0, s1, s2, s3))


def products(basis, pairs):
    return [jnp.sum(basis[j] * basis[l], axis=0, keepdims=True) for j, l in pairs]


def before_last(slopes, v, ye, wa, wb, v0, v1, v2, base, known):
    before_advance(3, slopes, v, ye, wa, wb, base)
    basis = [x[...] for x in (v0, v1, v2, v)]
    known[...] = jnp.concatenate(products(basis, PAIRS[:10]) + [jnp.zeros((6, 128), F32)], axis=0)


def last_kernel(base, ye, h0, h1, h2, h3, wa, wb, gather, v0, v1, v2, v3, known, v4, gram):
    v4[...] = advance(base, ye, h0, h1, h2, h3, (wa, wb), gather)
    basis = [v[...] for v in (v0, v1, v2, v3, v4)]
    rows = [known[0:10, :]] + products(basis, PAIRS[10:]) + [jnp.zeros((113, 128), F32)]
    sums = lax.dot_general(
        jnp.ones((8, 128), F32),
        jnp.concatenate(rows, axis=0),
        LAST,
        precision=lax.Precision.HIGHEST,
        preferred_element_type=F32,
    )
    gram[...] = sums[0:1]


def orthogonal_kernel(total, grams, v0, v1, v2, v3, v4, q_out, r_out):
    sums = jnp.sum(grams[...], axis=0, keepdims=True) * (1.0 / (2.0 * total))
    g = {pair: sums[:, n : n + 1] for n, pair in enumerate(PAIRS)}
    lower = {}
    for j in range(5):
        d = g[(j, j)]
        for k in range(j):
            d = d - lower[(j, k)] * lower[(j, k)]
        lower[(j, j)] = jnp.sqrt(d)
        for i in range(j + 1, 5):
            t = g[(j, i)]
            for k in range(j):
                t = t - lower[(i, k)] * lower[(j, k)]
            lower[(i, j)] = t / lower[(j, j)]
    at_row = lax.broadcasted_iota(jnp.int32, (8, 128), 0)
    at_col = lax.broadcasted_iota(jnp.int32, (8, 128), 1)
    r = jnp.zeros((8, 128), F32)
    for (i, j), value in lower.items():
        r = jnp.where((at_row == j) & (at_col == i), value, r)
    r_out[...] = r[0:5, 0:5]
    solved = []
    for i, v in enumerate((v0, v1, v2, v3, v4)):
        t = v[...]
        for k in range(i):
            t = t - lower[(i, k)] * solved[k]
        t = t / lower[(i, i)]
        solved.append(t)
        q_out[i] = t[:, 0:BS]


def shape(*dims, dtype=F32):
    return jax.ShapeDtypeStruct(dims, dtype)


def kept(*dims, dtype=F32):
    return pltpu.VMEM(dims, dtype)


def call(kernel, outs, *args, specs=None, scratch=(), flops=2_000_000, name=None):
    return pl.pallas_call(
        kernel,
        out_shape=outs,
        in_specs=specs or [VM] * len(args),
        out_specs=jax.tree.map(lambda _: VM, outs),
        scratch_shapes=list(scratch),
        compiler_params=pltpu.CompilerParams(vmem_limit_bytes=24 << 20),
        cost_estimate=pl.CostEstimate(flops=flops, bytes_accessed=100_000, transcendentals=0),
        name=name,
    )(*args)


def swap_pairs(count, phase):
    if phase == 0:
        return [(i, i ^ 1) for i in range(count)]
    return [(i, (i - 1) % count if i % 2 == 0 else (i + 1) % count) for i in range(count)]


def exchange(sends):
    nx, ny = lax.axis_size("gx"), lax.axis_size("gy")
    return (
        lax.ppermute(sends[0], "gx", swap_pairs(nx, 1)),
        lax.ppermute(sends[1], "gx", swap_pairs(nx, 0)),
        lax.ppermute(sends[2], "gy", swap_pairs(ny, 1)),
        lax.ppermute(sends[3], "gy", swap_pairs(ny, 0)),
    )


def everywhere(x):
    count = lax.axis_size("gx") * lax.axis_size("gy")
    y = jnp.broadcast_to(x[None], (count,) + x.shape)
    return lax.all_to_all(y, ("gx", "gy"), split_axis=0, concat_axis=0, tiled=True)


def everywhere_by_core(x):
    nx, ny = lax.axis_size("gx"), lax.axis_size("gy")
    groups = [[p * ny + q for p in range(nx) for q in range(core, ny, 2)] for core in range(2)]
    y = jnp.broadcast_to(x[None], (nx * ny // 2,) + x.shape)
    same = lax.all_to_all(y, ("gx", "gy"), split_axis=0, concat_axis=0, tiled=True, axis_index_groups=groups)
    return same, lax.ppermute(same, "gy", swap_pairs(ny, 0))


def per_device(start, shifts, diag_blocks, off_blocks, jacobi_inv, prolong, coarse_inv, cols, send_rows, owner, agg_slot):
    halo = [shape(HALO, 128)] * 4
    matrices = [pltpu.with_memory_space_constraint(x, pltpu.HBM) for x in (off_blocks, diag_blocks, jnp.transpose(cols))]
    sources = [
        start,
        jacobi_inv.reshape(ROWS * BS, BS),
        jnp.transpose(prolong, (0, 2, 1)),
        jnp.transpose(coarse_inv, (1, 2, 0)).reshape(BS, 24),
        send_rows[0],
        owner.reshape(1, ROWS),
        agg_slot.reshape(1, ROWS),
        shifts.reshape(1, 4),
    ]
    v, wj, ptd, pick, z, ze, id_col, extra, slopes, *sends, near = call(
        first_kernel,
        [
            shape(ROWS, 128),
            kept(128, ROWS * BS, dtype=BF16),
            shape(CW, ROWS, 128),
            shape(4 * HALO, ROWS, dtype=BF16),
            shape(ROWS, 128),
            shape(ROWS, 128),
            shape(ROWS, 128),
            shape(16, 128),
            shape(4, 128),
        ]
        + [shape(6, HALO, 128)] * 4
        + [kept(EARLY, KOFF, BS, BS)],
        *[pltpu.with_memory_space_constraint(x, pltpu.HBM) for x in sources],
        matrices[0],
        specs=[HBM] * (len(sources) + 1),
        scratch=[pltpu.VMEM(x.shape, x.dtype) for x in sources]
        + [pltpu.SemaphoreType.DMA((len(sources),)), pltpu.SemaphoreType.DMA],
        name="first",
    )
    got = exchange(sends)
    half = kept(WIDTH, ROWS * BS // 2, dtype=BF16)
    *w_op, gather = call(
        operator_kernel,
        [half, half, shape(3 * ROWS, 256, dtype=BF16)],
        *matrices,
        near,
        specs=[HBM] * 3 + [VM],
        scratch=[
            pltpu.VMEM((ROWS - EARLY, KOFF, BS, BS), F32),
            pltpu.VMEM((ROWS, BS, BS), F32),
            pltpu.VMEM((KOFF, ROWS), jnp.int32),
            pltpu.SemaphoreType.DMA((2 + (ROWS - EARLY) // 8,)),
        ],
        flops=2_000_000_000,
        name="operator",
    )
    around = [g[0] for g in got]
    basis = [v]
    mask = pte = None
    for k in range(4):
        (base,) = call(before_restrict, [shape(ROWS, 128)], v, ze, *w_op, flops=500_000_000, name="before_restrict")
        w, p = call(
            restrict_kernel,
            [shape(ROWS, 128), shape(4 if k else 16, 128)],
            base,
            ze,
            *around,
            *w_op,
            gather,
            ptd,
            *([] if k else [extra]),
            name="restrict",
        )
        if k == 0:
            mask, pte, x = call(
                coarse_kernel,
                [kept(64 * 128, 128, dtype=BF16), shape(CW, EXT, 128), shape(64, 8, 128)],
                *everywhere_by_core(p),
                id_col,
                ptd,
                *got,
                name="coarse",
            )
        else:
            x = everywhere(p).reshape(64, 8, 128)
        ye, *sends = call(
            correct_kernel,
            [shape(ROWS, 128)] + halo,
            x,
            mask,
            pte,
            z,
            w,
            *w_op,
            gather,
            wj,
            pick,
            scratch=[pltpu.VMEM((16, 64 * 128), BF16)],
            name="correct",
        )
        around = exchange(sends)
        base, *known = call(
            functools.partial(before_advance, k) if k < 3 else before_last,
            [shape(ROWS, 128)] if k < 3 else [shape(ROWS, 128), shape(16, 128)],
            slopes,
            v,
            ye,
            *w_op,
            *([] if k < 3 else basis[:3]),
            flops=500_000_000,
            name="before_advance",
        )
        if k < 3:
            v, z, ze, *sends = call(
                advance_kernel,
                [shape(ROWS, 128)] * 3 + halo,
                base,
                ye,
                *around,
                *w_op,
                gather,
                wj,
                pick,
                name="advance",
            )
            basis.append(v)
            around = exchange(sends)
    v, gram = call(
        last_kernel,
        [shape(ROWS, 128), shape(1, 128)],
        base,
        ye,
        *around,
        *w_op,
        gather,
        *basis,
        *known,
        name="last",
    )
    basis.append(v)
    grams = everywhere(gram).reshape(128, 128)
    total = float(ROWS * BS * 128)
    return tuple(
        call(
            functools.partial(orthogonal_kernel, total),
            [shape(5, ROWS, BS), shape(5, 5)],
            grams,
            *basis,
            name="orthogonal",
        )
    )


def solution(mesh):
    rows = ("gx", "gy")
    in_specs = (
        P(rows, None),
        P(),
        P(rows, None, None),
        P(rows, None, None, None),
        P(rows, None, None),
        P(rows, None, None),
        P(rows, None, None),
        P(rows, None),
        P(rows, None, None),
        P(rows, None),
        P(rows),
    )
    return jax.shard_map(
        per_device, mesh=mesh, in_specs=in_specs, out_specs=(P(None, rows, None), P()), check_vma=False
    )
```

```python
import functools

import jax
import jax.numpy as jnp
from jax import lax
from jax.experimental import pallas as pl
from jax.experimental.pallas import tpu as pltpu
from jax.sharding import PartitionSpec as P

F32 = jnp.float32
BF16 = jnp.bfloat16
ROWS = 48
BS = 64
CW = 8
HALO = 16
EXT = ROWS + 4 * HALO
KOFF = 6
EARLY = 8
OWN = 6 * 128
WIDTH = 7 * 128
jacobi_weight = 2.0 / 3.0
PAIRS = [(j, l) for l in range(5) for j in range(l + 1)]

VM = pl.BlockSpec(memory_space=pltpu.VMEM)
HBM = pl.BlockSpec(memory_space=pltpu.HBM)
LAST = (((1,), (1,)), ((), ()))


def low_lanes(x):
    return lax.broadcasted_iota(jnp.int32, x.shape, 1) < BS


def swap(x):
    return pltpu.roll(x, BS, 1)


def twice(x):
    return jnp.concatenate([x, x], axis=1)


def pack(x):
    high = x.astype(BF16).astype(F32)
    return jnp.where(low_lanes(x), high, (x - high).astype(BF16).astype(F32))


def lhs_parts(packed):
    low = low_lanes(packed)
    turned = swap(packed)
    return jnp.where(low, packed, turned), jnp.where(low, turned, 0.0)


def row_blocks(top, bottom, w_ref, first=0):
    out = []
    for g in range(ROWS // 8):
        lhs = jnp.concatenate([top[8 * g : 8 * g + 8], bottom[8 * g : 8 * g + 8]], axis=0).astype(BF16)
        ref, n = (w_ref[g // 3], g % 3) if isinstance(w_ref, tuple) else (w_ref, g)
        r = jnp.dot(
            lhs, ref[first : first + top.shape[1], 512 * n : 512 * n + 512], preferred_element_type=F32
        )
        s = r[:8] + r[8:]
        own = lax.broadcasted_iota(jnp.int32, s.shape, 0) == lax.broadcasted_iota(jnp.int32, s.shape, 1) // BS
        s = jnp.where(own, s, 0.0)
        t = (s[:, 0:128] + s[:, 128:256]) + (s[:, 256:384] + s[:, 384:512])
        out.append(t + swap(t))
    return jnp.concatenate(out, axis=0)


def smooth(x, wj_ref):
    top, bottom = lhs_parts(pack(x))
    return row_blocks(top, bottom, wj_ref)


def operate_own(packed, w_ref):
    top, bottom = lhs_parts(packed)
    return row_blocks(top, bottom, w_ref, OWN)


def operate(packed, w_ref, gather_ref, own=True):
    e = jnp.concatenate([packed, jnp.zeros((128 - EXT, 128), F32)], axis=0)
    s = swap(e)
    low = low_lanes(e)
    zero = jnp.zeros_like(e)
    rhs = jnp.concatenate(
        [
            jnp.concatenate([jnp.where(low, e, zero), jnp.where(low, s, zero)], axis=1),
            jnp.concatenate([jnp.where(low, zero, s), jnp.where(low, zero, e)], axis=1),
        ],
        axis=0,
    ).astype(BF16)
    x = jnp.dot(gather_ref[...], rhs, preferred_element_type=F32)
    high = [x[ROWS * p : ROWS * p + ROWS, 0:128] for p in range(3)]
    rest = [x[ROWS * p : ROWS * p + ROWS, 128:256] for p in range(3)]
    none = [jnp.zeros((ROWS, 128), F32)] * 3
    top, bottom = high + high, rest + none
    if own:
        for x, part in zip((top, bottom), lhs_parts(packed[:ROWS])):
            x.append(part)
    return row_blocks(jnp.concatenate(top, axis=1), jnp.concatenate(bottom, axis=1), w_ref)


def send_lists(packed, pick_ref, outs):
    picked = jnp.dot(pick_ref[...], packed.astype(BF16), preferred_element_type=F32)
    for s, out in enumerate(outs):
        out[...] = picked[HALO * s : HALO * s + HALO]


def pair_rows(x):
    t = twice(x).T
    high = t.astype(BF16).astype(F32)
    return jnp.where(lax.broadcasted_iota(jnp.int32, t.shape, 0) < BS, high, t - high).astype(BF16)


def column(line):
    line = jnp.concatenate([line, jnp.zeros((1, 128 - line.shape[1]), F32)], axis=1)
    return jnp.broadcast_to(line, (128, 128)).T


def first_kernel(*refs):
    sources, off, rest = refs[:7], refs[7], refs[8:]
    v, wj, ptd, pick, z, ze, ids, spared, slopes, s0, s1, s2, s3, near = rest[:14]
    here, sems, far = rest[14:21], rest[21], rest[22]
    copies = [pltpu.make_async_copy(x, y, sems.at[n]) for n, (x, y) in enumerate(zip(sources, here))]
    for c in copies:
        c.start()
    ahead = pltpu.make_async_copy(off.at[pl.ds(0, EARLY)], near, far)
    ahead.start()
    for c in copies:
        c.wait()
    start, jac, pt, listed, owner, slot, shifts = here
    v[...] = twice(start[...])
    for n in range(ROWS // 2):
        wj[:, 128 * n : 128 * n + 128] = pair_rows(jac[128 * n : 128 * n + 128, :] * jacobi_weight)
    z[...] = smooth(v[...], wj)
    ze[...] = pack(z[...])
    even_x = lax.axis_index("gx") % 2 == 0
    even_y = lax.axis_index("gy") % 2 == 0
    lists = listed[...].astype(F32)
    order = [
        jnp.where(even_x, lists[1:2], lists[0:1]),
        jnp.where(even_x, lists[0:1], lists[1:2]),
        jnp.where(even_y, lists[3:4], lists[2:3]),
        jnp.where(even_y, lists[2:3], lists[3:4]),
    ]
    chosen = jnp.concatenate([column(x)[0:HALO, 0:ROWS] for x in order], axis=0)
    chosen = (chosen == lax.broadcasted_iota(jnp.int32, (4 * HALO, ROWS), 1).astype(F32)).astype(F32)
    pick[...] = chosen.astype(BF16)
    number = (owner[...] * 24 + slot[...]).astype(F32)
    ids[...] = column(number)[0:ROWS]
    for c in range(CW):
        ptd[c] = twice(pt[:, c, :])
    low = lax.broadcasted_iota(jnp.int32, (ROWS, 128), 1) < BS
    parts = [jnp.where(low, ptd[r], ptd[r + 4]) for r in range(4)] + [ids[...]]
    parts = [jnp.dot(chosen, x, precision=lax.Precision.HIGHEST, preferred_element_type=F32) for x in parts]
    parts = [jnp.dot(pick[...], ze[...].astype(BF16), preferred_element_type=F32)] + parts
    for s, out in enumerate((s0, s1, s2, s3)):
        for k, x in enumerate(parts):
            out[k] = x[HALO * s : HALO * s + HALO]
    number = jnp.concatenate([number, jnp.zeros((1, 128 - ROWS), F32)], axis=1)
    lane = lax.broadcasted_iota(jnp.int32, (1, 128), 1)
    spare = (lane >= ROWS) & (lane < BS)
    for r in range(3):
        spared[r : r + 1, :] = jnp.where(spare, pltpu.roll(jnp.broadcast_to(number, (8, 128)), ROWS - 16 * r, 1)[0:1], 0.0)
    spared[3:4, :] = jnp.zeros((1, 128), F32)
    for k in range(4):
        slopes[k : k + 1, :] = jnp.broadcast_to(shifts[:, k : k + 1], (1, 128))
    ahead.wait()


def pack_rows(buf, n, dbuf, row, w):
    at = BS * (row % (ROWS // 2))
    at = slice(at, at + 128)
    for p in range(3):
        x = jnp.concatenate(
            [
                jnp.concatenate([buf[n, 2 * p], buf[n, 2 * p + 1]], axis=1),
                jnp.concatenate([buf[n + 1, 2 * p], buf[n + 1, 2 * p + 1]], axis=1),
            ],
            axis=0,
        ).T
        high = x.astype(BF16)
        w[128 * p : 128 * p + 128, at] = high
        w[384 + 128 * p : 512 + 128 * p, at] = (x - high.astype(F32)).astype(BF16)
    w[768:896, at] = pair_rows(jnp.concatenate([dbuf[row], dbuf[row + 1]], axis=0))


def operator_kernel(off, diag, cols, inverse, near, wa, wb, gather, inv, buf, dbuf, cbuf, ibuf, sems, isem):
    steps = (ROWS - EARLY) // 8
    named = pltpu.make_async_copy(cols, cbuf, sems.at[0])
    named.start()
    small = pltpu.make_async_copy(inverse, ibuf, isem)
    small.start()
    middle = pltpu.make_async_copy(diag, dbuf, sems.at[1])
    middle.start()
    later = [
        pltpu.make_async_copy(off.at[pl.ds(EARLY + 8 * g, 8)], buf.at[pl.ds(8 * g, 8)], sems.at[2 + g])
        for g in range(steps)
    ]
    for c in later[:3]:
        c.start()
    named.wait()
    turn_x = (lax.axis_index("gx") % 2) * HALO
    turn_y = (lax.axis_index("gy") % 2) * HALO
    number = cbuf[...]
    beyond = number - ROWS
    turned = ROWS + (beyond ^ jnp.where(beyond < 2 * HALO, turn_x, turn_y))
    number = jnp.where(beyond >= 0, turned, number).astype(F32)
    number = jnp.concatenate([number, jnp.zeros((KOFF, 128 - ROWS), F32)], axis=1)
    number = jnp.concatenate([number, jnp.zeros((128 - KOFF, 128), F32)], axis=0).T[0:ROWS]
    lane = lax.broadcasted_iota(jnp.int32, (ROWS, 256), 1).astype(F32)
    for p in range(3):
        hit = (lane == number[:, 2 * p : 2 * p + 1]) | (lane == number[:, 2 * p + 1 : 2 * p + 2] + 128.0)
        gather[ROWS * p : ROWS * p + ROWS, :] = hit.astype(F32).astype(BF16)
    small.wait()
    wide = jnp.concatenate([ibuf[...], jnp.zeros((BS, 104), F32)], axis=1)
    wide = jnp.concatenate([wide, jnp.zeros((BS, 128), F32)], axis=0).T[0:24]
    inv[...] = wide[0:12] + swap(wide[12:24])
    middle.wait()
    for n in range(0, EARLY, 2):
        pack_rows(near, n, dbuf, n, wa)
    for g in range(steps):
        later[g].wait()
        if g + 3 < steps:
            later[g + 3].start()
        for n in range(8 * g, 8 * g + 8, 2):
            pack_rows(buf, n, dbuf, EARLY + n, wa if EARLY + n < ROWS // 2 else wb)


def before_restrict(v, ze, wa, wb, base):
    base[...] = v[...] - operate_own(ze[...], (wa, wb))


def before_advance(k, slopes, v, ye, wa, wb, base):
    base[...] = operate_own(ye[...], (wa, wb)) - slopes[k : k + 1, :] * v[...]


def restrict_kernel(base, ze, h0, h1, h2, h3, wa, wb, gather, ptd, *rest):
    *extra, w, p = rest
    ext = jnp.concatenate([ze[...], h0[...], h1[...], h2[...], h3[...]], axis=0)
    r = base[...] - operate(ext, (wa, wb), gather, own=False)
    w[...] = r
    ones = jnp.ones((16, 128), BF16)
    pad = jnp.zeros((16, 128), F32)
    for k in range(4):
        x = jnp.concatenate([pack(ptd[k] * r), pad, pack(ptd[k + 4] * r), pad], axis=0).astype(BF16)
        line = lax.dot_general(ones, x, LAST, preferred_element_type=F32)[0:1]
        p[k : k + 1, :] = line + extra[0][k : k + 1, :] if extra else line
    if extra:
        p[4:16, :] = extra[1][...]


def coarse_kernel(same, other, ids, ptd, g0, g1, g2, g3, mask, pte, xp):
    idc = jnp.concatenate(
        [ids[...], g0[5], g1[5], g2[5], g3[5], jnp.full((128 - EXT, 128), -1.0, F32)], axis=0
    )
    wanted = idc.T[0:1]
    even = lax.axis_index("gy") % 2 == 0

    def by_core(x, y):
        return jnp.where(even, x, y), jnp.where(even, y, x)

    given = [jnp.concatenate(by_core(same[:, r, :], other[:, r, :]), axis=0).T[ROWS:BS] for r in range(3)] + [jnp.full((BS - ROWS, 128), -1.0, F32)]
    given = jnp.concatenate(given + given, axis=0)
    for q in range(64):
        line = jnp.concatenate([given[0:BS, q : q + 1], given[BS:128, BS + q : BS + q + 1]], axis=0)
        mask[128 * q : 128 * q + 128, :] = (line == wanted).astype(F32).astype(BF16)
        xp[q] = jnp.concatenate(by_core(same[q, 0:4, :], other[q, 0:4, :]), axis=0)
    device = jnp.floor((idc + 0.5) * (1.0 / 24.0))
    slot = idc - 24.0 * device
    upper = slot >= 11.5
    chip = jnp.floor(device * 0.5)
    core = device - 2.0 * chip
    core = jnp.where(even, core, 1.0 - core)
    place = core * 1024.0 + chip * 16.0 + 4.0 + jnp.where(upper, slot - 12.0, slot)
    high, rest = [], []
    for b in range(8):
        src = (same if b < 4 else other)[16 * (b % 4) : 16 * (b % 4) + 16].reshape(256, 128)
        high.append(src.astype(BF16))
        rest.append((src - high[-1].astype(F32)).astype(BF16))
    lane = lax.broadcasted_iota(jnp.int32, (128, 128), 1).astype(F32)
    hit = jnp.concatenate([(place - 128.0 * b == lane).astype(F32).astype(BF16) for b in range(16)], axis=1)
    source = jnp.concatenate([jnp.concatenate(high, axis=0), jnp.concatenate(rest, axis=0)], axis=1)
    total = jnp.dot(hit, source, preferred_element_type=F32)
    total = total[:, 0:128] + total[:, 128:256]
    inverse = jnp.where(upper, swap(total), total)[:EXT]
    wide = []
    for c in range(CW):
        around = [g[1 + c % 4] for g in (g0, g1, g2, g3)]
        around = jnp.concatenate(around, axis=0)
        lowh = low_lanes(around)
        turned = swap(around)
        around = jnp.where(lowh, around, turned) if c < 4 else jnp.where(lowh, turned, around)
        wide.append(jnp.concatenate([ptd[c], around], axis=0))
    for d in range(CW):
        acc = wide[0] * inverse[:, d : d + 1]
        for c in range(1, CW):
            acc = acc + wide[c] * inverse[:, c * CW + d : c * CW + d + 1]
        pte[d] = acc


def correct_kernel(x, mask, pte, z, w, wa, wb, gather, wj, pick, ye, s0, s1, s2, s3, parts):
    sub = lax.broadcasted_iota(jnp.int32, (8, 128), 0) < 4
    lane = lax.broadcasted_iota(jnp.int32, (8, 128), 1) < BS
    keep = sub == lane
    for q in range(64):
        t = x[q]
        t = jnp.where(keep, t, pltpu.roll(swap(t), 4, 0))
        high = t.astype(BF16).astype(F32)
        parts[:, 128 * q : 128 * q + 128] = jnp.concatenate([high, t - high], axis=0).astype(BF16)
    got = jnp.dot(parts[...], mask[...], preferred_element_type=F32)
    coarse = jnp.concatenate([got[0:8] + got[8:16], jnp.zeros((120, 128), F32)], axis=0).T[:EXT]
    u = pte[0] * coarse[:, 0:1]
    for d in range(1, CW):
        u = u + pte[d] * coarse[:, d : d + 1]
    r = w[...] - operate(pack(u), (wa, wb), gather)
    y = z[...] + u[:ROWS] + smooth(r, wj)
    ye[...] = pack(y)
    send_lists(ye[...], pick, (s0, s1, s2, s3))


def advance(base, ye, h0, h1, h2, h3, w_op, gather):
    ext = jnp.concatenate([ye[...], h0[...], h1[...], h2[...], h3[...]], axis=0)
    return operate(ext, w_op, gather, own=False) + base[...]


def advance_kernel(base, ye, h0, h1, h2, h3, wa, wb, gather, wj, pick, vn, z, ze, s0, s1, s2, s3):
    vn[...] = advance(base, ye, h0, h1, h2, h3, (wa, wb), gather)
    z[...] = smooth(vn[...], wj)
    ze[...] = pack(z[...])
    send_lists(ze[...], pick, (s0, s1, s2, s3))


def products(basis, pairs):
    return [jnp.sum(basis[j] * basis[l], axis=0, keepdims=True) for j, l in pairs]


def before_last(slopes, v, ye, wa, wb, v0, v1, v2, base, known):
    before_advance(3, slopes, v, ye, wa, wb, base)
    basis = [x[...] for x in (v0, v1, v2, v)]
    known[...] = jnp.concatenate(products(basis, PAIRS[:10]) + [jnp.zeros((6, 128), F32)], axis=0)


def last_kernel(base, ye, h0, h1, h2, h3, wa, wb, gather, v0, v1, v2, v3, known, v4, gram):
    v4[...] = advance(base, ye, h0, h1, h2, h3, (wa, wb), gather)
    basis = [v[...] for v in (v0, v1, v2, v3, v4)]
    rows = [known[0:10, :]] + products(basis, PAIRS[10:]) + [jnp.zeros((113, 128), F32)]
    sums = lax.dot_general(
        jnp.ones((8, 128), F32),
        jnp.concatenate(rows, axis=0),
        LAST,
        precision=lax.Precision.HIGHEST,
        preferred_element_type=F32,
    )
    gram[...] = sums[0:1]


def orthogonal_kernel(total, grams, v0, v1, v2, v3, v4, q_out, r_out):
    sums = jnp.sum(grams[...], axis=0, keepdims=True) * (1.0 / (2.0 * total))
    g = {pair: sums[:, n : n + 1] for n, pair in enumerate(PAIRS)}
    lower = {}
    for j in range(5):
        d = g[(j, j)]
        for k in range(j):
            d = d - lower[(j, k)] * lower[(j, k)]
        lower[(j, j)] = jnp.sqrt(d)
        for i in range(j + 1, 5):
            t = g[(j, i)]
            for k in range(j):
                t = t - lower[(i, k)] * lower[(j, k)]
            lower[(i, j)] = t / lower[(j, j)]
    at_row = lax.broadcasted_iota(jnp.int32, (8, 128), 0)
    at_col = lax.broadcasted_iota(jnp.int32, (8, 128), 1)
    r = jnp.zeros((8, 128), F32)
    for (i, j), value in lower.items():
        r = jnp.where((at_row == j) & (at_col == i), value, r)
    r_out[...] = r[0:5, 0:5]
    solved = []
    for i, v in enumerate((v0, v1, v2, v3, v4)):
        t = v[...]
        for k in range(i):
            t = t - lower[(i, k)] * solved[k]
        t = t / lower[(i, i)]
        solved.append(t)
        q_out[i] = t[:, 0:BS]


def shape(*dims, dtype=F32):
    return jax.ShapeDtypeStruct(dims, dtype)


def kept(*dims, dtype=F32):
    return pltpu.VMEM(dims, dtype)


def call(kernel, outs, *args, specs=None, scratch=(), flops=2_000_000, name=None):
    return pl.pallas_call(
        kernel,
        out_shape=outs,
        in_specs=specs or [VM] * len(args),
        out_specs=jax.tree.map(lambda _: VM, outs),
        scratch_shapes=list(scratch),
        compiler_params=pltpu.CompilerParams(vmem_limit_bytes=24 << 20),
        cost_estimate=pl.CostEstimate(flops=flops, bytes_accessed=100_000, transcendentals=0),
        name=name,
    )(*args)


def swap_pairs(count, phase):
    if phase == 0:
        return [(i, i ^ 1) for i in range(count)]
    return [(i, (i - 1) % count if i % 2 == 0 else (i + 1) % count) for i in range(count)]


def exchange(sends):
    nx, ny = lax.axis_size("gx"), lax.axis_size("gy")
    return (
        lax.ppermute(sends[0], "gx", swap_pairs(nx, 1)),
        lax.ppermute(sends[1], "gx", swap_pairs(nx, 0)),
        lax.ppermute(sends[2], "gy", swap_pairs(ny, 1)),
        lax.ppermute(sends[3], "gy", swap_pairs(ny, 0)),
    )


def everywhere(x):
    count = lax.axis_size("gx") * lax.axis_size("gy")
    y = jnp.broadcast_to(x[None], (count,) + x.shape)
    return lax.all_to_all(y, ("gx", "gy"), split_axis=0, concat_axis=0, tiled=True)


def everywhere_by_core(x):
    nx, ny = lax.axis_size("gx"), lax.axis_size("gy")
    groups = [[p * ny + q for p in range(nx) for q in range(core, ny, 2)] for core in range(2)]
    y = jnp.broadcast_to(x[None], (nx * ny // 2,) + x.shape)
    same = lax.all_to_all(y, ("gx", "gy"), split_axis=0, concat_axis=0, tiled=True, axis_index_groups=groups)
    return same, lax.ppermute(same, "gy", swap_pairs(ny, 0))


def per_device(start, shifts, diag_blocks, off_blocks, jacobi_inv, prolong, coarse_inv, cols, send_rows, owner, agg_slot):
    halo = [shape(HALO, 128)] * 4
    matrices = [pltpu.with_memory_space_constraint(x, pltpu.HBM) for x in (off_blocks, diag_blocks, jnp.transpose(cols))]
    sources = [
        start,
        jacobi_inv.reshape(ROWS * BS, BS),
        jnp.transpose(prolong, (0, 2, 1)),
        send_rows[0],
        owner.reshape(1, ROWS),
        agg_slot.reshape(1, ROWS),
        shifts.reshape(1, 4),
    ]
    v, wj, ptd, pick, z, ze, id_col, spared, slopes, *sends, near = call(
        first_kernel,
        [
            shape(ROWS, 128),
            kept(128, ROWS * BS, dtype=BF16),
            shape(CW, ROWS, 128),
            shape(4 * HALO, ROWS, dtype=BF16),
            shape(ROWS, 128),
            shape(ROWS, 128),
            shape(ROWS, 128),
            shape(4, 128),
            shape(4, 128),
        ]
        + [shape(6, HALO, 128)] * 4
        + [kept(EARLY, KOFF, BS, BS)],
        *[pltpu.with_memory_space_constraint(x, pltpu.HBM) for x in sources],
        matrices[0],
        specs=[HBM] * (len(sources) + 1),
        scratch=[pltpu.VMEM(x.shape, x.dtype) for x in sources]
        + [pltpu.SemaphoreType.DMA((len(sources),)), pltpu.SemaphoreType.DMA],
        name="first",
    )
    got = exchange(sends)
    half = kept(WIDTH, ROWS * BS // 2, dtype=BF16)
    inverse = jnp.transpose(coarse_inv, (1, 2, 0)).reshape(BS, 24)
    *w_op, gather, inv = call(
        operator_kernel,
        [half, half, shape(3 * ROWS, 256, dtype=BF16), shape(12, 128)],
        *matrices,
        pltpu.with_memory_space_constraint(inverse, pltpu.HBM),
        near,
        specs=[HBM] * 4 + [VM],
        scratch=[
            pltpu.VMEM((ROWS - EARLY, KOFF, BS, BS), F32),
            pltpu.VMEM((ROWS, BS, BS), F32),
            pltpu.VMEM((KOFF, ROWS), jnp.int32),
            pltpu.VMEM((BS, 24), F32),
            pltpu.SemaphoreType.DMA((2 + (ROWS - EARLY) // 8,)),
            pltpu.SemaphoreType.DMA,
        ],
        flops=2_000_000_000,
        name="operator",
    )
    around = [g[0] for g in got]
    basis = [v]
    mask = pte = None
    for k in range(4):
        (base,) = call(before_restrict, [shape(ROWS, 128)], v, ze, *w_op, flops=500_000_000, name="before_restrict")
        w, p = call(
            restrict_kernel,
            [shape(ROWS, 128), shape(4 if k else 16, 128)],
            base,
            ze,
            *around,
            *w_op,
            gather,
            ptd,
            *([] if k else [spared, inv]),
            name="restrict",
        )
        if k == 0:
            mask, pte, x = call(
                coarse_kernel,
                [kept(64 * 128, 128, dtype=BF16), shape(CW, EXT, 128), shape(64, 8, 128)],
                *everywhere_by_core(p),
                id_col,
                ptd,
                *got,
                name="coarse",
            )
        else:
            x = everywhere(p).reshape(64, 8, 128)
        ye, *sends = call(
            correct_kernel,
            [shape(ROWS, 128)] + halo,
            x,
            mask,
            pte,
            z,
            w,
            *w_op,
            gather,
            wj,
            pick,
            scratch=[pltpu.VMEM((16, 64 * 128), BF16)],
            name="correct",
        )
        around = exchange(sends)
        base, *known = call(
            functools.partial(before_advance, k) if k < 3 else before_last,
            [shape(ROWS, 128)] if k < 3 else [shape(ROWS, 128), shape(16, 128)],
            slopes,
            v,
            ye,
            *w_op,
            *([] if k < 3 else basis[:3]),
            flops=500_000_000,
            name="before_advance",
        )
        if k < 3:
            v, z, ze, *sends = call(
                advance_kernel,
                [shape(ROWS, 128)] * 3 + halo,
                base,
                ye,
                *around,
                *w_op,
                gather,
                wj,
                pick,
                name="advance",
            )
            basis.append(v)
            around = exchange(sends)
    v, gram = call(
        last_kernel,
        [shape(ROWS, 128), shape(1, 128)],
        base,
        ye,
        *around,
        *w_op,
        gather,
        *basis,
        *known,
        name="last",
    )
    basis.append(v)
    grams = everywhere(gram).reshape(128, 128)
    total = float(ROWS * BS * 128)
    return tuple(
        call(
            functools.partial(orthogonal_kernel, total),
            [shape(5, ROWS, BS), shape(5, 5)],
            grams,
            *basis,
            name="orthogonal",
        )
    )


def solution(mesh):
    rows = ("gx", "gy")
    in_specs = (
        P(rows, None),
        P(),
        P(rows, None, None),
        P(rows, None, None, None),
        P(rows, None, None),
        P(rows, None, None),
        P(rows, None, None),
        P(rows, None),
        P(rows, None, None),
        P(rows, None),
        P(rows),
    )
    return jax.shard_map(
        per_device, mesh=mesh, in_specs=in_specs, out_specs=(P(None, rows, None), P()), check_vma=False
    )
```

```python
import functools

import jax
import jax.numpy as jnp
from jax import lax
from jax.experimental import pallas as pl
from jax.experimental.pallas import tpu as pltpu
from jax.sharding import PartitionSpec as P

F32 = jnp.float32
BF16 = jnp.bfloat16
ROWS = 48
BS = 64
CW = 8
HALO = 16
EXT = ROWS + 4 * HALO
KOFF = 6
EARLY = 16
OWN = 6 * 128
WIDTH = 7 * 128
jacobi_weight = 2.0 / 3.0
PAIRS = [(j, l) for l in range(5) for j in range(l + 1)]

VM = pl.BlockSpec(memory_space=pltpu.VMEM)
HBM = pl.BlockSpec(memory_space=pltpu.HBM)
LAST = (((1,), (1,)), ((), ()))


def low_lanes(x):
    return lax.broadcasted_iota(jnp.int32, x.shape, 1) < BS


def swap(x):
    return pltpu.roll(x, BS, 1)


def twice(x):
    return jnp.concatenate([x, x], axis=1)


def pack(x):
    high = x.astype(BF16).astype(F32)
    return jnp.where(low_lanes(x), high, (x - high).astype(BF16).astype(F32))


def lhs_parts(packed):
    low = low_lanes(packed)
    turned = swap(packed)
    return jnp.where(low, packed, turned), jnp.where(low, turned, 0.0)


def row_blocks(top, bottom, w_ref, first=0):
    out = []
    for g in range(ROWS // 8):
        lhs = jnp.concatenate([top[8 * g : 8 * g + 8], bottom[8 * g : 8 * g + 8]], axis=0).astype(BF16)
        ref, n = (w_ref[g // 3], g % 3) if isinstance(w_ref, tuple) else (w_ref, g)
        r = jnp.dot(
            lhs, ref[first : first + top.shape[1], 512 * n : 512 * n + 512], preferred_element_type=F32
        )
        s = r[:8] + r[8:]
        own = lax.broadcasted_iota(jnp.int32, s.shape, 0) == lax.broadcasted_iota(jnp.int32, s.shape, 1) // BS
        s = jnp.where(own, s, 0.0)
        t = (s[:, 0:128] + s[:, 128:256]) + (s[:, 256:384] + s[:, 384:512])
        out.append(t + swap(t))
    return jnp.concatenate(out, axis=0)


def smooth(x, wj_ref):
    top, bottom = lhs_parts(pack(x))
    return row_blocks(top, bottom, wj_ref)


def operate_own(packed, w_ref):
    top, bottom = lhs_parts(packed)
    return row_blocks(top, bottom, w_ref, OWN)


def operate(packed, w_ref, gather_ref, own=True):
    e = jnp.concatenate([packed, jnp.zeros((128 - EXT, 128), F32)], axis=0)
    s = swap(e)
    low = low_lanes(e)
    zero = jnp.zeros_like(e)
    rhs = jnp.concatenate(
        [
            jnp.concatenate([jnp.where(low, e, zero), jnp.where(low, s, zero)], axis=1),
            jnp.concatenate([jnp.where(low, zero, s), jnp.where(low, zero, e)], axis=1),
        ],
        axis=0,
    ).astype(BF16)
    x = jnp.dot(gather_ref[...], rhs, preferred_element_type=F32)
    high = [x[ROWS * p : ROWS * p + ROWS, 0:128] for p in range(3)]
    rest = [x[ROWS * p : ROWS * p + ROWS, 128:256] for p in range(3)]
    none = [jnp.zeros((ROWS, 128), F32)] * 3
    top, bottom = high + high, rest + none
    if own:
        for x, part in zip((top, bottom), lhs_parts(packed[:ROWS])):
            x.append(part)
    return row_blocks(jnp.concatenate(top, axis=1), jnp.concatenate(bottom, axis=1), w_ref)


def send_lists(packed, pick_ref, outs):
    picked = jnp.dot(pick_ref[...], packed.astype(BF16), preferred_element_type=F32)
    for s, out in enumerate(outs):
        out[...] = picked[HALO * s : HALO * s + HALO]


def pair_rows(x):
    t = twice(x).T
    high = t.astype(BF16).astype(F32)
    return jnp.where(lax.broadcasted_iota(jnp.int32, t.shape, 0) < BS, high, t - high).astype(BF16)


def column(line):
    line = jnp.concatenate([line, jnp.zeros((1, 128 - line.shape[1]), F32)], axis=1)
    return jnp.broadcast_to(line, (128, 128)).T


def first_kernel(*refs):
    sources, off, rest = refs[:8], refs[8], refs[9:]
    v, wj, ptd, pick, z, ze, ids, extra, slopes, s0, s1, s2, s3, near = rest[:14]
    here, sems, far = rest[14:22], rest[22], rest[23]
    copies = [pltpu.make_async_copy(x, y, sems.at[n]) for n, (x, y) in enumerate(zip(sources, here))]
    for c in copies:
        c.start()
    ahead = pltpu.make_async_copy(off.at[pl.ds(0, EARLY)], near, far)
    ahead.start()
    for c in copies:
        c.wait()
    start, jac, pt, inverse, listed, owner, slot, shifts = here
    v[...] = twice(start[...])
    for n in range(ROWS // 2):
        wj[:, 128 * n : 128 * n + 128] = pair_rows(jac[128 * n : 128 * n + 128, :] * jacobi_weight)
    z[...] = smooth(v[...], wj)
    ze[...] = pack(z[...])
    even_x = lax.axis_index("gx") % 2 == 0
    even_y = lax.axis_index("gy") % 2 == 0
    lists = listed[...].astype(F32)
    order = [
        jnp.where(even_x, lists[1:2], lists[0:1]),
        jnp.where(even_x, lists[0:1], lists[1:2]),
        jnp.where(even_y, lists[3:4], lists[2:3]),
        jnp.where(even_y, lists[2:3], lists[3:4]),
    ]
    chosen = jnp.concatenate([column(x)[0:HALO, 0:ROWS] for x in order], axis=0)
    chosen = (chosen == lax.broadcasted_iota(jnp.int32, (4 * HALO, ROWS), 1).astype(F32)).astype(F32)
    pick[...] = chosen.astype(BF16)
    number = (owner[...] * 24 + slot[...]).astype(F32)
    ids[...] = column(number)[0:ROWS]
    for c in range(CW):
        ptd[c] = twice(pt[:, c, :])
    low = lax.broadcasted_iota(jnp.int32, (ROWS, 128), 1) < BS
    parts = [jnp.where(low, ptd[r], ptd[r + 4]) for r in range(4)] + [ids[...]]
    high = [x.astype(BF16) for x in parts]
    rest = [(x - y.astype(F32)).astype(BF16) for x, y in zip(parts, high)]
    picked = jnp.concatenate([ze[...].astype(BF16)] + high + rest, axis=1)
    picked = jnp.dot(pick[...], picked, preferred_element_type=F32)
    parts = [picked[:, 0:128]]
    for k in range(1, 6):
        parts.append(picked[:, 128 * k : 128 * k + 128] + picked[:, 128 * k + 640 : 128 * k + 768])
    for s, out in enumerate((s0, s1, s2, s3)):
        for k, x in enumerate(parts):
            out[k] = x[HALO * s : HALO * s + HALO]
    wide = jnp.concatenate([inverse[...], jnp.zeros((BS, 104), F32)], axis=1)
    wide = jnp.concatenate([wide, jnp.zeros((BS, 128), F32)], axis=0).T[0:24]
    extra[4:16, :] = wide[0:12] + swap(wide[12:24])
    number = jnp.concatenate([number, jnp.zeros((1, 128 - ROWS), F32)], axis=1)
    lane = lax.broadcasted_iota(jnp.int32, (1, 128), 1)
    spare = (lane >= ROWS) & (lane < BS)
    for r in range(3):
        extra[r : r + 1, :] = jnp.where(spare, pltpu.roll(jnp.broadcast_to(number, (8, 128)), ROWS - 16 * r, 1)[0:1], 0.0)
    extra[3:4, :] = jnp.zeros((1, 128), F32)
    for k in range(4):
        slopes[k : k + 1, :] = jnp.broadcast_to(shifts[:, k : k + 1], (1, 128))
    ahead.wait()


def pack_rows(buf, n, dbuf, row, w):
    at = BS * (row % (ROWS // 2))
    at = slice(at, at + 128)
    for p in range(3):
        x = jnp.concatenate(
            [
                jnp.concatenate([buf[n, 2 * p], buf[n, 2 * p + 1]], axis=1),
                jnp.concatenate([buf[n + 1, 2 * p], buf[n + 1, 2 * p + 1]], axis=1),
            ],
            axis=0,
        ).T
        high = x.astype(BF16)
        w[128 * p : 128 * p + 128, at] = high
        w[384 + 128 * p : 512 + 128 * p, at] = (x - high.astype(F32)).astype(BF16)
    w[768:896, at] = pair_rows(jnp.concatenate([dbuf[row], dbuf[row + 1]], axis=0))


def operator_kernel(off, diag, cols, near, wa, wb, gather, buf, dbuf, cbuf, sems):
    steps = (ROWS - EARLY) // 8
    named = pltpu.make_async_copy(cols, cbuf, sems.at[0])
    named.start()
    middle = pltpu.make_async_copy(diag, dbuf, sems.at[1])
    middle.start()
    later = [
        pltpu.make_async_copy(off.at[pl.ds(EARLY + 8 * g, 8)], buf.at[pl.ds(8 * g, 8)], sems.at[2 + g])
        for g in range(steps)
    ]
    for c in later:
        c.start()
    named.wait()
    turn_x = (lax.axis_index("gx") % 2) * HALO
    turn_y = (lax.axis_index("gy") % 2) * HALO
    number = cbuf[...]
    beyond = number - ROWS
    turned = ROWS + (beyond ^ jnp.where(beyond < 2 * HALO, turn_x, turn_y))
    number = jnp.where(beyond >= 0, turned, number).astype(F32)
    number = jnp.concatenate([number, jnp.zeros((KOFF, 128 - ROWS), F32)], axis=1)
    number = jnp.concatenate([number, jnp.zeros((128 - KOFF, 128), F32)], axis=0).T[0:ROWS]
    lane = lax.broadcasted_iota(jnp.int32, (ROWS, 256), 1).astype(F32)
    for p in range(3):
        hit = (lane == number[:, 2 * p : 2 * p + 1]) | (lane == number[:, 2 * p + 1 : 2 * p + 2] + 128.0)
        gather[ROWS * p : ROWS * p + ROWS, :] = hit.astype(F32).astype(BF16)
    middle.wait()
    for n in range(0, EARLY, 2):
        pack_rows(near, n, dbuf, n, wa)
    for g in range(steps):
        later[g].wait()
        for n in range(8 * g, 8 * g + 8, 2):
            pack_rows(buf, n, dbuf, EARLY + n, wa if EARLY + n < ROWS // 2 else wb)


def before_restrict(v, ze, wa, wb, base):
    base[...] = v[...] - operate_own(ze[...], (wa, wb))


def before_advance(k, slopes, v, ye, wa, wb, base):
    base[...] = operate_own(ye[...], (wa, wb)) - slopes[k : k + 1, :] * v[...]


def restrict_kernel(base, ze, h0, h1, h2, h3, wa, wb, gather, ptd, *rest):
    *extra, w, p = rest
    ext = jnp.concatenate([ze[...], h0[...], h1[...], h2[...], h3[...]], axis=0)
    r = base[...] - operate(ext, (wa, wb), gather, own=False)
    w[...] = r
    ones = jnp.ones((16, 128), BF16)
    pad = jnp.zeros((16, 128), F32)
    for k in range(4):
        x = jnp.concatenate([pack(ptd[k] * r), pad, pack(ptd[k + 4] * r), pad], axis=0).astype(BF16)
        line = lax.dot_general(ones, x, LAST, preferred_element_type=F32)[0:1]
        p[k : k + 1, :] = line + extra[0][k : k + 1, :] if extra else line
    if extra:
        p[4:16, :] = extra[0][4:16, :]


def coarse_kernel(same, other, ids, ptd, g0, g1, g2, g3, mask, pte, xp):
    idc = jnp.concatenate(
        [ids[...], g0[5], g1[5], g2[5], g3[5], jnp.full((128 - EXT, 128), -1.0, F32)], axis=0
    )
    wanted = idc.T[0:1]
    even = lax.axis_index("gy") % 2 == 0

    def by_core(x, y):
        return jnp.where(even, x, y), jnp.where(even, y, x)

    given = [jnp.concatenate(by_core(same[:, r, :], other[:, r, :]), axis=0).T[ROWS:BS] for r in range(3)] + [jnp.full((BS - ROWS, 128), -1.0, F32)]
    given = jnp.concatenate(given + given, axis=0)
    for q in range(64):
        line = jnp.concatenate([given[0:BS, q : q + 1], given[BS:128, BS + q : BS + q + 1]], axis=0)
        mask[128 * q : 128 * q + 128, :] = (line == wanted).astype(F32).astype(BF16)
        xp[q] = jnp.concatenate(by_core(same[q, 0:4, :], other[q, 0:4, :]), axis=0)
    device = jnp.floor((idc + 0.5) * (1.0 / 24.0))
    slot = idc - 24.0 * device
    upper = slot >= 11.5
    chip = jnp.floor(device * 0.5)
    core = device - 2.0 * chip
    core = jnp.where(even, core, 1.0 - core)
    place = core * 1024.0 + chip * 16.0 + 4.0 + jnp.where(upper, slot - 12.0, slot)
    high, rest = [], []
    for b in range(8):
        src = (same if b < 4 else other)[16 * (b % 4) : 16 * (b % 4) + 16].reshape(256, 128)
        high.append(src.astype(BF16))
        rest.append((src - high[-1].astype(F32)).astype(BF16))
    lane = lax.broadcasted_iota(jnp.int32, (128, 128), 1).astype(F32)
    hit = jnp.concatenate([(place - 128.0 * b == lane).astype(F32).astype(BF16) for b in range(16)], axis=1)
    source = jnp.concatenate([jnp.concatenate(high, axis=0), jnp.concatenate(rest, axis=0)], axis=1)
    total = jnp.dot(hit, source, preferred_element_type=F32)
    total = total[:, 0:128] + total[:, 128:256]
    inverse = jnp.where(upper, swap(total), total)[:EXT]
    wide = []
    for c in range(CW):
        around = [g[1 + c % 4] for g in (g0, g1, g2, g3)]
        around = jnp.concatenate(around, axis=0)
        lowh = low_lanes(around)
        turned = swap(around)
        around = jnp.where(lowh, around, turned) if c < 4 else jnp.where(lowh, turned, around)
        wide.append(jnp.concatenate([ptd[c], around], axis=0))
    for d in range(CW):
        acc = wide[0] * inverse[:, d : d + 1]
        for c in range(1, CW):
            acc = acc + wide[c] * inverse[:, c * CW + d : c * CW + d + 1]
        pte[d] = acc


def correct_kernel(x, mask, pte, z, w, wa, wb, gather, wj, pick, ye, s0, s1, s2, s3, parts):
    sub = lax.broadcasted_iota(jnp.int32, (8, 128), 0) < 4
    lane = lax.broadcasted_iota(jnp.int32, (8, 128), 1) < BS
    keep = sub == lane
    for q in range(64):
        t = x[q]
        t = jnp.where(keep, t, pltpu.roll(swap(t), 4, 0))
        high = t.astype(BF16).astype(F32)
        parts[:, 128 * q : 128 * q + 128] = jnp.concatenate([high, t - high], axis=0).astype(BF16)
    got = jnp.dot(parts[...], mask[...], preferred_element_type=F32)
    coarse = jnp.concatenate([got[0:8] + got[8:16], jnp.zeros((120, 128), F32)], axis=0).T[:EXT]
    u = pte[0] * coarse[:, 0:1]
    for d in range(1, CW):
        u = u + pte[d] * coarse[:, d : d + 1]
    r = w[...] - operate(pack(u), (wa, wb), gather)
    y = z[...] + u[:ROWS] + smooth(r, wj)
    ye[...] = pack(y)
    send_lists(ye[...], pick, (s0, s1, s2, s3))


def advance(base, ye, h0, h1, h2, h3, w_op, gather):
    ext = jnp.concatenate([ye[...], h0[...], h1[...], h2[...], h3[...]], axis=0)
    return operate(ext, w_op, gather, own=False) + base[...]


def advance_kernel(base, ye, h0, h1, h2, h3, wa, wb, gather, wj, pick, vn, z, ze, s0, s1, s2, s3):
    vn[...] = advance(base, ye, h0, h1, h2, h3, (wa, wb), gather)
    z[...] = smooth(vn[...], wj)
    ze[...] = pack(z[...])
    send_lists(ze[...], pick, (s0, s1, s2, s3))


def products(basis, pairs):
    return [jnp.sum(basis[j] * basis[l], axis=0, keepdims=True) for j, l in pairs]


def before_last(slopes, v, ye, wa, wb, v0, v1, v2, base, known):
    before_advance(3, slopes, v, ye, wa, wb, base)
    basis = [x[...] for x in (v0, v1, v2, v)]
    known[...] = jnp.concatenate(products(basis, PAIRS[:10]) + [jnp.zeros((6, 128), F32)], axis=0)


def last_kernel(base, ye, h0, h1, h2, h3, wa, wb, gather, v0, v1, v2, v3, known, v4, gram):
    v4[...] = advance(base, ye, h0, h1, h2, h3, (wa, wb), gather)
    basis = [v[...] for v in (v0, v1, v2, v3, v4)]
    rows = [known[0:10, :]] + products(basis, PAIRS[10:]) + [jnp.zeros((113, 128), F32)]
    sums = lax.dot_general(
        jnp.ones((8, 128), F32),
        jnp.concatenate(rows, axis=0),
        LAST,
        precision=lax.Precision.HIGHEST,
        preferred_element_type=F32,
    )
    gram[...] = sums[0:1]


def orthogonal_kernel(total, grams, v0, v1, v2, v3, v4, q_out, r_out):
    sums = jnp.sum(grams[...], axis=0, keepdims=True) * (1.0 / (2.0 * total))
    g = {pair: sums[:, n : n + 1] for n, pair in enumerate(PAIRS)}
    lower = {}
    for j in range(5):
        d = g[(j, j)]
        for k in range(j):
            d = d - lower[(j, k)] * lower[(j, k)]
        lower[(j, j)] = jnp.sqrt(d)
        for i in range(j + 1, 5):
            t = g[(j, i)]
            for k in range(j):
                t = t - lower[(i, k)] * lower[(j, k)]
            lower[(i, j)] = t / lower[(j, j)]
    at_row = lax.broadcasted_iota(jnp.int32, (8, 128), 0)
    at_col = lax.broadcasted_iota(jnp.int32, (8, 128), 1)
    r = jnp.zeros((8, 128), F32)
    for (i, j), value in lower.items():
        r = jnp.where((at_row == j) & (at_col == i), value, r)
    r_out[...] = r[0:5, 0:5]
    solved = []
    for i, v in enumerate((v0, v1, v2, v3, v4)):
        t = v[...]
        for k in range(i):
            t = t - lower[(i, k)] * solved[k]
        t = t / lower[(i, i)]
        solved.append(t)
        q_out[i] = t[:, 0:BS]


def shape(*dims, dtype=F32):
    return jax.ShapeDtypeStruct(dims, dtype)


def kept(*dims, dtype=F32):
    return pltpu.VMEM(dims, dtype)


def call(kernel, outs, *args, specs=None, scratch=(), flops=2_000_000, name=None):
    return pl.pallas_call(
        kernel,
        out_shape=outs,
        in_specs=specs or [VM] * len(args),
        out_specs=jax.tree.map(lambda _: VM, outs),
        scratch_shapes=list(scratch),
        compiler_params=pltpu.CompilerParams(vmem_limit_bytes=24 << 20),
        cost_estimate=pl.CostEstimate(flops=flops, bytes_accessed=100_000, transcendentals=0),
        name=name,
    )(*args)


def swap_pairs(count, phase):
    if phase == 0:
        return [(i, i ^ 1) for i in range(count)]
    return [(i, (i - 1) % count if i % 2 == 0 else (i + 1) % count) for i in range(count)]


def exchange(sends):
    nx, ny = lax.axis_size("gx"), lax.axis_size("gy")
    return (
        lax.ppermute(sends[0], "gx", swap_pairs(nx, 1)),
        lax.ppermute(sends[1], "gx", swap_pairs(nx, 0)),
        lax.ppermute(sends[2], "gy", swap_pairs(ny, 1)),
        lax.ppermute(sends[3], "gy", swap_pairs(ny, 0)),
    )


def everywhere(x):
    count = lax.axis_size("gx") * lax.axis_size("gy")
    y = jnp.broadcast_to(x[None], (count,) + x.shape)
    return lax.all_to_all(y, ("gx", "gy"), split_axis=0, concat_axis=0, tiled=True)


def everywhere_by_core(x):
    nx, ny = lax.axis_size("gx"), lax.axis_size("gy")
    groups = [[p * ny + q for p in range(nx) for q in range(core, ny, 2)] for core in range(2)]
    y = jnp.broadcast_to(x[None], (nx * ny // 2,) + x.shape)
    same = lax.all_to_all(y, ("gx", "gy"), split_axis=0, concat_axis=0, tiled=True, axis_index_groups=groups)
    return same, lax.ppermute(same, "gy", swap_pairs(ny, 0))


def per_device(start, shifts, diag_blocks, off_blocks, jacobi_inv, prolong, coarse_inv, cols, send_rows, owner, agg_slot):
    halo = [shape(HALO, 128)] * 4
    matrices = [pltpu.with_memory_space_constraint(x, pltpu.HBM) for x in (off_blocks, diag_blocks, jnp.transpose(cols))]
    sources = [
        start,
        jacobi_inv.reshape(ROWS * BS, BS),
        jnp.transpose(prolong, (0, 2, 1)),
        jnp.transpose(coarse_inv, (1, 2, 0)).reshape(BS, 24),
        send_rows[0],
        owner.reshape(1, ROWS),
        agg_slot.reshape(1, ROWS),
        shifts.reshape(1, 4),
    ]
    v, wj, ptd, pick, z, ze, id_col, extra, slopes, *sends, near = call(
        first_kernel,
        [
            shape(ROWS, 128),
            kept(128, ROWS * BS, dtype=BF16),
            shape(CW, ROWS, 128),
            shape(4 * HALO, ROWS, dtype=BF16),
            shape(ROWS, 128),
            shape(ROWS, 128),
            shape(ROWS, 128),
            shape(16, 128),
            shape(4, 128),
        ]
        + [shape(6, HALO, 128)] * 4
        + [kept(EARLY, KOFF, BS, BS)],
        *[pltpu.with_memory_space_constraint(x, pltpu.HBM) for x in sources],
        matrices[0],
        specs=[HBM] * (len(sources) + 1),
        scratch=[pltpu.VMEM(x.shape, x.dtype) for x in sources]
        + [pltpu.SemaphoreType.DMA((len(sources),)), pltpu.SemaphoreType.DMA],
        name="first",
    )
    got = exchange(sends)
    half = kept(WIDTH, ROWS * BS // 2, dtype=BF16)
    *w_op, gather = call(
        operator_kernel,
        [half, half, shape(3 * ROWS, 256, dtype=BF16)],
        *matrices,
        near,
        specs=[HBM] * 3 + [VM],
        scratch=[
            pltpu.VMEM((ROWS - EARLY, KOFF, BS, BS), F32),
            pltpu.VMEM((ROWS, BS, BS), F32),
            pltpu.VMEM((KOFF, ROWS), jnp.int32),
            pltpu.SemaphoreType.DMA((2 + (ROWS - EARLY) // 8,)),
        ],
        flops=2_000_000_000,
        name="operator",
    )
    around = [g[0] for g in got]
    basis = [v]
    mask = pte = None
    for k in range(4):
        (base,) = call(before_restrict, [shape(ROWS, 128)], v, ze, *w_op, flops=500_000_000, name="before_restrict")
        w, p = call(
            restrict_kernel,
            [shape(ROWS, 128), shape(4 if k else 16, 128)],
            base,
            ze,
            *around,
            *w_op,
            gather,
            ptd,
            *([] if k else [extra]),
            name="restrict",
        )
        if k == 0:
            mask, pte, x = call(
                coarse_kernel,
                [kept(64 * 128, 128, dtype=BF16), shape(CW, EXT, 128), shape(64, 8, 128)],
                *everywhere_by_core(p),
                id_col,
                ptd,
                *got,
                name="coarse",
            )
        else:
            x = everywhere(p).reshape(64, 8, 128)
        ye, *sends = call(
            correct_kernel,
            [shape(ROWS, 128)] + halo,
            x,
            mask,
            pte,
            z,
            w,
            *w_op,
            gather,
            wj,
            pick,
            scratch=[pltpu.VMEM((16, 64 * 128), BF16)],
            name="correct",
        )
        around = exchange(sends)
        base, *known = call(
            functools.partial(before_advance, k) if k < 3 else before_last,
            [shape(ROWS, 128)] if k < 3 else [shape(ROWS, 128), shape(16, 128)],
            slopes,
            v,
            ye,
            *w_op,
            *([] if k < 3 else basis[:3]),
            flops=500_000_000,
            name="before_advance",
        )
        if k < 3:
            v, z, ze, *sends = call(
                advance_kernel,
                [shape(ROWS, 128)] * 3 + halo,
                base,
                ye,
                *around,
                *w_op,
                gather,
                wj,
                pick,
                name="advance",
            )
            basis.append(v)
            around = exchange(sends)
    v, gram = call(
        last_kernel,
        [shape(ROWS, 128), shape(1, 128)],
        base,
        ye,
        *around,
        *w_op,
        gather,
        *basis,
        *known,
        name="last",
    )
    basis.append(v)
    grams = everywhere(gram).reshape(128, 128)
    total = float(ROWS * BS * 128)
    return tuple(
        call(
            functools.partial(orthogonal_kernel, total),
            [shape(5, ROWS, BS), shape(5, 5)],
            grams,
            *basis,
            name="orthogonal",
        )
    )


def solution(mesh):
    rows = ("gx", "gy")
    in_specs = (
        P(rows, None),
        P(),
        P(rows, None, None),
        P(rows, None, None, None),
        P(rows, None, None),
        P(rows, None, None),
        P(rows, None, None),
        P(rows, None),
        P(rows, None, None),
        P(rows, None),
        P(rows),
    )
    return jax.shard_map(
        per_device, mesh=mesh, in_specs=in_specs, out_specs=(P(None, rows, None), P()), check_vma=False
    )
```

```python
import functools

import jax
import jax.numpy as jnp
from jax import lax
from jax.experimental import pallas as pl
from jax.experimental.pallas import tpu as pltpu
from jax.sharding import PartitionSpec as P

F32 = jnp.float32
BF16 = jnp.bfloat16
ROWS = 48
BS = 64
CW = 8
HALO = 16
EXT = ROWS + 4 * HALO
KOFF = 6
EARLY = 16
OWN = 6 * 128
WIDTH = 7 * 128
jacobi_weight = 2.0 / 3.0
PAIRS = [(j, l) for l in range(5) for j in range(l + 1)]

VM = pl.BlockSpec(memory_space=pltpu.VMEM)
HBM = pl.BlockSpec(memory_space=pltpu.HBM)
LAST = (((1,), (1,)), ((), ()))


def low_lanes(x):
    return lax.broadcasted_iota(jnp.int32, x.shape, 1) < BS


def swap(x):
    return pltpu.roll(x, BS, 1)


def twice(x):
    return jnp.concatenate([x, x], axis=1)


def pack(x):
    high = x.astype(BF16).astype(F32)
    return jnp.where(low_lanes(x), high, (x - high).astype(BF16).astype(F32))


def lhs_parts(packed):
    low = low_lanes(packed)
    turned = swap(packed)
    return jnp.where(low, packed, turned), jnp.where(low, turned, 0.0)


def row_blocks(top, bottom, w_ref, first=0):
    out = []
    for g in range(ROWS // 8):
        lhs = jnp.concatenate([top[8 * g : 8 * g + 8], bottom[8 * g : 8 * g + 8]], axis=0).astype(BF16)
        ref, n = (w_ref[g // 3], g % 3) if isinstance(w_ref, tuple) else (w_ref, g)
        r = jnp.dot(
            lhs, ref[first : first + top.shape[1], 512 * n : 512 * n + 512], preferred_element_type=F32
        )
        s = r[:8] + r[8:]
        own = lax.broadcasted_iota(jnp.int32, s.shape, 0) == lax.broadcasted_iota(jnp.int32, s.shape, 1) // BS
        s = jnp.where(own, s, 0.0)
        t = (s[:, 0:128] + s[:, 128:256]) + (s[:, 256:384] + s[:, 384:512])
        out.append(t + swap(t))
    return jnp.concatenate(out, axis=0)


def smooth(x, wj_ref):
    top, bottom = lhs_parts(pack(x))
    return row_blocks(top, bottom, wj_ref)


def operate_own(packed, w_ref):
    top, bottom = lhs_parts(packed)
    return row_blocks(top, bottom, w_ref, OWN)


def operate(packed, w_ref, gather_ref, own=True):
    e = jnp.concatenate([packed, jnp.zeros((128 - EXT, 128), F32)], axis=0)
    s = swap(e)
    low = low_lanes(e)
    zero = jnp.zeros_like(e)
    rhs = jnp.concatenate(
        [
            jnp.concatenate([jnp.where(low, e, zero), jnp.where(low, s, zero)], axis=1),
            jnp.concatenate([jnp.where(low, zero, s), jnp.where(low, zero, e)], axis=1),
        ],
        axis=0,
    ).astype(BF16)
    x = jnp.dot(gather_ref[...], rhs, preferred_element_type=F32)
    high = [x[ROWS * p : ROWS * p + ROWS, 0:128] for p in range(3)]
    rest = [x[ROWS * p : ROWS * p + ROWS, 128:256] for p in range(3)]
    none = [jnp.zeros((ROWS, 128), F32)] * 3
    top, bottom = high + high, rest + none
    if own:
        for x, part in zip((top, bottom), lhs_parts(packed[:ROWS])):
            x.append(part)
    return row_blocks(jnp.concatenate(top, axis=1), jnp.concatenate(bottom, axis=1), w_ref)


def send_lists(packed, pick_ref, outs):
    picked = jnp.dot(pick_ref[...], packed.astype(BF16), preferred_element_type=F32)
    for s, out in enumerate(outs):
        out[...] = picked[HALO * s : HALO * s + HALO]


def pair_rows(x):
    t = twice(x).T
    high = t.astype(BF16).astype(F32)
    return jnp.where(lax.broadcasted_iota(jnp.int32, t.shape, 0) < BS, high, t - high).astype(BF16)


def column(line):
    line = jnp.concatenate([line, jnp.zeros((1, 128 - line.shape[1]), F32)], axis=1)
    return jnp.broadcast_to(line, (128, 128)).T


def first_kernel(*refs):
    sources, off, rest = refs[:8], refs[8], refs[9:]
    v, wj, ptd, pick, z, ze, ids, extra, slopes, s0, s1, s2, s3, near = rest[:14]
    here, sems, far = rest[14:22], rest[22], rest[23]
    copies = [pltpu.make_async_copy(x, y, sems.at[n]) for n, (x, y) in enumerate(zip(sources, here))]
    for c in copies:
        c.start()
    ahead = pltpu.make_async_copy(off.at[pl.ds(0, EARLY)], near, far)
    ahead.start()
    for c in copies:
        c.wait()
    start, jac, pt, inverse, listed, owner, slot, shifts = here
    v[...] = twice(start[...])
    for n in range(ROWS // 2):
        wj[:, 128 * n : 128 * n + 128] = pair_rows(jac[128 * n : 128 * n + 128, :] * jacobi_weight)
    z[...] = smooth(v[...], wj)
    ze[...] = pack(z[...])
    even_x = lax.axis_index("gx") % 2 == 0
    even_y = lax.axis_index("gy") % 2 == 0
    lists = listed[...].astype(F32)
    order = [
        jnp.where(even_x, lists[1:2], lists[0:1]),
        jnp.where(even_x, lists[0:1], lists[1:2]),
        jnp.where(even_y, lists[3:4], lists[2:3]),
        jnp.where(even_y, lists[2:3], lists[3:4]),
    ]
    chosen = jnp.concatenate([column(x)[0:HALO, 0:ROWS] for x in order], axis=0)
    chosen = (chosen == lax.broadcasted_iota(jnp.int32, (4 * HALO, ROWS), 1).astype(F32)).astype(F32)
    pick[...] = chosen.astype(BF16)
    number = (owner[...] * 24 + slot[...]).astype(F32)
    ids[...] = column(number)[0:ROWS]
    for c in range(CW):
        ptd[c] = twice(pt[:, c, :])
    low = lax.broadcasted_iota(jnp.int32, (ROWS, 128), 1) < BS
    parts = [jnp.where(low, ptd[r], ptd[r + 4]) for r in range(4)] + [ids[...]]
    high = [x.astype(BF16) for x in parts]
    rest = [(x - y.astype(F32)).astype(BF16) for x, y in zip(parts, high)]
    picked = jnp.concatenate([ze[...].astype(BF16)] + high + rest, axis=1)
    picked = jnp.dot(pick[...], picked, preferred_element_type=F32)
    parts = [picked[:, 0:128]]
    for k in range(1, 6):
        parts.append(picked[:, 128 * k : 128 * k + 128] + picked[:, 128 * k + 640 : 128 * k + 768])
    for s, out in enumerate((s0, s1, s2, s3)):
        for k, x in enumerate(parts):
            out[k] = x[HALO * s : HALO * s + HALO]
    wide = jnp.concatenate([inverse[...], jnp.zeros((BS, 104), F32)], axis=1)
    wide = jnp.concatenate([wide, jnp.zeros((BS, 128), F32)], axis=0).T[0:24]
    extra[4:16, :] = wide[0:12] + swap(wide[12:24])
    number = jnp.concatenate([number, jnp.zeros((1, 128 - ROWS), F32)], axis=1)
    lane = lax.broadcasted_iota(jnp.int32, (1, 128), 1)
    spare = (lane >= ROWS) & (lane < BS)
    for r in range(3):
        extra[r : r + 1, :] = jnp.where(spare, pltpu.roll(jnp.broadcast_to(number, (8, 128)), ROWS - 16 * r, 1)[0:1], 0.0)
    extra[3:4, :] = jnp.zeros((1, 128), F32)
    for k in range(4):
        slopes[k : k + 1, :] = jnp.broadcast_to(shifts[:, k : k + 1], (1, 128))
    ahead.wait()


def pack_rows(buf, n, dbuf, row, w):
    at = BS * (row % (ROWS // 2))
    at = slice(at, at + 128)
    for p in range(3):
        x = jnp.concatenate(
            [
                jnp.concatenate([buf[n, 2 * p], buf[n, 2 * p + 1]], axis=1),
                jnp.concatenate([buf[n + 1, 2 * p], buf[n + 1, 2 * p + 1]], axis=1),
            ],
            axis=0,
        ).T
        high = x.astype(BF16)
        w[128 * p : 128 * p + 128, at] = high
        w[384 + 128 * p : 512 + 128 * p, at] = (x - high.astype(F32)).astype(BF16)
    w[768:896, at] = pair_rows(jnp.concatenate([dbuf[row], dbuf[row + 1]], axis=0))


def operator_kernel(off, diag, cols, near, wa, wb, gather, buf, dbuf, cbuf, sems):
    steps = (ROWS - EARLY) // 8
    named = pltpu.make_async_copy(cols, cbuf, sems.at[0])
    named.start()
    middle = pltpu.make_async_copy(diag, dbuf, sems.at[1])
    middle.start()
    later = [
        pltpu.make_async_copy(off.at[pl.ds(EARLY + 8 * g, 8)], buf.at[pl.ds(8 * g, 8)], sems.at[2 + g])
        for g in range(steps)
    ]
    for c in later:
        c.start()
    named.wait()
    turn_x = (lax.axis_index("gx") % 2) * HALO
    turn_y = (lax.axis_index("gy") % 2) * HALO
    number = cbuf[...]
    beyond = number - ROWS
    turned = ROWS + (beyond ^ jnp.where(beyond < 2 * HALO, turn_x, turn_y))
    number = jnp.where(beyond >= 0, turned, number).astype(F32)
    number = jnp.concatenate([number, jnp.zeros((KOFF, 128 - ROWS), F32)], axis=1)
    number = jnp.concatenate([number, jnp.zeros((128 - KOFF, 128), F32)], axis=0).T[0:ROWS]
    lane = lax.broadcasted_iota(jnp.int32, (ROWS, 256), 1).astype(F32)
    for p in range(3):
        hit = (lane == number[:, 2 * p : 2 * p + 1]) | (lane == number[:, 2 * p + 1 : 2 * p + 2] + 128.0)
        gather[ROWS * p : ROWS * p + ROWS, :] = hit.astype(F32).astype(BF16)
    middle.wait()
    for n in range(0, EARLY, 2):
        pack_rows(near, n, dbuf, n, wa)
    for g in range(steps):
        later[g].wait()
        for n in range(8 * g, 8 * g + 8, 2):
            pack_rows(buf, n, dbuf, EARLY + n, wa if EARLY + n < ROWS // 2 else wb)


def before_restrict(v, ze, wa, wb, base):
    base[...] = v[...] - operate_own(ze[...], (wa, wb))


def before_advance(k, slopes, v, ye, wa, wb, base):
    base[...] = operate_own(ye[...], (wa, wb)) - slopes[k : k + 1, :] * v[...]


def restrict_kernel(base, ze, h0, h1, h2, h3, wa, wb, gather, ptd, *rest):
    *extra, w, p = rest
    ext = jnp.concatenate([ze[...], h0[...], h1[...], h2[...], h3[...]], axis=0)
    r = base[...] - operate(ext, (wa, wb), gather, own=False)
    w[...] = r
    ones = jnp.ones((16, 128), BF16)
    pad = jnp.zeros((16, 128), F32)
    for k in range(4):
        x = jnp.concatenate([pack(ptd[k] * r), pad, pack(ptd[k + 4] * r), pad], axis=0).astype(BF16)
        line = lax.dot_general(ones, x, LAST, preferred_element_type=F32)[0:1]
        p[k : k + 1, :] = line + extra[0][k : k + 1, :] if extra else line
    if extra:
        p[4:16, :] = extra[0][4:16, :]


def coarse_kernel(same, other, ids, ptd, g0, g1, g2, g3, mask, pte, xp):
    idc = jnp.concatenate(
        [ids[...], g0[5], g1[5], g2[5], g3[5], jnp.full((128 - EXT, 128), -1.0, F32)], axis=0
    )
    wanted = idc.T[0:1]
    even = lax.axis_index("gy") % 2 == 0

    def by_core(x, y):
        return jnp.where(even, x, y), jnp.where(even, y, x)

    given = [jnp.concatenate(by_core(same[:, r, :], other[:, r, :]), axis=0).T[ROWS:BS] for r in range(3)] + [jnp.full((BS - ROWS, 128), -1.0, F32)]
    given = jnp.concatenate(given + given, axis=0)
    for q in range(64):
        line = jnp.concatenate([given[0:BS, q : q + 1], given[BS:128, BS + q : BS + q + 1]], axis=0)
        mask[128 * q : 128 * q + 128, :] = (line == wanted).astype(F32).astype(BF16)

    def in_order(x, y):
        for q in range(64):
            xp[q] = jnp.concatenate([x[q, 0:4, :], y[q, 0:4, :]], axis=0)

    pl.when(even)(lambda: in_order(same, other))
    pl.when(jnp.logical_not(even))(lambda: in_order(other, same))
    device = jnp.floor((idc + 0.5) * (1.0 / 24.0))
    slot = idc - 24.0 * device
    upper = slot >= 11.5
    chip = jnp.floor(device * 0.5)
    core = device - 2.0 * chip
    core = jnp.where(even, core, 1.0 - core)
    place = core * 1024.0 + chip * 16.0 + 4.0 + jnp.where(upper, slot - 12.0, slot)
    high, rest = [], []
    for b in range(8):
        src = (same if b < 4 else other)[16 * (b % 4) : 16 * (b % 4) + 16].reshape(256, 128)
        high.append(src.astype(BF16))
        rest.append((src - high[-1].astype(F32)).astype(BF16))
    lane = lax.broadcasted_iota(jnp.int32, (128, 128), 1).astype(F32)
    hit = jnp.concatenate([(place - 128.0 * b == lane).astype(F32).astype(BF16) for b in range(16)], axis=1)
    source = jnp.concatenate([jnp.concatenate(high, axis=0), jnp.concatenate(rest, axis=0)], axis=1)
    total = jnp.dot(hit, source, preferred_element_type=F32)
    total = total[:, 0:128] + total[:, 128:256]
    inverse = jnp.where(upper, swap(total), total)[:EXT]
    wide = []
    for c in range(CW):
        around = [g[1 + c % 4] for g in (g0, g1, g2, g3)]
        around = jnp.concatenate(around, axis=0)
        lowh = low_lanes(around)
        turned = swap(around)
        around = jnp.where(lowh, around, turned) if c < 4 else jnp.where(lowh, turned, around)
        wide.append(jnp.concatenate([ptd[c], around], axis=0))
    for d in range(CW):
        acc = wide[0] * inverse[:, d : d + 1]
        for c in range(1, CW):
            acc = acc + wide[c] * inverse[:, c * CW + d : c * CW + d + 1]
        pte[d] = acc


def correct_kernel(x, mask, pte, z, w, wa, wb, gather, wj, pick, ye, s0, s1, s2, s3, parts):
    sub = lax.broadcasted_iota(jnp.int32, (8, 128), 0) < 4
    lane = lax.broadcasted_iota(jnp.int32, (8, 128), 1) < BS
    keep = sub == lane
    for q in range(64):
        t = x[q]
        t = jnp.where(keep, t, pltpu.roll(swap(t), 4, 0))
        high = t.astype(BF16).astype(F32)
        parts[:, 128 * q : 128 * q + 128] = jnp.concatenate([high, t - high], axis=0).astype(BF16)
    got = jnp.dot(parts[...], mask[...], preferred_element_type=F32)
    coarse = jnp.concatenate([got[0:8] + got[8:16], jnp.zeros((120, 128), F32)], axis=0).T[:EXT]
    u = pte[0] * coarse[:, 0:1]
    for d in range(1, CW):
        u = u + pte[d] * coarse[:, d : d + 1]
    r = w[...] - operate(pack(u), (wa, wb), gather)
    y = z[...] + u[:ROWS] + smooth(r, wj)
    ye[...] = pack(y)
    send_lists(ye[...], pick, (s0, s1, s2, s3))


def advance(base, ye, h0, h1, h2, h3, w_op, gather):
    ext = jnp.concatenate([ye[...], h0[...], h1[...], h2[...], h3[...]], axis=0)
    return operate(ext, w_op, gather, own=False) + base[...]


def advance_kernel(base, ye, h0, h1, h2, h3, wa, wb, gather, wj, pick, vn, z, ze, s0, s1, s2, s3):
    vn[...] = advance(base, ye, h0, h1, h2, h3, (wa, wb), gather)
    z[...] = smooth(vn[...], wj)
    ze[...] = pack(z[...])
    send_lists(ze[...], pick, (s0, s1, s2, s3))


def products(basis, pairs):
    return [jnp.sum(basis[j] * basis[l], axis=0, keepdims=True) for j, l in pairs]


def before_last(slopes, v, ye, wa, wb, v0, v1, v2, base, known):
    before_advance(3, slopes, v, ye, wa, wb, base)
    basis = [x[...] for x in (v0, v1, v2, v)]
    known[...] = jnp.concatenate(products(basis, PAIRS[:10]) + [jnp.zeros((6, 128), F32)], axis=0)


def last_kernel(base, ye, h0, h1, h2, h3, wa, wb, gather, v0, v1, v2, v3, known, v4, gram):
    v4[...] = advance(base, ye, h0, h1, h2, h3, (wa, wb), gather)
    basis = [v[...] for v in (v0, v1, v2, v3, v4)]
    rows = [known[0:10, :]] + products(basis, PAIRS[10:]) + [jnp.zeros((113, 128), F32)]
    sums = lax.dot_general(
        jnp.ones((8, 128), F32),
        jnp.concatenate(rows, axis=0),
        LAST,
        precision=lax.Precision.HIGHEST,
        preferred_element_type=F32,
    )
    gram[...] = sums[0:1]


def orthogonal_kernel(total, grams, v0, v1, v2, v3, v4, q_out, r_out):
    sums = jnp.sum(grams[...], axis=0, keepdims=True) * (1.0 / (2.0 * total))
    g = {pair: sums[:, n : n + 1] for n, pair in enumerate(PAIRS)}
    lower = {}
    for j in range(5):
        d = g[(j, j)]
        for k in range(j):
            d = d - lower[(j, k)] * lower[(j, k)]
        lower[(j, j)] = jnp.sqrt(d)
        for i in range(j + 1, 5):
            t = g[(j, i)]
            for k in range(j):
                t = t - lower[(i, k)] * lower[(j, k)]
            lower[(i, j)] = t / lower[(j, j)]
    at_row = lax.broadcasted_iota(jnp.int32, (8, 128), 0)
    at_col = lax.broadcasted_iota(jnp.int32, (8, 128), 1)
    r = jnp.zeros((8, 128), F32)
    for (i, j), value in lower.items():
        r = jnp.where((at_row == j) & (at_col == i), value, r)
    r_out[...] = r[0:5, 0:5]
    solved = []
    for i, v in enumerate((v0, v1, v2, v3, v4)):
        t = v[...]
        for k in range(i):
            t = t - lower[(i, k)] * solved[k]
        t = t * (1.0 / lower[(i, i)])
        solved.append(t)
        q_out[i] = t[:, 0:BS]


def shape(*dims, dtype=F32):
    return jax.ShapeDtypeStruct(dims, dtype)


def kept(*dims, dtype=F32):
    return pltpu.VMEM(dims, dtype)


def call(kernel, outs, *args, specs=None, scratch=(), flops=2_000_000, name=None):
    return pl.pallas_call(
        kernel,
        out_shape=outs,
        in_specs=specs or [VM] * len(args),
        out_specs=jax.tree.map(lambda _: VM, outs),
        scratch_shapes=list(scratch),
        compiler_params=pltpu.CompilerParams(vmem_limit_bytes=24 << 20),
        cost_estimate=pl.CostEstimate(flops=flops, bytes_accessed=100_000, transcendentals=0),
        name=name,
    )(*args)


def swap_pairs(count, phase):
    if phase == 0:
        return [(i, i ^ 1) for i in range(count)]
    return [(i, (i - 1) % count if i % 2 == 0 else (i + 1) % count) for i in range(count)]


def exchange(sends):
    nx, ny = lax.axis_size("gx"), lax.axis_size("gy")
    return (
        lax.ppermute(sends[0], "gx", swap_pairs(nx, 1)),
        lax.ppermute(sends[1], "gx", swap_pairs(nx, 0)),
        lax.ppermute(sends[2], "gy", swap_pairs(ny, 1)),
        lax.ppermute(sends[3], "gy", swap_pairs(ny, 0)),
    )


def everywhere(x):
    count = lax.axis_size("gx") * lax.axis_size("gy")
    y = jnp.broadcast_to(x[None], (count,) + x.shape)
    return lax.all_to_all(y, ("gx", "gy"), split_axis=0, concat_axis=0, tiled=True)


def everywhere_by_core(x):
    nx, ny = lax.axis_size("gx"), lax.axis_size("gy")
    groups = [[p * ny + q for p in range(nx) for q in range(core, ny, 2)] for core in range(2)]
    y = jnp.broadcast_to(x[None], (nx * ny // 2,) + x.shape)
    same = lax.all_to_all(y, ("gx", "gy"), split_axis=0, concat_axis=0, tiled=True, axis_index_groups=groups)
    return same, lax.ppermute(same, "gy", swap_pairs(ny, 0))


def per_device(start, shifts, diag_blocks, off_blocks, jacobi_inv, prolong, coarse_inv, cols, send_rows, owner, agg_slot):
    halo = [shape(HALO, 128)] * 4
    matrices = [pltpu.with_memory_space_constraint(x, pltpu.HBM) for x in (off_blocks, diag_blocks, jnp.transpose(cols))]
    sources = [
        start,
        jacobi_inv.reshape(ROWS * BS, BS),
        jnp.transpose(prolong, (0, 2, 1)),
        jnp.transpose(coarse_inv, (1, 2, 0)).reshape(BS, 24),
        send_rows[0],
        owner.reshape(1, ROWS),
        agg_slot.reshape(1, ROWS),
        shifts.reshape(1, 4),
    ]
    v, wj, ptd, pick, z, ze, id_col, extra, slopes, *sends, near = call(
        first_kernel,
        [
            shape(ROWS, 128),
            kept(128, ROWS * BS, dtype=BF16),
            shape(CW, ROWS, 128),
            shape(4 * HALO, ROWS, dtype=BF16),
            shape(ROWS, 128),
            shape(ROWS, 128),
            shape(ROWS, 128),
            shape(16, 128),
            shape(4, 128),
        ]
        + [shape(6, HALO, 128)] * 4
        + [kept(EARLY, KOFF, BS, BS)],
        *[pltpu.with_memory_space_constraint(x, pltpu.HBM) for x in sources],
        matrices[0],
        specs=[HBM] * (len(sources) + 1),
        scratch=[pltpu.VMEM(x.shape, x.dtype) for x in sources]
        + [pltpu.SemaphoreType.DMA((len(sources),)), pltpu.SemaphoreType.DMA],
        name="first",
    )
    got = exchange(sends)
    half = kept(WIDTH, ROWS * BS // 2, dtype=BF16)
    *w_op, gather = call(
        operator_kernel,
        [half, half, shape(3 * ROWS, 256, dtype=BF16)],
        *matrices,
        near,
        specs=[HBM] * 3 + [VM],
        scratch=[
            pltpu.VMEM((ROWS - EARLY, KOFF, BS, BS), F32),
            pltpu.VMEM((ROWS, BS, BS), F32),
            pltpu.VMEM((KOFF, ROWS), jnp.int32),
            pltpu.SemaphoreType.DMA((2 + (ROWS - EARLY) // 8,)),
        ],
        flops=2_000_000_000,
        name="operator",
    )
    around = [g[0] for g in got]
    basis = [v]
    mask = pte = None
    for k in range(4):
        (base,) = call(before_restrict, [shape(ROWS, 128)], v, ze, *w_op, flops=500_000_000, name="before_restrict")
        w, p = call(
            restrict_kernel,
            [shape(ROWS, 128), shape(4 if k else 16, 128)],
            base,
            ze,
            *around,
            *w_op,
            gather,
            ptd,
            *([] if k else [extra]),
            name="restrict",
        )
        if k == 0:
            mask, pte, x = call(
                coarse_kernel,
                [kept(64 * 128, 128, dtype=BF16), shape(CW, EXT, 128), shape(64, 8, 128)],
                *everywhere_by_core(p),
                id_col,
                ptd,
                *got,
                name="coarse",
            )
        else:
            x = everywhere(p).reshape(64, 8, 128)
        ye, *sends = call(
            correct_kernel,
            [shape(ROWS, 128)] + halo,
            x,
            mask,
            pte,
            z,
            w,
            *w_op,
            gather,
            wj,
            pick,
            scratch=[pltpu.VMEM((16, 64 * 128), BF16)],
            name="correct",
        )
        around = exchange(sends)
        base, *known = call(
            functools.partial(before_advance, k) if k < 3 else before_last,
            [shape(ROWS, 128)] if k < 3 else [shape(ROWS, 128), shape(16, 128)],
            slopes,
            v,
            ye,
            *w_op,
            *([] if k < 3 else basis[:3]),
            flops=500_000_000,
            name="before_advance",
        )
        if k < 3:
            v, z, ze, *sends = call(
                advance_kernel,
                [shape(ROWS, 128)] * 3 + halo,
                base,
                ye,
                *around,
                *w_op,
                gather,
                wj,
                pick,
                name="advance",
            )
            basis.append(v)
            around = exchange(sends)
    v, gram = call(
        last_kernel,
        [shape(ROWS, 128), shape(1, 128)],
        base,
        ye,
        *around,
        *w_op,
        gather,
        *basis,
        *known,
        name="last",
    )
    basis.append(v)
    grams = everywhere(gram).reshape(128, 128)
    total = float(ROWS * BS * 128)
    return tuple(
        call(
            functools.partial(orthogonal_kernel, total),
            [shape(5, ROWS, BS), shape(5, 5)],
            grams,
            *basis,
            name="orthogonal",
        )
    )


def solution(mesh):
    rows = ("gx", "gy")
    in_specs = (
        P(rows, None),
        P(),
        P(rows, None, None),
        P(rows, None, None, None),
        P(rows, None, None),
        P(rows, None, None),
        P(rows, None, None),
        P(rows, None),
        P(rows, None, None),
        P(rows, None),
        P(rows),
    )
    return jax.shard_map(
        per_device, mesh=mesh, in_specs=in_specs, out_specs=(P(None, rows, None), P()), check_vma=False
    )
```
